32 devices in a mesh: ctx: 16 (over z, x, core), tp: 2 (over y).
Axes of the slice: x: 2, y: 2, z: 4, core: 2. Of those that a mesh axis runs over, the one named last changes fastest.
Arguments:
- light_query: bfloat16 [4096, 8192], P('ctx', 'tp'), may hold values from -6 to 6
- light_key: bfloat16 [4096, 8192], P('ctx', 'tp'), may hold values from -6 to 6
- light_value: bfloat16 [4096, 8192], P('ctx', 'tp'), may hold values from -400 to 400
- log_decay: float32 [4096, 64], P('ctx', 'tp'), may hold values from -1 to 0
- out_gate: bfloat16 [4096, 8192], P('ctx', 'tp'), may hold values from -6 to 6
- norm_gain: float32 [8192], P('tp'), may hold values from 0.1 to 1.9
- soft_query: bfloat16 [4096, 8192], P('ctx', 'tp'), may hold values from -6 to 6
- soft_key: bfloat16 [4096, 1024], P('ctx', 'tp'), may hold values from -6 to 6
- soft_value: bfloat16 [4096, 1024], P('ctx', 'tp'), may hold values from -6 to 6
Outputs:
- light_out: bfloat16 [4096, 8192], P('ctx', 'tp')
- soft_out: bfloat16 [4096, 8192], P('ctx', 'tp')
The draws below stay inside these ranges and needn't reach their ends.
All inputs are finite; a program needn't handle non-finite values.
Results may differ from the reference program's by a relative error of at most 0.0075.
Values may be sent and summed in bfloat16 or wider, within the bound.
No kernel may reach another device: no remote copies, remote signals or barrier semaphores. Data moves between devices by JAX's collectives and lax.ppermute only.
A program may use at most 384 MiB of HBM per device.

```python
import math
import jax
import jax.numpy as jnp
from jax import lax

HEADS = 64
HD = 128
KV_HEADS = 8
TOK_DEV = 256
TOKENS = 4096


def draw_soft_query(key, part):
    key = jax.random.fold_in(key, 7)
    drawn = jnp.clip(jax.random.normal(key, (TOKENS, HEADS * HD), jnp.float32), -4.0, 4.0)
    return drawn.astype(jnp.bfloat16)


def draw_soft_key(key, part):
    key = jax.random.fold_in(key, 13)
    drawn = jnp.clip(jax.random.normal(key, (TOKENS, KV_HEADS * HD), jnp.float32), -4.0, 4.0)
    return drawn.astype(jnp.bfloat16)


def draw_light_value(key, part):
    key = jax.random.fold_in(key, 23)
    keys = jax.random.split(key, 3)
    width = HEADS * HD
    rising = jnp.power(3.0, jnp.arange(width).astype(jnp.float32) / (width - 1))
    column = jnp.exp(jax.random.uniform(keys[0], (width,), jnp.float32, 0.0, math.log(10.0))) * rising
    row = jnp.exp(jax.random.uniform(keys[1], (TOKENS, 1), jnp.float32, math.log(0.3), math.log(3.0)))
    base = jnp.clip(jax.random.normal(keys[2], (TOKENS, width), jnp.float32), -4.0, 4.0)
    return (base * row * column[None, :]).astype(jnp.bfloat16)


def draw_log_decay(key, part):
    key = jax.random.fold_in(key, 31)
    keys = jax.random.split(key, 5)
    fast_share = 4
    fast = jax.random.randint(keys[0], (HEADS,), 0, 8) < fast_share
    base = jnp.where(fast, -1.0 / 40.0, -0.4 / TOKENS)
    blocks = TOKENS // TOK_DEV
    factor = jnp.exp(jax.random.uniform(keys[1], (blocks, 1, HEADS), jnp.float32, math.log(0.5), math.log(2.0)))
    factor = jnp.broadcast_to(factor, (blocks, TOK_DEV, HEADS)).reshape(TOKENS, HEADS)
    rough = jax.random.uniform(keys[2], (TOKENS, HEADS), jnp.float32, 0.7, 1.4)
    rate = base[None, :] * factor * rough
    spots = jax.random.randint(keys[3], (2, HEADS), 0, TOKENS)
    depth = jax.random.uniform(keys[4], (2, HEADS), jnp.float32, math.log(0.5), math.log(0.8))
    position = jnp.arange(TOKENS)[:, None]
    rate = rate + jnp.where(position == spots[0][None, :], depth[0][None, :], 0.0)
    rate = rate + jnp.where(position == spots[1][None, :], depth[1][None, :], 0.0)
    return rate


def shard_levels(own_key, shape, cuts, low, top_value):
    level = 1.0
    for dim, shards_of in cuts:
        steps = jax.random.uniform(jax.random.fold_in(jax.random.fold_in(own_key, 6), dim), (shards_of,), jnp.float32, low / len(cuts), top_value / len(cuts))
        level = level * jnp.repeat(jnp.exp(steps), shape[dim] // shards_of).reshape((-1,) + (1,) * (len(shape) - 1 - dim))
    return level


def noise(own_key, dims, deviation, reach, shards=(), held_as=jnp.bfloat16):
    gain = shard_levels(own_key, dims, shards, -0.22, 0.18) if shards else 1.0
    drawn = jax.random.normal(own_key, dims, jnp.float32) * deviation * gain
    return jnp.minimum(jnp.maximum(drawn, -reach), reach).astype(held_as)


def setup_inputs(seed: int = 0) -> dict:
    splits = jax.random.split(jax.random.key(seed), 10)
    return {
        "light_query": noise(splits[0], (TOKENS, HEADS * HD), 1.0, 6.0, ((0, 16), (1, 2))),
        "light_key": noise(splits[1], (TOKENS, HEADS * HD), 1.0, 6.0, ((0, 16), (1, 2))),
        "light_value": draw_light_value(jax.random.fold_in(splits[9], 71), 0),
        "log_decay": draw_log_decay(jax.random.fold_in(splits[9], 71), 0),
        "out_gate": noise(splits[4], (TOKENS, HEADS * HD), 1.5, 6.0, ((0, 16), (1, 2))),
        "norm_gain": jnp.clip(1.0 + 0.18 * jax.random.normal(splits[5], (HEADS * HD,), jnp.float32), 0.1, 1.9),
        "soft_query": draw_soft_query(jax.random.fold_in(splits[9], 71), 0),
        "soft_key": draw_soft_key(jax.random.fold_in(splits[9], 71), 0),
        "soft_value": noise(splits[8], (TOKENS, KV_HEADS * HD), 1.0, 6.0, ((0, 16), (1, 2))),
    }


def lightning(light_query, light_key, light_value, log_decay):
    blocks = TOKENS // TOK_DEV
    query = light_query.reshape(blocks, TOK_DEV, HEADS, HD)
    keyed = light_key.reshape(blocks, TOK_DEV, HEADS, HD)
    valued = light_value.reshape(blocks, TOK_DEV, HEADS, HD)
    decay = log_decay.reshape(blocks, TOK_DEV, HEADS)
    causal = jnp.arange(TOK_DEV)[:, None] >= jnp.arange(TOK_DEV)[None, :]

    def advance(state, pieces):
        q_block, k_block, v_block, d_block = pieces
        cumulative = jnp.cumsum(d_block, axis=0)
        final = cumulative[-1]
        scores = jnp.einsum('thd,shd->hts', q_block.astype(jnp.float32), k_block.astype(jnp.float32))
        ctime = cumulative.T
        spread = jnp.where(causal[None], ctime[:, :, None] - ctime[:, None, :], 0.0)
        weights = jnp.where(causal[None], scores * jnp.exp(spread), 0.0).astype(jnp.bfloat16)
        weights = lax.optimization_barrier(weights).astype(jnp.float32)
        inner = jnp.einsum('hts,shd->thd', weights, v_block.astype(jnp.float32))
        carried = jnp.einsum('thd,hde->the', q_block.astype(jnp.float32), state, precision=lax.Precision.HIGHEST)
        carried = jnp.exp(cumulative)[:, :, None] * carried
        decayed = k_block.astype(jnp.float32) * jnp.exp(final[None, :] - cumulative)[:, :, None]
        local_state = jnp.einsum('shd,she->hde', decayed, v_block.astype(jnp.float32), precision=lax.Precision.HIGHEST)
        fresh = jnp.exp(final)[:, None, None] * state + local_state
        return (fresh, inner + carried)
    start_state = jnp.zeros((HEADS, HD, HD), jnp.float32)
    _, output = lax.scan(advance, start_state, (query, keyed, valued, decay))
    return output.reshape(TOKENS, HEADS * HD)

def softmax_layer(soft_query, soft_key, soft_value):
    groups = HEADS // KV_HEADS
    keys_all = soft_key.astype(jnp.float32).reshape(TOKENS, KV_HEADS, HD)
    values_all = soft_value.astype(jnp.float32).reshape(TOKENS, KV_HEADS, HD)
    scale = HD ** (-0.5)
    key_pos = jnp.arange(TOKENS)

    def one_block(index):
        start = (index * TOK_DEV).astype(jnp.int32)
        q_block = lax.dynamic_slice_in_dim(soft_query, start, TOK_DEV, 0)
        q_block = q_block.astype(jnp.float32).reshape(TOK_DEV, KV_HEADS, groups, HD)
        scores = jnp.einsum('tkgd,skd->kgts', q_block, keys_all) * scale
        query_pos = start + jnp.arange(TOK_DEV)
        allowed = key_pos[None, :] <= query_pos[:, None]
        scores = jnp.where(allowed, scores, -1e+30)
        top = lax.optimization_barrier(jnp.max(scores, axis=-1, keepdims=True))
        probs = jnp.where(allowed, jnp.exp(scores - top), 0.0)
        total = lax.optimization_barrier(jnp.sum(probs, axis=-1))
        rounded = lax.optimization_barrier(probs.astype(jnp.bfloat16)).astype(jnp.float32)
        summed = jnp.einsum('kgts,skd->kgtd', rounded, values_all) / total[..., None]
        return summed.transpose(2, 0, 1, 3).reshape(TOK_DEV, HEADS * HD).astype(jnp.bfloat16)
    blocks = TOKENS // TOK_DEV
    output = lax.map(one_block, jnp.arange(blocks, dtype=jnp.int32))
    return output.reshape(TOKENS, HEADS * HD)

def reference(light_query, light_key, light_value, log_decay, out_gate, norm_gain, soft_query, soft_key, soft_value):
    light_raw = lightning(light_query, light_key, light_value, log_decay)
    mean_square = lax.optimization_barrier(jnp.mean(light_raw * light_raw, axis=1, keepdims=True))
    light_out = light_raw * lax.rsqrt(mean_square + 1e-06) * norm_gain[None, :] * jax.nn.sigmoid(out_gate.astype(jnp.float32))
    soft_out = softmax_layer(soft_query, soft_key, soft_value)
    return (light_out.astype(jnp.bfloat16), soft_out)
```

```python
import functools
import math

import jax
import jax.numpy as jnp
from jax import lax
from jax.experimental import pallas as pl
from jax.experimental.pallas import tpu as pltpu
from jax.sharding import PartitionSpec as P

HD = 128
EPS = 1e-06
LOW = -1e30
PLANE = 4
TAIL = 16
VMEM = 60 * 2**20
F32 = jnp.float32
BF16 = jnp.bfloat16
HIGH = lax.Precision.HIGHEST
SCALE2 = HD ** (-0.5) * math.log2(math.e)


def params(**more):
    return pltpu.CompilerParams(vmem_limit_bytes=VMEM, **more)


def mm(a, b):
    return lax.dot_general(a, b, (((1,), (0,)), ((), ())), preferred_element_type=F32)


def mm_bt(a, b):
    return lax.dot_general(a, b, (((1,), (1,)), ((), ())), preferred_element_type=F32)


def mm_at(a, b):
    return lax.dot_general(a, b, (((0,), (0,)), ((), ())), preferred_element_type=F32)


def iota(shape, dim):
    return lax.broadcasted_iota(jnp.int32, shape, dim)


def state_kernel(pos, k_ref, v_ref, ld_ref, send_ref, keep_ref, cum_ref, cumt_ref, fin, *, qh, heads):
    step = pl.program_id(0)
    rows = ld_ref.shape[0]

    @pl.when(step == 0)
    def _():
        tri = (iota((rows, rows), 0) >= iota((rows, rows), 1)).astype(F32)
        ld = ld_ref[...]
        cum = lax.dot_general(tri, ld, (((1,), (0,)), ((), ())), precision=HIGH, preferred_element_type=F32)
        cumt = lax.dot_general(ld, tri, (((0,), (1,)), ((), ())), precision=HIGH, preferred_element_type=F32)
        ends = lax.dot_general(
            ld, jnp.ones((rows, HD), F32), (((0,), (0,)), ((), ())), precision=HIGH, preferred_element_type=F32
        )
        cum_ref[...] = jnp.zeros_like(cum_ref)
        cumt_ref[...] = jnp.zeros_like(cumt_ref)
        fin[...] = jnp.zeros_like(fin)
        for i in range(4):
            cum_ref[i, :, 0:qh] = cum[:, i * qh : (i + 1) * qh]
            cumt_ref[i, 0:qh, :] = cumt[i * qh : (i + 1) * qh, :]
            fin[i, 0:qh, :] = ends[i * qh : (i + 1) * qh, :]

    core = pos[2]
    kept = step // 2
    part = step % 2
    quarter = part * 2 + jnp.where(kept == 1, core, 1 - core)
    cum = cum_ref[quarter]
    weight = jnp.exp(cum[rows - 1 : rows, :] - cum)
    tail = fin[quarter]
    high = tail.astype(BF16).astype(F32)
    tail = jnp.concatenate([high, tail - high], axis=0).astype(BF16)
    states = []
    for i in range(qh):
        cols = slice(i * HD, (i + 1) * HD)
        keyed = (k_ref[:, cols].astype(F32) * weight[:, i : i + 1]).astype(BF16)
        states.append(mm_at(keyed, v_ref[:, cols]).astype(BF16))

    def put(ref):
        for i in range(qh):
            ref[part, i * HD : (i + 1) * HD, :] = states[i]
        ref[part, qh * HD : qh * HD + TAIL, :] = tail

    @pl.when(kept == 0)
    def _():
        put(send_ref)

    @pl.when(kept == 1)
    def _():
        put(keep_ref)


def local_state(pos, key, value, log_decay):
    rows, heads = log_decay.shape
    qh = heads // 4
    length = qh * HD + TAIL

    def columns(step, pos):
        core = pos[2]
        return (0, (step % 2) * 2 + jnp.where(step // 2 == 1, core, 1 - core))

    whole = lambda *shape: pl.BlockSpec(shape, lambda step, pos: (0,) * len(shape))
    return pl.pallas_call(
        functools.partial(state_kernel, qh=qh, heads=heads),
        grid_spec=pltpu.PrefetchScalarGridSpec(
            num_scalar_prefetch=1,
            grid=(4,),
            in_specs=[
                pl.BlockSpec((rows, qh * HD), columns),
                pl.BlockSpec((rows, qh * HD), columns),
                whole(rows, heads),
            ],
            out_specs=[
                whole(2, length, HD),
                whole(2, length, HD),
                whole(4, rows, HD),
                whole(4, 8, rows),
            ],
            scratch_shapes=[pltpu.VMEM((4, 8, HD), F32)],
        ),
        out_shape=[
            jax.ShapeDtypeStruct((2, length, HD), BF16),
            jax.ShapeDtypeStruct((2, length, HD), BF16),
            jax.ShapeDtypeStruct((4, rows, HD), F32),
            jax.ShapeDtypeStruct((4, 8, rows), F32),
        ],
        compiler_params=params(),
        cost_estimate=pl.CostEstimate(
            flops=2 * heads * rows * HD * HD * 4, bytes_accessed=rows * heads * HD * 4 + heads * HD * HD * 2, transcendentals=0
        ),
        name="local_state",
    )(pos, key, value, log_decay)


def spread(item, qh):
    tail = item[qh * HD : qh * HD + TAIL, :].astype(F32)
    return item[0 : qh * HD, :].astype(F32), tail[0:8, :] + tail[8:16, :]


def pack(states, logs):
    high = logs.astype(BF16).astype(F32)
    return states.astype(BF16), jnp.concatenate([high, logs - high], axis=0).astype(BF16)


def decay(states, logs, qh):
    factor = jnp.exp(logs)
    return jnp.concatenate(
        [states[i * HD : (i + 1) * HD, :] * factor[i : i + 1, :] for i in range(qh)], axis=0
    )


def joined(early, late, qh):
    return decay(early[0], late[1], qh) + late[0], early[1] + late[1]


def store(ref, item, qh):
    states, tail = pack(*item)
    ref[0 : qh * HD, :] = states
    ref[qh * HD : qh * HD + TAIL, :] = tail


def chip_kernel(pos, keep_ref, recv_ref, send_out, keep_out, *, qh):
    first = pos[2] == 0
    for out, part in ((send_out, 1 - pos[1]), (keep_out, pos[1])):
        own, other = keep_ref[part], recv_ref[part]
        early = spread(jnp.where(first, own, other), qh)
        late = spread(jnp.where(first, other, own), qh)
        store(out, joined(early, late, qh), qh)


def plane_kernel(pos, keep_ref, recv_ref, out, *, qh):
    first = pos[1] == 0
    own, other = keep_ref[...], recv_ref[...]
    early = spread(jnp.where(first, own, other), qh)
    late = spread(jnp.where(first, other, own), qh)
    store(out, joined(early, late, qh), qh)


def enter_kernel(pos, keep_ref, recv_ref, *refs, qh):
    planes, (send_out, keep_out) = refs[:-2], refs[-2:]
    total = None
    for ref in reversed(planes):
        item = spread(ref[...], qh)
        total = item if total is None else joined(total, item, qh)
    first = pos[1] == 0
    early = spread(jnp.where(first, keep_ref[...], recv_ref[...]), qh)
    if total is None:
        total = (jnp.zeros_like(early[0]), jnp.zeros_like(early[1]))
    later = joined(total, early, qh)
    zero, one = pack(*total), pack(*later)
    for out, take in ((send_out, first), (keep_out, jnp.logical_not(first))):
        out[0 : qh * HD, :] = jnp.where(take, one[0], zero[0])
        out[qh * HD : qh * HD + TAIL, :] = jnp.where(take, one[1], zero[1])


def core_kernel(pos, enter_keep, enter_recv, keep_ref, recv_ref, send_out, keep_out, *, qh):
    first = pos[2] == 0
    for part in range(2):
        entering = spread(jnp.where(pos[1] == part, enter_keep[...], enter_recv[...]), qh)
        own = spread(jnp.where(first, keep_ref[part], recv_ref[part]), qh)
        later = joined(entering, own, qh)[0].astype(BF16)
        now = entering[0].astype(BF16)
        send_out[part] = jnp.where(first, later, now)
        keep_out[part] = jnp.where(first, now, later)


def small(kernel, pos, arrays, outs, qh, name):
    nbytes = sum(a.size * 2 for a in arrays) + sum(math.prod(s) * 2 for s in outs)
    return pl.pallas_call(
        functools.partial(kernel, qh=qh),
        in_specs=[pl.BlockSpec(memory_space=pltpu.SMEM)] + [pl.BlockSpec(memory_space=pltpu.VMEM)] * len(arrays),
        out_specs=[pl.BlockSpec(memory_space=pltpu.VMEM)] * len(outs),
        out_shape=[jax.ShapeDtypeStruct(s, BF16) for s in outs],
        compiler_params=params(),
        cost_estimate=pl.CostEstimate(flops=nbytes, bytes_accessed=nbytes, transcendentals=0),
        name=name,
    )(pos, *arrays)


def intra_kernel(q_ref, k_ref, v_ref, cum_ref, cumt_ref, out_ref, *, qh):
    rows = q_ref.shape[0]
    causal = iota((rows, rows), 0) >= iota((rows, rows), 1)
    cum, cumt = cum_ref[0], cumt_ref[0]
    for i in range(qh):
        cols = slice(i * HD, (i + 1) * HD)
        scores = mm_bt(q_ref[:, cols], k_ref[:, cols])
        gap = jnp.where(causal, cum[:, i : i + 1] - cumt[i : i + 1, :], LOW)
        weights = (scores * jnp.exp(gap)).astype(BF16)
        out_ref[:, cols] = mm(weights, v_ref[:, cols])


def intra(query, key, value, cum, cumt):
    rows, width = query.shape
    wide = width // 4
    block = pl.BlockSpec((rows, wide), lambda i: (0, i))
    return pl.pallas_call(
        functools.partial(intra_kernel, qh=wide // HD),
        grid=(4,),
        in_specs=[
            block,
            block,
            block,
            pl.BlockSpec((1, rows, HD), lambda i: (i, 0, 0)),
            pl.BlockSpec((1, 8, rows), lambda i: (i, 0, 0)),
        ],
        out_specs=block,
        out_shape=jax.ShapeDtypeStruct((rows, width), F32),
        compiler_params=params(),
        cost_estimate=pl.CostEstimate(
            flops=8 * rows * rows * width, bytes_accessed=rows * width * 10, transcendentals=rows * rows * width // HD
        ),
        name="intra",
    )(query, key, value, cum, cumt)


def carry_kernel(pos, q_ref, intra_ref, cum_ref, keep_ref, recv_ref, out_ref, ss_ref, *, qh):
    quarter = pl.program_id(0)
    part = quarter // 2
    mine = quarter % 2 == pos[2]
    factor = jnp.exp(cum_ref[0])
    state = jnp.where(mine, keep_ref[part], recv_ref[part])
    total = jnp.zeros((q_ref.shape[0], HD), F32)
    for i in range(qh):
        cols = slice(i * HD, (i + 1) * HD)
        carried = mm(q_ref[:, cols], state[i * HD : (i + 1) * HD, :])
        raw = intra_ref[:, cols] + factor[:, i : i + 1] * carried
        out_ref[:, cols] = raw
        total = total + raw * raw

    @pl.when(quarter == 0)
    def _():
        ss_ref[...] = total

    @pl.when(quarter > 0)
    def _():
        ss_ref[...] += total


def carry(pos, query, inner, cum, keep, recv):
    rows, width = query.shape
    wide = width // 4
    block = pl.BlockSpec((rows, wide), lambda i: (0, i))
    whole = pl.BlockSpec(keep.shape, lambda i: (0, 0, 0))
    return pl.pallas_call(
        functools.partial(carry_kernel, qh=wide // HD),
        grid=(4,),
        in_specs=[
            pl.BlockSpec(memory_space=pltpu.SMEM),
            block,
            block,
            pl.BlockSpec((1, rows, HD), lambda i: (i, 0, 0)),
            whole,
            whole,
        ],
        out_specs=[block, pl.BlockSpec((rows, HD), lambda i: (0, 0))],
        out_shape=[jax.ShapeDtypeStruct((rows, width), F32), jax.ShapeDtypeStruct((rows, HD), F32)],
        input_output_aliases={2: 0},
        compiler_params=params(),
        cost_estimate=pl.CostEstimate(flops=4 * rows * width * HD, bytes_accessed=rows * width * 10, transcendentals=0),
        name="carry",
    )(pos, query, inner, cum, keep, recv)


def finish_kernel(raw_ref, ss_ref, gain_ref, gate_ref, out_ref, *, features):
    mean = jnp.sum(ss_ref[...], axis=1, keepdims=True) / features
    factor = lax.rsqrt(mean + EPS)
    gate = jax.nn.sigmoid(gate_ref[...].astype(F32))
    out_ref[...] = (raw_ref[...] * factor * gain_ref[...] * gate).astype(BF16)


def finish(raw, square, gain, gate, features):
    rows, width = raw.shape
    wide = width // 4
    block = pl.BlockSpec((rows, wide), lambda i: (0, i))
    return pl.pallas_call(
        functools.partial(finish_kernel, features=features),
        grid=(4,),
        in_specs=[
            block,
            pl.BlockSpec((rows, HD), lambda i: (0, 0)),
            pl.BlockSpec((1, wide), lambda i: (0, i)),
            block,
        ],
        out_specs=block,
        out_shape=jax.ShapeDtypeStruct((rows, width), BF16),
        compiler_params=params(),
        cost_estimate=pl.CostEstimate(flops=10 * rows * width, bytes_accessed=rows * width * 8, transcendentals=rows * width),
        name="finish",
    )(raw, square, gain.reshape(1, width), gate)


def soft_kernel(pos, q_ref, *refs, group, first, last, distance):
    keys, values, refs = refs[:PLANE], refs[PLANE : 2 * PLANE], refs[2 * PLANE :]
    if not first:
        acc_in, stat_in, refs = refs[0], refs[1], refs[2:]
    acc_out = refs[0]
    stat_out = None if last else refs[1]
    rows = q_ref.shape[0]
    lane = iota((rows, HD), 1)

    def attend():
        ones = jnp.ones((rows, HD), BF16)
        wide = [jnp.concatenate([v[...], ones], axis=1) for v in values]
        keyed = [k[...] for k in keys]
        if first:
            causal = iota((rows, rows), 0) >= iota((rows, rows), 1)
            x_later, core_later = pos[1] == 1, pos[2] == 1
            bias = [jnp.where(flag, 0.0, LOW).astype(F32) for flag in (x_later, core_later, x_later)]
        stat = jnp.zeros((rows, HD), F32)
        for g in range(group):
            cols = slice(g * HD, (g + 1) * HD)
            query = q_ref[:, cols]
            scores = [mm_bt(query, k) for k in keyed]
            if first:
                scores = [jnp.where(causal, scores[0], LOW)] + [s + b for s, b in zip(scores[1:], bias)]
            top = jnp.maximum(jnp.maximum(scores[0], scores[1]), jnp.maximum(scores[2], scores[3]))
            top = jnp.max(top, axis=1, keepdims=True)
            if not first:
                before = stat_in[0, :, g : g + 1]
                top = jnp.maximum(top, before)
            shift = top * SCALE2
            out = None
            for s, v in zip(scores, wide):
                probs = jnp.exp2(s * SCALE2 - shift).astype(BF16)
                piece = mm(probs, v)
                out = piece if out is None else out + piece
            summed, total = out[:, :HD], out[:, HD:]
            if not first:
                keep = jnp.exp2(before * SCALE2 - shift)
                summed = summed + keep * acc_in[:, cols]
                total = total + keep * stat_in[0, :, group + g : group + g + 1]
            if last:
                acc_out[:, cols] = (summed / total).astype(BF16)
            else:
                acc_out[:, cols] = summed
                stat = jnp.where(lane == g, top, stat)
                stat = jnp.where(lane == group + g, total, stat)
        if not last:
            stat_out[0] = stat

    def passing():
        for g in range(group):
            cols = slice(g * HD, (g + 1) * HD)
            if last:
                acc_out[:, cols] = (acc_in[:, cols] / stat_in[0, :, group + g : group + g + 1]).astype(BF16)
            else:
                acc_out[:, cols] = acc_in[:, cols]
        if not last:
            stat_out[0] = stat_in[0]

    if first:
        attend()
    else:
        pl.when(pos[0] >= distance)(attend)
        pl.when(pos[0] < distance)(passing)


def soft_step(pos, query, pieces, state, kv_count, distance, last):
    rows, width = query.shape
    halves = 2
    group = width // HD // kv_count // halves
    first = state is None
    block = pl.BlockSpec((rows, group * HD), lambda k, h: (0, k * halves + h))
    stat = pl.BlockSpec((1, rows, HD), lambda k, h: (k * halves + h, 0, 0))
    keys = pl.BlockSpec((rows, HD), lambda k, h: (0, k))
    values = pl.BlockSpec((rows, HD), lambda k, h: (0, kv_count + k))
    in_specs = [pl.BlockSpec(memory_space=pltpu.SMEM), block] + [keys] * PLANE + [values] * PLANE
    operands = [pos, query] + pieces + pieces
    aliases = {}
    if not first:
        if not last:
            aliases = {len(operands): 0, len(operands) + 1: 1}
        in_specs += [block, stat]
        operands += list(state)
    out_specs = [block]
    out_shape = [jax.ShapeDtypeStruct((rows, width), BF16 if last else F32)]
    if not last:
        out_specs.append(stat)
        out_shape.append(jax.ShapeDtypeStruct((kv_count * halves, rows, HD), F32))
    return pl.pallas_call(
        functools.partial(soft_kernel, group=group, first=first, last=last, distance=distance),
        grid=(kv_count, halves),
        in_specs=in_specs,
        out_specs=out_specs,
        out_shape=out_shape,
        input_output_aliases=aliases,
        compiler_params=params(),
        cost_estimate=pl.CostEstimate(
            flops=8 * rows * rows * PLANE * width, bytes_accessed=rows * width * 12, transcendentals=rows * rows * PLANE * width // HD
        ),
        name="softmax",
    )(*operands)


def local(
    light_query,
    light_key,
    light_value,
    log_decay,
    out_gate,
    norm_gain,
    soft_query,
    soft_key,
    soft_value,
    *,
    ctx,
    tp,
):
    rows, heads = log_decay.shape
    qh = heads // 4
    length = qh * HD + TAIL
    planes = ctx // PLANE
    kv_count = soft_key.shape[1] // HD
    place = lax.axis_index("ctx")
    pos = jnp.stack([place // 4, (place // 2) % 2, place % 2]).astype(jnp.int32)

    def over_core(a):
        return lax.ppermute(a, "ctx", [(i, i ^ 1) for i in range(ctx)])

    def over_x(a):
        return lax.ppermute(a, "ctx", [(i, i ^ 2) for i in range(ctx)])

    def over_z(a, d):
        return lax.ppermute(a, "ctx", [(i, i + PLANE * d) for i in range(ctx - PLANE * d)])

    paired = jnp.concatenate([soft_key, soft_value], axis=1)
    arrived = [paired] + [over_z(paired, d) for d in range(1, planes)]
    pieces = []
    for a in arrived:
        b = over_x(a)
        pieces.append([a, b, over_core(a), over_core(b)])

    send, keep, cum, cumt = local_state(pos, light_key, light_value, log_decay)
    other = over_core(send)
    quarter = (length, HD)
    chip_send, chip_keep = small(chip_kernel, pos, [keep, other], [quarter, quarter], qh, "chip")
    chip_other = over_x(chip_send)
    (plane,) = small(plane_kernel, pos, [chip_keep, chip_other], [quarter], qh, "plane")
    earlier = [over_z(plane, d) for d in range(1, planes)]
    enter_send, enter_keep = small(
        enter_kernel, pos, [chip_keep, chip_other] + earlier, [quarter, quarter], qh, "enter"
    )
    enter_other = over_x(enter_send)
    half = (2, qh * HD, HD)
    state_send, state_keep = small(
        core_kernel, pos, [enter_keep, enter_other, keep, other], [half, half], qh, "core"
    )
    state_other = over_core(state_send)

    inner = intra(light_query, light_key, light_value, cum, cumt)
    raw, square = carry(pos, light_query, inner, cum, state_keep, state_other)
    step = 1
    while step < tp:
        square = square + lax.ppermute(square, "tp", [(i, i ^ step) for i in range(tp)])
        step *= 2
    light_out = finish(raw, square, norm_gain, out_gate, heads * HD * tp)

    state = None
    for d, piece in enumerate(pieces):
        state = soft_step(pos, soft_query, piece, state, kv_count, d, d == planes - 1)
    return (light_out, state[0])


def solution(mesh):
    both = P("ctx", "tp")
    return jax.shard_map(
        functools.partial(local, ctx=mesh.shape["ctx"], tp=mesh.shape["tp"]),
        mesh=mesh,
        in_specs=(both, both, both, both, both, P("tp"), both, both, both),
        out_specs=(both, both),
        check_vma=False,
    )
```

```python
import functools
import math

import jax
import jax.numpy as jnp
from jax import lax
from jax.experimental import pallas as pl
from jax.experimental.pallas import tpu as pltpu
from jax.sharding import PartitionSpec as P

HD = 128
EPS = 1e-06
LOW = -1e30
PLANE = 4
TAIL = 16
VMEM = 60 * 2**20
F32 = jnp.float32
BF16 = jnp.bfloat16
HIGH = lax.Precision.HIGHEST
SCALAR = pl.BlockSpec(memory_space=pltpu.SMEM)
ANY = pl.BlockSpec(memory_space=pl.ANY)
NEXT = jax.ShapeDtypeStruct((1,), jnp.int32)
COST = pl.CostEstimate(flops=1000, bytes_accessed=2**20, transcendentals=0)
SCALE2 = HD ** (-0.5) * math.log2(math.e)


def params(**more):
    return pltpu.CompilerParams(vmem_limit_bytes=VMEM, **more)


def mm(a, b):
    return lax.dot_general(a, b, (((1,), (0,)), ((), ())), preferred_element_type=F32)


def mm_bt(a, b):
    return lax.dot_general(a, b, (((1,), (1,)), ((), ())), preferred_element_type=F32)


def mm_at(a, b):
    return lax.dot_general(a, b, (((0,), (0,)), ((), ())), preferred_element_type=F32)


def z_of(pos):
    return pos[0] // PLANE


def x_of(pos):
    return (pos[0] // 2) % 2


def core_of(pos):
    return pos[0] % 2


def iota(shape, dim):
    return lax.broadcasted_iota(jnp.int32, shape, dim)


def state_kernel(pos, k_ref, v_ref, ld_ref, send_ref, keep_ref, cum_ref, cumt_ref, after, fin, *, qh, heads):
    after[0] = pos[0]
    step = pl.program_id(0)
    rows = ld_ref.shape[1]

    @pl.when(step == 0)
    def _():
        upper = (iota((rows, rows), 0) <= iota((rows, rows), 1)).astype(F32).astype(BF16)
        ld = ld_ref[...]
        high = ld.astype(BF16)
        rest = ld - high.astype(F32)
        middle = rest.astype(BF16)
        low = (rest - middle.astype(F32)).astype(BF16)
        cumt = mm(high, upper) + (mm(middle, upper) + mm(low, upper))
        full = jnp.concatenate([cumt, jnp.zeros((HD - heads, rows), F32)], axis=0)
        cum = jnp.transpose(full)
        ends = jnp.broadcast_to(cumt[:, rows - 1 : rows], (heads, HD))
        fin[...] = jnp.zeros_like(fin)
        cumt_ref[...] = jnp.zeros_like(cumt_ref)
        cum_ref[...] = jnp.zeros_like(cum_ref)
        for i in range(4):
            cum_ref[i, :, 0:qh] = cum[:, i * qh : (i + 1) * qh]
            cumt_ref[i, 0:qh, :] = cumt[i * qh : (i + 1) * qh, :]
            fin[i, 0:qh, :] = ends[i * qh : (i + 1) * qh, :]

    core = pos[0] & 1
    kept = step // 2
    part = step % 2
    quarter = part * 2 + jnp.where(kept == 1, core, 1 - core)
    cum = cum_ref[quarter]
    weight = jnp.exp(cum[rows - 1 : rows, :] - cum)
    tail = fin[quarter]
    high = tail.astype(BF16).astype(F32)
    tail = jnp.concatenate([high, tail - high], axis=0).astype(BF16)
    states = []
    for i in range(qh):
        cols = slice(i * HD, (i + 1) * HD)
        keyed = (k_ref[:, cols].astype(F32) * weight[:, i : i + 1]).astype(BF16)
        states.append(mm_at(keyed, v_ref[:, cols]).astype(BF16))

    def put(ref):
        for i in range(qh):
            ref[part, i * HD : (i + 1) * HD, :] = states[i]
        ref[part, qh * HD : qh * HD + TAIL, :] = tail

    @pl.when(kept == 0)
    def _():
        put(send_ref)

    @pl.when(kept == 1)
    def _():
        put(keep_ref)


def local_state(pos, key, value, log_decay):
    heads, rows = log_decay.shape
    qh = heads // 4
    length = qh * HD + TAIL

    def columns(step, pos):
        core = pos[0] & 1
        return (0, (step % 2) * 2 + jnp.where(step // 2 == 1, core, 1 - core))

    whole = lambda *shape: pl.BlockSpec(shape, lambda step, pos: (0,) * len(shape))
    return pl.pallas_call(
        functools.partial(state_kernel, qh=qh, heads=heads),
        grid_spec=pltpu.PrefetchScalarGridSpec(
            num_scalar_prefetch=1,
            grid=(4,),
            in_specs=[
                pl.BlockSpec((rows, qh * HD), columns),
                pl.BlockSpec((rows, qh * HD), columns),
                whole(heads, rows),
            ],
            out_specs=[
                whole(2, length, HD),
                whole(2, length, HD),
                whole(4, rows, HD),
                whole(4, 8, rows),
                SCALAR,
            ],
            scratch_shapes=[pltpu.VMEM((4, 8, HD), F32)],
        ),
        out_shape=[
            jax.ShapeDtypeStruct((2, length, HD), BF16),
            jax.ShapeDtypeStruct((2, length, HD), BF16),
            jax.ShapeDtypeStruct((4, rows, HD), F32),
            jax.ShapeDtypeStruct((4, 8, rows), F32),
            NEXT,
        ],
        compiler_params=params(),
        cost_estimate=COST,
        name="local_state",
    )(pos, key, value, log_decay)


def spread(item, qh):
    tail = item[qh * HD : qh * HD + TAIL, :].astype(F32)
    return item[0 : qh * HD, :].astype(F32), tail[0:8, :] + tail[8:16, :]


def pack(states, logs):
    high = logs.astype(BF16).astype(F32)
    return states.astype(BF16), jnp.concatenate([high, logs - high], axis=0).astype(BF16)


def decay(states, logs, qh):
    factor = jnp.exp(logs)
    return jnp.concatenate(
        [states[i * HD : (i + 1) * HD, :] * factor[i : i + 1, :] for i in range(qh)], axis=0
    )


def joined(early, late, qh):
    return decay(early[0], late[1], qh) + late[0], early[1] + late[1]


def store(ref, item, qh):
    states, tail = pack(*item)
    ref[0 : qh * HD, :] = states
    ref[qh * HD : qh * HD + TAIL, :] = tail


def chip_kernel(pos, keep_ref, recv_ref, send_out, keep_out, *, qh):
    first = core_of(pos) == 0
    for out, part in ((send_out, 1 - x_of(pos)), (keep_out, x_of(pos))):
        own, other = keep_ref[part], recv_ref[part]
        early = spread(jnp.where(first, own, other), qh)
        late = spread(jnp.where(first, other, own), qh)
        store(out, joined(early, late, qh), qh)


def plane_kernel(pos, keep_ref, recv_ref, out, *, qh):
    first = x_of(pos) == 0
    own, other = keep_ref[...], recv_ref[...]
    early = spread(jnp.where(first, own, other), qh)
    late = spread(jnp.where(first, other, own), qh)
    store(out, joined(early, late, qh), qh)


def enter_kernel(pos, keep_ref, recv_ref, *refs, qh):
    planes, (send_out, keep_out) = refs[:-2], refs[-2:]
    total = None
    for ref in reversed(planes):
        item = spread(ref[...], qh)
        total = item if total is None else joined(total, item, qh)
    first = x_of(pos) == 0
    early = spread(jnp.where(first, keep_ref[...], recv_ref[...]), qh)
    if total is None:
        total = (jnp.zeros_like(early[0]), jnp.zeros_like(early[1]))
    later = joined(total, early, qh)
    zero, one = pack(*total), pack(*later)
    for out, take in ((send_out, first), (keep_out, jnp.logical_not(first))):
        out[0 : qh * HD, :] = jnp.where(take, one[0], zero[0])
        out[qh * HD : qh * HD + TAIL, :] = jnp.where(take, one[1], zero[1])


def core_kernel(pos, enter_keep, enter_recv, keep_ref, recv_ref, send_out, keep_out, *, qh):
    first = core_of(pos) == 0
    for part in range(2):
        entering = spread(jnp.where(x_of(pos) == part, enter_keep[...], enter_recv[...]), qh)
        own = spread(jnp.where(first, keep_ref[part], recv_ref[part]), qh)
        later = joined(entering, own, qh)[0].astype(BF16)
        now = entering[0].astype(BF16)
        send_out[part] = jnp.where(first, later, now)
        keep_out[part] = jnp.where(first, now, later)


def with_token(kernel, pos, token, *refs):
    refs[-1][0] = token[0]
    kernel(pos, *refs[:-1])


def small(kernel, pos, arrays, outs, qh, name, token):
    return pl.pallas_call(
        functools.partial(with_token, functools.partial(kernel, qh=qh)),
        in_specs=[SCALAR, SCALAR] + [pl.BlockSpec(memory_space=pltpu.VMEM)] * len(arrays),
        out_specs=[pl.BlockSpec(memory_space=pltpu.VMEM)] * len(outs) + [SCALAR],
        out_shape=[jax.ShapeDtypeStruct(s, BF16) for s in outs] + [NEXT],
        compiler_params=pltpu.CompilerParams(vmem_limit_bytes=24 * 2**20),
        cost_estimate=COST,
        name=name,
    )(pos, token, *arrays)


def light_kernel(pos, q_ref, k_ref, v_ref, cum_ref, cumt_ref, keep_ref, recv_ref, token, out_ref, ss_ref, after, *, qh):
    after[0] = token[0]
    rows = q_ref.shape[0]
    quarter = pl.program_id(0)
    part = quarter // 2
    mine = quarter % 2 == core_of(pos)
    causal = iota((rows, rows), 0) >= iota((rows, rows), 1)
    cum, cumt = cum_ref[0], cumt_ref[0]
    factor = jnp.exp(cum)
    state = jnp.where(mine, keep_ref[part], recv_ref[part])
    total = jnp.zeros((rows, HD), F32)
    for i in range(qh):
        cols = slice(i * HD, (i + 1) * HD)
        query = q_ref[:, cols]
        scores = mm_bt(query, k_ref[:, cols])
        gap = jnp.where(causal, cum[:, i : i + 1] - cumt[i : i + 1, :], LOW)
        weights = (scores * jnp.exp(gap)).astype(BF16)
        carried = mm(query, state[i * HD : (i + 1) * HD, :])
        raw = mm(weights, v_ref[:, cols]) + factor[:, i : i + 1] * carried
        out_ref[:, cols] = raw.astype(BF16)
        total = total + raw * raw

    @pl.when(quarter == 0)
    def _():
        ss_ref[...] = total

    @pl.when(quarter > 0)
    def _():
        ss_ref[...] += total


def light(pos, query, key, value, cum, cumt, keep, recv, token):
    rows, width = query.shape
    wide = width // 4
    block = pl.BlockSpec((rows, wide), lambda i: (0, i))
    whole = pl.BlockSpec(keep.shape, lambda i: (0, 0, 0))
    return pl.pallas_call(
        functools.partial(light_kernel, qh=wide // HD),
        grid=(4,),
        in_specs=[
            SCALAR,
            block,
            block,
            block,
            pl.BlockSpec((1, rows, HD), lambda i: (i, 0, 0)),
            pl.BlockSpec((1, 8, rows), lambda i: (i, 0, 0)),
            whole,
            whole,
            SCALAR,
        ],
        out_specs=[block, pl.BlockSpec((rows, HD), lambda i: (0, 0)), SCALAR],
        out_shape=[jax.ShapeDtypeStruct((rows, width), BF16), jax.ShapeDtypeStruct((rows, HD), F32), NEXT],
        compiler_params=params(),
        cost_estimate=COST,
        name="light",
    )(pos, query, key, value, cum, cumt, keep, recv, token)


def finish_kernel(raw_ref, ss_ref, gain_ref, gate_ref, token, out_ref, *, features):
    mean = jnp.sum(ss_ref[...], axis=1, keepdims=True) / features
    factor = lax.rsqrt(mean + EPS)
    gate = 0.5 * jnp.tanh(0.5 * gate_ref[...].astype(F32)) + 0.5
    out_ref[...] = (raw_ref[...].astype(F32) * factor * gain_ref[...] * gate).astype(BF16)


def finish(raw, square, gain, gate, features, token):
    rows, width = raw.shape
    wide = min(width, 512)
    block = pl.BlockSpec((rows, wide), lambda i: (0, i))
    return pl.pallas_call(
        functools.partial(finish_kernel, features=features),
        grid=(width // wide,),
        in_specs=[
            block,
            pl.BlockSpec((rows, HD), lambda i: (0, 0)),
            pl.BlockSpec((1, wide), lambda i: (0, i)),
            block,
            SCALAR,
        ],
        out_specs=block,
        out_shape=jax.ShapeDtypeStruct((rows, width), BF16),
        compiler_params=params(),
        cost_estimate=COST,
        name="finish",
    )(raw, square, gain.reshape(1, width), gate, token)


def soft_kernel(pos, q_ref, *refs, group, distances, last, passed):
    chunks = []
    for _ in distances:
        chunks.append((refs[:PLANE], refs[PLANE : 2 * PLANE]))
        refs = refs[2 * PLANE :]
    first = distances[0] == 0
    if not first:
        acc_in, stat_in, refs = refs[0], refs[1], refs[2:]
    token, refs = refs[0], refs[passed:]
    if last:
        out_ref, after, acc, stat = refs
    else:
        acc, stat, after = refs
        stat = stat.at[0]
    after[0] = token[0]
    rows = q_ref.shape[0]
    lane = iota((rows, HD), 1)
    pair = min(group, 2)

    if not first:
        acc[...] = acc_in[...]
        stat[...] = stat_in[0]

    def attend(keys, values, fresh):
        keyed = jnp.concatenate([k[...] for k in keys], axis=0)
        valued = jnp.concatenate([v[...] for v in values], axis=0)
        valued = jnp.concatenate([valued, jnp.ones_like(valued)], axis=1)
        if fresh:
            causal = iota((rows, rows), 0) >= iota((rows, rows), 1)
            part = iota((1, (PLANE - 1) * rows), 1) // rows
            shown = jnp.where(part == 1, core_of(pos), x_of(pos))
            bias = jnp.where(shown == 1, 0.0, LOW).astype(F32)

        def scored(i):
            query = jnp.concatenate([q_ref[:, g * HD : (g + 1) * HD] for g in range(i, i + pair)], axis=0)
            return mm_bt(query, keyed)

        def masked(s):
            return jnp.concatenate([jnp.where(causal, s[:, :rows], LOW), s[:, rows:] + bias], axis=1)

        scores = scored(0)
        for i in range(0, group, pair):
            ahead = scored(i + pair) if i + pair < group else None
            if fresh:
                scores = jnp.concatenate(
                    [masked(scores[n * rows : (n + 1) * rows]) for n in range(pair)], axis=0
                )
            top = jnp.max(scores, axis=1, keepdims=True)
            if not fresh:
                before = jnp.concatenate([stat[:, g : g + 1] for g in range(i, i + pair)], axis=0)
                top = jnp.maximum(top, before)
            shift = top * SCALE2
            probs = jnp.exp2(scores * SCALE2 - shift).astype(BF16)
            out = mm(probs, valued)
            for n in range(pair):
                g = i + n
                cols = slice(g * HD, (g + 1) * HD)
                band = slice(n * rows, (n + 1) * rows)
                summed, total = out[band, :HD], out[band, HD:]
                if not fresh:
                    keep = jnp.exp2(before[band] * SCALE2 - shift[band])
                    summed = summed + keep * acc[:, cols]
                    total = total + keep * stat[:, group + g : group + g + 1]
                acc[:, cols] = summed
                now = jnp.where(lane == g, top[band], stat[...])
                stat[...] = jnp.where(lane == group + g, total, now)
            scores = ahead

    for (keys, values), distance in zip(chunks, distances):
        if distance == 0:
            attend(keys, values, True)
        else:
            pl.when(z_of(pos) >= distance)(functools.partial(attend, keys, values, False))
    if last:
        for g in range(group):
            cols = slice(g * HD, (g + 1) * HD)
            out_ref[:, cols] = (acc[:, cols] / stat[:, group + g : group + g + 1]).astype(BF16)


def soft_step(pos, query, pieces, distances, state, into, span, kv_count, last, token):
    rows, width = query.shape
    group = width // HD // kv_count
    first = distances[0] == 0
    begin, count = span
    block = pl.BlockSpec((rows, group * HD), lambda k: (0, begin + k))
    stat = pl.BlockSpec((1, rows, HD), lambda k: (begin + k, 0, 0))
    keys = pl.BlockSpec((rows, HD), lambda k: (0, begin + k))
    values = pl.BlockSpec((rows, HD), lambda k: (0, kv_count + begin + k))
    in_specs = [SCALAR, block]
    operands = [pos, query]
    for d in distances:
        in_specs += [keys] * PLANE + [values] * PLANE
        operands += pieces[d] + pieces[d]
    aliases = {}
    if not first:
        if not last:
            aliases = {len(operands): 0, len(operands) + 1: 1}
        in_specs += [block, stat]
        operands += list(state)
    passed = 1
    in_specs.append(SCALAR)
    operands.append(token)
    if into is not None:
        passed += len(into)
        for i, a in enumerate(into):
            aliases[len(operands)] = i
            in_specs.append(ANY)
            operands.append(a)
    if last:
        out_specs = [block, SCALAR]
        out_shape = [jax.ShapeDtypeStruct((rows, width), BF16), NEXT]
        scratch = [pltpu.VMEM((rows, group * HD), F32), pltpu.VMEM((rows, HD), F32)]
    else:
        out_specs = [block, stat, SCALAR]
        out_shape = [
            jax.ShapeDtypeStruct((rows, width), F32),
            jax.ShapeDtypeStruct((kv_count, rows, HD), F32),
            NEXT,
        ]
        scratch = []
    return pl.pallas_call(
        functools.partial(soft_kernel, group=group, distances=distances, last=last, passed=passed),
        grid=(count,),
        in_specs=in_specs,
        out_specs=out_specs,
        out_shape=out_shape,
        scratch_shapes=scratch,
        input_output_aliases=aliases,
        compiler_params=params(),
        cost_estimate=COST,
        name="softmax",
    )(*operands)


def local(
    light_query,
    light_key,
    light_value,
    log_decay,
    out_gate,
    norm_gain,
    soft_query,
    soft_key,
    soft_value,
    *,
    ctx,
    tp,
):
    rows, heads = log_decay.shape
    qh = heads // 4
    length = qh * HD + TAIL
    planes = ctx // PLANE
    kv_count = soft_key.shape[1] // HD
    place = lax.axis_index("ctx")
    pos = place.astype(jnp.int32).reshape(1)

    def over_core(a):
        return lax.ppermute(a, "ctx", [(i, i ^ 1) for i in range(ctx)])

    def over_x(a):
        return lax.ppermute(a, "ctx", [(i, i ^ 2) for i in range(ctx)])

    def over_z(a, d):
        return lax.ppermute(a, "ctx", [(i, i + PLANE * d) for i in range(ctx - PLANE * d)])

    def after(a, token):
        return lax.optimization_barrier((a, token))[0]

    paired = jnp.concatenate([soft_key, soft_value], axis=1)
    crossed = over_x(paired)
    arrived = [paired]
    for _ in range(1, planes):
        arrived.append(over_z(arrived[-1], 1))
    pieces = [[paired, crossed, over_core(paired), over_core(crossed)]]

    half = max(kv_count // 2, 1)
    spans = [(0, half), (half, kv_count - half)] if kv_count > 1 else [(0, 1)]

    def soft(distances, state, last, token, span=None, into=None):
        *state, token = soft_step(
            pos, soft_query, pieces, distances, state, into, span or (0, kv_count), kv_count, last, token
        )
        return state, token

    send, keep, cum, cumt, token = local_state(
        pos, light_key, light_value, after(log_decay.T, pieces[0][2])
    )
    other = over_core(send)
    quarter = (length, HD)

    def cross(d, token):
        a = after(arrived[d], token)
        pieces.append([a, over_x(a)])

    def spread_core(d, token):
        pieces[d] += [over_core(after(a, token)) for a in pieces[d]]

    cross(1, token)
    state, token = soft((0,), None, False, token, spans[0])
    chip_send, chip_keep, token = small(chip_kernel, pos, [keep, other], [quarter, quarter], qh, "chip", token)
    chip_other = over_x(chip_send)
    cross(2, token)
    if len(spans) > 1:
        state, token = soft((0,), None, False, token, spans[1], state)
    plane, token = small(plane_kernel, pos, [chip_keep, chip_other], [quarter], qh, "plane", token)
    earlier = [over_z(plane, d) for d in range(1, planes)]
    spread_core(1, token)
    spread_core(2, token)
    for d in range(1, planes - 2):
        cross(d + 2, token)
        state, token = soft((d,), state, False, token)
        if d > 1:
            spread_core(d + 1, token)
    state, token = soft((planes - 2,), state, False, token, spans[0])
    enter_send, enter_keep, token = small(
        enter_kernel, pos, [chip_keep, chip_other] + earlier, [quarter, quarter], qh, "enter", token
    )
    enter_other = over_x(enter_send)
    if len(spans) > 1:
        state, token = soft((planes - 2,), state, False, token, spans[1])
    spread_core(planes - 1, token)
    both = (2, qh * HD, HD)
    state_send, state_keep, token = small(
        core_kernel, pos, [enter_keep, enter_other, keep, other], [both, both], qh, "core", token
    )
    state_other = over_core(state_send)
    soft_out, token = soft((planes - 1,), state, True, token, spans[0])
    raw, square, token = light(
        pos, light_query, light_key, light_value, cum, cumt, state_keep, state_other, token
    )
    step = 1
    while step < tp:
        square = square + lax.ppermute(square, "tp", [(i, i ^ step) for i in range(tp)])
        step *= 2
    if len(spans) > 1:
        soft_out, token = soft((planes - 1,), state, True, token, spans[1], soft_out)
    light_out = finish(raw, square, norm_gain, out_gate, heads * HD * tp, token)
    return (light_out, soft_out[0])


def solution(mesh):
    both = P("ctx", "tp")
    return jax.shard_map(
        functools.partial(local, ctx=mesh.shape["ctx"], tp=mesh.shape["tp"]),
        mesh=mesh,
        in_specs=(both, both, both, both, both, P("tp"), both, both, both),
        out_specs=(both, both),
        check_vma=False,
    )
```

```python
import functools
import math

import jax
import jax.numpy as jnp
from jax import lax
from jax.experimental import pallas as pl
from jax.experimental.pallas import tpu as pltpu
from jax.sharding import PartitionSpec as P

HD = 128
EPS = 1e-06
LOW = -1e30
LIMIT = 2.0**100
PLANE = 4
TAIL = 16
VMEM = 32 * 2**20
F32 = jnp.float32
BF16 = jnp.bfloat16
HIGH = lax.Precision.HIGHEST
SCALAR = pl.BlockSpec(memory_space=pltpu.SMEM)
ANY = pl.BlockSpec(memory_space=pl.ANY)
NEXT = jax.ShapeDtypeStruct((1,), jnp.int32)
COST = pl.CostEstimate(flops=1000, bytes_accessed=2**20, transcendentals=0)
SCALE2 = HD ** (-0.5) * math.log2(math.e)


def params(**more):
    return pltpu.CompilerParams(vmem_limit_bytes=VMEM, **more)


def mm(a, b):
    return lax.dot_general(a, b, (((1,), (0,)), ((), ())), preferred_element_type=F32)


def mm_bt(a, b):
    return lax.dot_general(a, b, (((1,), (1,)), ((), ())), preferred_element_type=F32)


def mm_at(a, b):
    return lax.dot_general(a, b, (((0,), (0,)), ((), ())), preferred_element_type=F32)


def z_of(pos):
    return pos[0] // PLANE


def x_of(pos):
    return (pos[0] // 2) % 2


def core_of(pos):
    return pos[0] % 2


def iota(shape, dim):
    return lax.broadcasted_iota(jnp.int32, shape, dim)


def state_kernel(pos, k_ref, v_ref, ld_ref, send_ref, keep_ref, cum_ref, cumt_ref, after, fin, *, qh, heads):
    after[0] = pos[0]
    step = pl.program_id(0)
    rows = ld_ref.shape[1]

    @pl.when(step == 0)
    def _():
        upper = (iota((rows, rows), 0) <= iota((rows, rows), 1)).astype(F32).astype(BF16)
        ld = ld_ref[...]
        high = ld.astype(BF16)
        rest = ld - high.astype(F32)
        middle = rest.astype(BF16)
        low = (rest - middle.astype(F32)).astype(BF16)
        cumt = mm(high, upper) + (mm(middle, upper) + mm(low, upper))
        full = jnp.concatenate([cumt, jnp.zeros((HD - heads, rows), F32)], axis=0)
        cum = jnp.transpose(full)
        ends = jnp.broadcast_to(cumt[:, rows - 1 : rows], (heads, HD))
        fin[...] = jnp.zeros_like(fin)
        cumt_ref[...] = jnp.zeros_like(cumt_ref)
        cum_ref[...] = jnp.zeros_like(cum_ref)
        for i in range(4):
            cum_ref[i, :, 0:qh] = cum[:, i * qh : (i + 1) * qh]
            cumt_ref[i, 0:qh, :] = cumt[i * qh : (i + 1) * qh, :]
            fin[i, 0:qh, :] = ends[i * qh : (i + 1) * qh, :]

    core = pos[0] & 1
    kept = step // 2
    part = step % 2
    quarter = part * 2 + jnp.where(kept == 1, core, 1 - core)
    cum = cum_ref[quarter]
    weight = jnp.exp(cum[rows - 1 : rows, :] - cum)
    tail = fin[quarter]
    high = tail.astype(BF16).astype(F32)
    tail = jnp.concatenate([high, tail - high], axis=0).astype(BF16)
    states = []
    for i in range(qh):
        cols = slice(i * HD, (i + 1) * HD)
        keyed = (k_ref[:, cols].astype(F32) * weight[:, i : i + 1]).astype(BF16)
        states.append(mm_at(keyed, v_ref[:, cols]).astype(BF16))

    def put(ref):
        for i in range(qh):
            ref[part, i * HD : (i + 1) * HD, :] = states[i]
        ref[part, qh * HD : qh * HD + TAIL, :] = tail

    @pl.when(kept == 0)
    def _():
        put(send_ref)

    @pl.when(kept == 1)
    def _():
        put(keep_ref)


def local_state(pos, key, value, log_decay):
    heads, rows = log_decay.shape
    qh = heads // 4
    length = qh * HD + TAIL

    def columns(step, pos):
        core = pos[0] & 1
        return (0, (step % 2) * 2 + jnp.where(step // 2 == 1, core, 1 - core))

    whole = lambda *shape: pl.BlockSpec(shape, lambda step, pos: (0,) * len(shape))
    return pl.pallas_call(
        functools.partial(state_kernel, qh=qh, heads=heads),
        grid_spec=pltpu.PrefetchScalarGridSpec(
            num_scalar_prefetch=1,
            grid=(4,),
            in_specs=[
                pl.BlockSpec((rows, qh * HD), columns),
                pl.BlockSpec((rows, qh * HD), columns),
                whole(heads, rows),
            ],
            out_specs=[
                whole(2, length, HD),
                whole(2, length, HD),
                whole(4, rows, HD),
                whole(4, 8, rows),
                SCALAR,
            ],
            scratch_shapes=[pltpu.VMEM((4, 8, HD), F32)],
        ),
        out_shape=[
            jax.ShapeDtypeStruct((2, length, HD), BF16),
            jax.ShapeDtypeStruct((2, length, HD), BF16),
            jax.ShapeDtypeStruct((4, rows, HD), F32),
            jax.ShapeDtypeStruct((4, 8, rows), F32),
            NEXT,
        ],
        compiler_params=params(),
        cost_estimate=COST,
        name="local_state",
    )(pos, key, value, log_decay)


def spread(item, qh):
    tail = item[qh * HD : qh * HD + TAIL, :].astype(F32)
    return item[0 : qh * HD, :].astype(F32), tail[0:8, :] + tail[8:16, :]


def pack(states, logs):
    high = logs.astype(BF16).astype(F32)
    return states.astype(BF16), jnp.concatenate([high, logs - high], axis=0).astype(BF16)


def decay(states, logs, qh):
    factor = jnp.exp(logs)
    return jnp.concatenate(
        [states[i * HD : (i + 1) * HD, :] * factor[i : i + 1, :] for i in range(qh)], axis=0
    )


def joined(early, late, qh):
    return decay(early[0], late[1], qh) + late[0], early[1] + late[1]


def store(ref, item, qh):
    states, tail = pack(*item)
    ref[0 : qh * HD, :] = states
    ref[qh * HD : qh * HD + TAIL, :] = tail


def chip_kernel(pos, keep_ref, recv_ref, send_out, keep_out, *, qh):
    first = core_of(pos) == 0
    for out, part in ((send_out, 1 - x_of(pos)), (keep_out, x_of(pos))):
        own, other = keep_ref[part], recv_ref[part]
        early = spread(jnp.where(first, own, other), qh)
        late = spread(jnp.where(first, other, own), qh)
        store(out, joined(early, late, qh), qh)


def plane_kernel(pos, keep_ref, recv_ref, out, *, qh):
    first = x_of(pos) == 0
    own, other = keep_ref[...], recv_ref[...]
    early = spread(jnp.where(first, own, other), qh)
    late = spread(jnp.where(first, other, own), qh)
    store(out, joined(early, late, qh), qh)


def enter_kernel(pos, keep_ref, recv_ref, *refs, qh):
    planes, (send_out, keep_out) = refs[:-2], refs[-2:]
    total = None
    for ref in reversed(planes):
        item = spread(ref[...], qh)
        total = item if total is None else joined(total, item, qh)
    first = x_of(pos) == 0
    early = spread(jnp.where(first, keep_ref[...], recv_ref[...]), qh)
    if total is None:
        total = (jnp.zeros_like(early[0]), jnp.zeros_like(early[1]))
    later = joined(total, early, qh)
    zero, one = pack(*total), pack(*later)
    for out, take in ((send_out, first), (keep_out, jnp.logical_not(first))):
        out[0 : qh * HD, :] = jnp.where(take, one[0], zero[0])
        out[qh * HD : qh * HD + TAIL, :] = jnp.where(take, one[1], zero[1])


def core_kernel(pos, enter_keep, enter_recv, keep_ref, recv_ref, send_out, keep_out, *, qh):
    first = core_of(pos) == 0
    for part in range(2):
        entering = spread(jnp.where(x_of(pos) == part, enter_keep[...], enter_recv[...]), qh)
        own = spread(jnp.where(first, keep_ref[part], recv_ref[part]), qh)
        later = joined(entering, own, qh)[0].astype(BF16)
        now = entering[0].astype(BF16)
        send_out[part] = jnp.where(first, later, now)
        keep_out[part] = jnp.where(first, now, later)


def with_token(kernel, pos, token, *refs):
    refs[-1][0] = token[0]
    kernel(pos, *refs[:-1])


def small(kernel, pos, arrays, outs, qh, name, token):
    return pl.pallas_call(
        functools.partial(with_token, functools.partial(kernel, qh=qh)),
        in_specs=[SCALAR, SCALAR] + [pl.BlockSpec(memory_space=pltpu.VMEM)] * len(arrays),
        out_specs=[pl.BlockSpec(memory_space=pltpu.VMEM)] * len(outs) + [SCALAR],
        out_shape=[jax.ShapeDtypeStruct(s, BF16) for s in outs] + [NEXT],
        compiler_params=pltpu.CompilerParams(vmem_limit_bytes=24 * 2**20),
        cost_estimate=COST,
        name=name,
    )(pos, token, *arrays)


def light_kernel(pos, q_ref, k_ref, v_ref, cum_ref, cumt_ref, keep_ref, recv_ref, token, out_ref, ss_ref, after, *, qh):
    after[0] = token[0]
    rows = q_ref.shape[0]
    quarter = pl.program_id(0)
    part = quarter // 2
    mine = quarter % 2 == core_of(pos)
    causal = iota((rows, rows), 0) >= iota((rows, rows), 1)
    cum, cumt = cum_ref[0], cumt_ref[0]
    factor = jnp.exp(cum)
    state = jnp.where(mine, keep_ref[part], recv_ref[part])
    total = jnp.zeros((rows, HD), F32)
    for i in range(qh):
        cols = slice(i * HD, (i + 1) * HD)
        query = q_ref[:, cols]
        scores = mm_bt(query, k_ref[:, cols])
        gap = jnp.where(causal, cum[:, i : i + 1] - cumt[i : i + 1, :], LOW)
        weights = (scores * jnp.exp(gap)).astype(BF16)
        carried = mm(query, state[i * HD : (i + 1) * HD, :])
        raw = mm(weights, v_ref[:, cols]) + factor[:, i : i + 1] * carried
        out_ref[:, cols] = raw.astype(BF16)
        total = total + raw * raw

    @pl.when(quarter == 0)
    def _():
        ss_ref[...] = total

    @pl.when(quarter > 0)
    def _():
        ss_ref[...] += total


def light(pos, query, key, value, cum, cumt, keep, recv, token):
    rows, width = query.shape
    wide = width // 4
    block = pl.BlockSpec((rows, wide), lambda i: (0, i))
    whole = pl.BlockSpec(keep.shape, lambda i: (0, 0, 0))
    return pl.pallas_call(
        functools.partial(light_kernel, qh=wide // HD),
        grid=(4,),
        in_specs=[
            SCALAR,
            block,
            block,
            block,
            pl.BlockSpec((1, rows, HD), lambda i: (i, 0, 0)),
            pl.BlockSpec((1, 8, rows), lambda i: (i, 0, 0)),
            whole,
            whole,
            SCALAR,
        ],
        out_specs=[block, pl.BlockSpec((rows, HD), lambda i: (0, 0)), SCALAR],
        out_shape=[jax.ShapeDtypeStruct((rows, width), BF16), jax.ShapeDtypeStruct((rows, HD), F32), NEXT],
        compiler_params=params(),
        cost_estimate=COST,
        name="light",
    )(pos, query, key, value, cum, cumt, keep, recv, token)


def finish_kernel(raw_ref, *refs, features):
    squares, (gain_ref, gate_ref, token, out_ref, factor) = refs[:-5], refs[-5:]

    @pl.when(pl.program_id(0) == 0)
    def _():
        square = squares[0][...]
        for more in squares[1:]:
            square = square + more[...]
        mean = jnp.sum(square, axis=1, keepdims=True) / features
        factor[...] = jnp.broadcast_to(lax.rsqrt(mean + EPS), factor.shape)

    for i in range(out_ref.shape[1] // HD):
        cols = slice(i * HD, (i + 1) * HD)
        gate = 0.5 * jnp.tanh(0.5 * gate_ref[:, cols].astype(F32)) + 0.5
        raw = raw_ref[:, cols].astype(F32)
        out_ref[:, cols] = (raw * factor[...] * gain_ref[:, cols] * gate).astype(BF16)


def finish(raw, squares, gain, gate, features, token):
    rows, width = raw.shape
    wide = width // 4
    block = pl.BlockSpec((rows, wide), lambda i: (0, i))
    return pl.pallas_call(
        functools.partial(finish_kernel, features=features),
        grid=(4,),
        in_specs=[block]
        + [pl.BlockSpec((rows, HD), lambda i: (0, 0))] * len(squares)
        + [pl.BlockSpec((1, wide), lambda i: (0, i)), block, SCALAR],
        out_specs=block,
        out_shape=jax.ShapeDtypeStruct((rows, width), BF16),
        scratch_shapes=[pltpu.VMEM((rows, HD), F32)],
        compiler_params=params(),
        cost_estimate=COST,
        name="finish",
    )(raw, *squares, gain.reshape(1, width), gate, token)


def soft_kernel(pos, q_ref, *refs, group, distances, planes, last, passed):
    count = planes * PLANE if last else len(distances) * PLANE
    keys, values, refs = refs[:count], refs[count : 2 * count], refs[2 * count :]
    first = distances[0] == 0
    if not first:
        acc_in, stat_in, refs = refs[0], refs[1], refs[2:]
    token, refs = refs[0], refs[passed:]
    if last:
        out_ref, after, acc, stat = refs
    else:
        acc, stat, after = refs
        stat = stat.at[0]
    after[0] = token[0]
    rows = q_ref.shape[0]
    lane = iota((rows, HD), 1)
    causal = iota((rows, rows), 0) >= iota((rows, rows), 1)
    pair = min(group, 2)
    flags = [None, x_of(pos) == 1, core_of(pos) == 1, x_of(pos) == 1]

    if not first:
        acc[...] = acc_in[...]
        stat[...] = stat_in[0]

    def attend(keyed, valued, fresh):
        wide = jnp.concatenate([v[...] for v in valued], axis=0)
        wide = jnp.concatenate([wide, jnp.ones_like(wide)], axis=1)
        if fresh:
            own = keyed[0][...].astype(F32)
            shifts = [
                jnp.sum(q_ref[:, g * HD : (g + 1) * HD].astype(F32) * own, axis=1, keepdims=True) * SCALE2
                for g in range(group)
            ]
        else:
            shifts = [stat[:, g : g + 1] for g in range(group)]

        def scored(i):
            query = jnp.concatenate([q_ref[:, g * HD : (g + 1) * HD] for g in range(i, i + pair)], axis=0)
            return [mm_bt(query, k[...]) for k in keyed]

        scores = scored(0)
        for i in range(0, group, pair):
            ahead = scored(i + pair) if i + pair < group else None
            shift = jnp.concatenate(shifts[i : i + pair], axis=0)
            probs = []
            for n, s in enumerate(scores):
                if fresh and n > 0:
                    x = s * SCALE2 - (shift + jnp.where(flags[n], 0.0, -LOW).astype(F32))
                else:
                    x = s * SCALE2 - shift
                if fresh and n == 0:
                    x = jnp.concatenate(
                        [jnp.where(causal, x[m * rows : (m + 1) * rows], LOW) for m in range(pair)], axis=0
                    )
                probs.append(jnp.exp2(x).astype(BF16))
            out = mm(jnp.concatenate(probs, axis=1), wide)
            for n in range(pair):
                g = i + n
                cols = slice(g * HD, (g + 1) * HD)
                band = slice(n * rows, (n + 1) * rows)
                summed, total = out[band, :HD], out[band, HD:]
                if fresh:
                    acc[:, cols] = summed
                    old = jnp.where(lane == g, shifts[g], 0.0 if g == 0 else stat[...])
                    stat[...] = jnp.where(lane == group + g, total, old)
                else:
                    acc[:, cols] += summed
                    stat[...] += jnp.where(lane == group + g, total, 0.0)
            scores = ahead

    for n, distance in enumerate(distances):
        here = slice((distance if last else n) * PLANE, ((distance if last else n) + 1) * PLANE)
        if distance == 0:
            attend(keys[here], values[here], True)
        else:
            pl.when(z_of(pos) >= distance)(functools.partial(attend, keys[here], values[here], False))
    if not last:
        return
    for g in range(group):
        cols = slice(g * HD, (g + 1) * HD)
        out_ref[:, cols] = (acc[:, cols] / stat[:, group + g : group + g + 1]).astype(BF16)

    sums = jnp.where((lane >= group) & (lane < 2 * group), stat[...], 0.0)
    fine = jnp.min(jnp.where(sums < LIMIT, 1.0, 0.0))

    @pl.when(fine < 0.5)
    def _():
        def one(g, carry):
            cols = pl.ds(pl.multiple_of(g * HD, HD), HD)
            query = q_ref[:, cols]
            top = total = summed = None
            for n in range(count):
                x = mm_bt(query, keys[n][...]) * SCALE2
                if n == 0:
                    x = jnp.where(causal, x, LOW)
                else:
                    shown = flags[n] if n < PLANE else z_of(pos) >= n // PLANE
                    x = jnp.where(shown, x, LOW)
                high = jnp.max(x, axis=1, keepdims=True)
                if n > 0:
                    high = jnp.maximum(high, top)
                probs = jnp.exp2(x - high)
                part = mm(probs.astype(BF16), values[n][...])
                more = jnp.sum(probs, axis=1, keepdims=True)
                if n > 0:
                    keep = jnp.exp2(top - high)
                    part = part + keep * summed
                    more = more + keep * total
                top, total, summed = high, more, part
            out_ref[:, cols] = (summed / total).astype(BF16)
            return carry

        lax.fori_loop(0, group, one, 0)


def soft_step(pos, query, pieces, distances, state, into, span, kv_count, planes, last, token):
    rows, width = query.shape
    group = width // HD // kv_count
    first = distances[0] == 0
    begin, count = span
    block = pl.BlockSpec((rows, group * HD), lambda k: (0, begin + k))
    stat = pl.BlockSpec((1, rows, HD), lambda k: (begin + k, 0, 0))
    keys = pl.BlockSpec((rows, HD), lambda k: (0, begin + k))
    values = pl.BlockSpec((rows, HD), lambda k: (0, kv_count + begin + k))
    used = [a for d in (range(planes) if last else distances) for a in pieces[d]]
    in_specs = [SCALAR, block] + [keys] * len(used) + [values] * len(used)
    operands = [pos, query] + used + used
    aliases = {}
    if not first:
        if not last:
            aliases = {len(operands): 0, len(operands) + 1: 1}
        in_specs += [block, stat]
        operands += list(state)
    passed = 1
    in_specs.append(SCALAR)
    operands.append(token)
    if into is not None:
        passed += len(into)
        for i, a in enumerate(into):
            aliases[len(operands)] = i
            in_specs.append(ANY)
            operands.append(a)
    if last:
        out_specs = [block, SCALAR]
        out_shape = [jax.ShapeDtypeStruct((rows, width), BF16), NEXT]
        scratch = [pltpu.VMEM((rows, group * HD), F32), pltpu.VMEM((rows, HD), F32)]
    else:
        out_specs = [block, stat, SCALAR]
        out_shape = [
            jax.ShapeDtypeStruct((rows, width), F32),
            jax.ShapeDtypeStruct((kv_count, rows, HD), F32),
            NEXT,
        ]
        scratch = []
    return pl.pallas_call(
        functools.partial(
            soft_kernel, group=group, distances=distances, planes=planes, last=last, passed=passed
        ),
        grid=(count,),
        in_specs=in_specs,
        out_specs=out_specs,
        out_shape=out_shape,
        scratch_shapes=scratch,
        input_output_aliases=aliases,
        compiler_params=params(),
        cost_estimate=COST,
        name="softmax",
    )(*operands)


def local(
    light_query,
    light_key,
    light_value,
    log_decay,
    out_gate,
    norm_gain,
    soft_query,
    soft_key,
    soft_value,
    *,
    ctx,
    tp,
):
    rows, heads = log_decay.shape
    qh = heads // 4
    length = qh * HD + TAIL
    planes = ctx // PLANE
    kv_count = soft_key.shape[1] // HD
    place = lax.axis_index("ctx")
    pos = place.astype(jnp.int32).reshape(1)

    def over_core(a):
        return lax.ppermute(a, "ctx", [(i, i ^ 1) for i in range(ctx)])

    def over_x(a):
        return lax.ppermute(a, "ctx", [(i, i ^ 2) for i in range(ctx)])

    def over_z(a, d):
        return lax.ppermute(a, "ctx", [(i, i + PLANE * d) for i in range(ctx - PLANE * d)])

    def after(a, token):
        return lax.optimization_barrier((a, token))[0]

    paired = jnp.concatenate([soft_key, soft_value], axis=1)
    crossed = over_x(paired)
    arrived = [paired, over_z(paired, 1)]

    def forward(token):
        arrived.append(over_z(after(arrived[-1], token), 1))

    pieces = [[paired, crossed, over_core(paired), over_core(crossed)]]

    half = max(kv_count // 2, 1)
    spans = [(0, half), (half, kv_count - half)] if kv_count > 1 else [(0, 1)]

    def soft(distances, state, last, token, span=None, into=None):
        *state, token = soft_step(
            pos, soft_query, pieces, distances, state, into, span or (0, kv_count), kv_count, planes, last, token
        )
        return state, token

    send, keep, cum, cumt, token = local_state(
        pos, light_key, light_value, after(log_decay.T, pieces[0][2])
    )
    other = over_core(send)
    quarter = (length, HD)

    def cross(d, token):
        a = after(arrived[d], token)
        pieces.append([a, over_x(a)])

    def spread_core(d, token):
        pieces[d] += [over_core(after(a, token)) for a in pieces[d]]

    cross(1, token)
    forward(token)
    state, token = soft((0,), None, False, token, spans[0])
    chip_send, chip_keep, token = small(chip_kernel, pos, [keep, other], [quarter, quarter], qh, "chip", token)
    chip_other = over_x(chip_send)
    cross(2, token)
    forward(token)
    if len(spans) > 1:
        state, token = soft((0,), None, False, token, spans[1], state)
    plane, token = small(plane_kernel, pos, [chip_keep, chip_other], [quarter], qh, "plane", token)
    earlier = [over_z(plane, d) for d in range(1, planes)]
    spread_core(1, token)
    spread_core(2, token)
    cross(3, token)
    for d in range(3, planes - 1):
        forward(token)
        cross(d + 1, token)
    both = (2, qh * HD, HD)
    rest = (planes - 1,)
    for middle in [(1, 2)] + [(d,) for d in range(3, planes - 1)]:
        for n, span in enumerate(spans):
            state, token = soft(middle, state, False, token, span)
            if n == 0:
                spread_core(middle[-1] + 1, token)
    enter_send, enter_keep, token = small(
        enter_kernel, pos, [chip_keep, chip_other] + earlier, [quarter, quarter], qh, "enter", token
    )
    enter_other = over_x(enter_send)
    soft_out, token = soft(rest, state, True, token, spans[0])
    state_send, state_keep, token = small(
        core_kernel, pos, [enter_keep, enter_other, keep, other], [both, both], qh, "core", token
    )
    state_other = over_core(state_send)
    for span in spans[1:]:
        soft_out, token = soft(rest, state, True, token, span, soft_out)
    raw, square, token = light(
        pos, light_query, light_key, light_value, cum, cumt, state_keep, state_other, token
    )
    squares = [square]
    step = 1
    while step < tp:
        square = sum(squares)
        squares = [square, lax.ppermute(square, "tp", [(i, i ^ step) for i in range(tp)])]
        step *= 2
    light_out = finish(raw, squares, norm_gain, out_gate, heads * HD * tp, token)
    return (light_out, soft_out[0])


def solution(mesh):
    both = P("ctx", "tp")
    return jax.shard_map(
        functools.partial(local, ctx=mesh.shape["ctx"], tp=mesh.shape["tp"]),
        mesh=mesh,
        in_specs=(both, both, both, both, both, P("tp"), both, both, both),
        out_specs=(both, both),
        check_vma=False,
    )
```

```python
import functools
import math

import jax
import jax.numpy as jnp
from jax import lax
from jax.experimental import pallas as pl
from jax.experimental.pallas import tpu as pltpu
from jax.sharding import PartitionSpec as P

HD = 128
EPS = 1e-06
LOW = -1e30
LIMIT = 2.0**100
PLANE = 4
TAIL = 16
VMEM = 32 * 2**20
BIG = 60 * 2**20
F32 = jnp.float32
BF16 = jnp.bfloat16
HIGH = lax.Precision.HIGHEST
SCALAR = pl.BlockSpec(memory_space=pltpu.SMEM)
ANY = pl.BlockSpec(memory_space=pl.ANY)
NEXT = jax.ShapeDtypeStruct((1,), jnp.int32)
FORMS = [(4, False), (2, True), (4, True), (2, True), (4, False), (2, False)]
COST = pl.CostEstimate(flops=1000, bytes_accessed=2**20, transcendentals=0)
SCALE2 = HD ** (-0.5) * math.log2(math.e)


def params(limit=None):
    return pltpu.CompilerParams(vmem_limit_bytes=limit or VMEM)


def mm(a, b):
    return lax.dot_general(a, b, (((1,), (0,)), ((), ())), preferred_element_type=F32)


def mm_bt(a, b):
    return lax.dot_general(a, b, (((1,), (1,)), ((), ())), preferred_element_type=F32)


def mm_at(a, b):
    return lax.dot_general(a, b, (((0,), (0,)), ((), ())), preferred_element_type=F32)


def z_of(pos):
    return pos[0] // PLANE


def x_of(pos):
    return (pos[0] // 2) % 2


def core_of(pos):
    return pos[0] % 2


def iota(shape, dim):
    return lax.broadcasted_iota(jnp.int32, shape, dim)


def state_kernel(pos, k_ref, v_ref, ld_ref, send_ref, keep_ref, cum_ref, cumt_ref, after, fin, *, qh, heads):
    after[0] = pos[0]
    step = pl.program_id(0)
    rows = ld_ref.shape[1]

    @pl.when(step == 0)
    def _():
        upper = (iota((rows, rows), 0) <= iota((rows, rows), 1)).astype(F32).astype(BF16)
        ld = ld_ref[...]
        high = ld.astype(BF16)
        rest = ld - high.astype(F32)
        middle = rest.astype(BF16)
        low = (rest - middle.astype(F32)).astype(BF16)
        cumt = mm(high, upper) + (mm(middle, upper) + mm(low, upper))
        full = jnp.concatenate([cumt, jnp.zeros((HD - heads, rows), F32)], axis=0)
        cum = jnp.transpose(full)
        ends = jnp.broadcast_to(cumt[:, rows - 1 : rows], (heads, HD))
        fin[...] = jnp.zeros_like(fin)
        cumt_ref[...] = jnp.zeros_like(cumt_ref)
        cum_ref[...] = jnp.zeros_like(cum_ref)
        for i in range(4):
            cum_ref[i, :, 0:qh] = cum[:, i * qh : (i + 1) * qh]
            cumt_ref[i, 0:qh, :] = cumt[i * qh : (i + 1) * qh, :]
            fin[i, 0:qh, :] = ends[i * qh : (i + 1) * qh, :]

    core = pos[0] & 1
    kept = step // 2
    part = step % 2
    quarter = part * 2 + jnp.where(kept == 1, core, 1 - core)
    cum = cum_ref[quarter]
    weight = jnp.exp(cum[rows - 1 : rows, :] - cum)
    tail = fin[quarter]
    high = tail.astype(BF16).astype(F32)
    tail = jnp.concatenate([high, tail - high], axis=0).astype(BF16)
    states = []
    for i in range(qh):
        cols = slice(i * HD, (i + 1) * HD)
        keyed = (k_ref[:, cols].astype(F32) * weight[:, i : i + 1]).astype(BF16)
        states.append(mm_at(keyed, v_ref[:, cols]).astype(BF16))

    def put(ref):
        for i in range(qh):
            ref[part, i * HD : (i + 1) * HD, :] = states[i]
        ref[part, qh * HD : qh * HD + TAIL, :] = tail

    @pl.when(kept == 0)
    def _():
        put(send_ref)

    @pl.when(kept == 1)
    def _():
        put(keep_ref)


def local_state(pos, key, value, log_decay):
    heads, rows = log_decay.shape
    qh = heads // 4
    length = qh * HD + TAIL

    def columns(step, pos):
        core = pos[0] & 1
        return (0, (step % 2) * 2 + jnp.where(step // 2 == 1, core, 1 - core))

    whole = lambda *shape: pl.BlockSpec(shape, lambda step, pos: (0,) * len(shape))
    return pl.pallas_call(
        functools.partial(state_kernel, qh=qh, heads=heads),
        grid_spec=pltpu.PrefetchScalarGridSpec(
            num_scalar_prefetch=1,
            grid=(4,),
            in_specs=[
                pl.BlockSpec((rows, qh * HD), columns),
                pl.BlockSpec((rows, qh * HD), columns),
                whole(heads, rows),
            ],
            out_specs=[
                whole(2, length, HD),
                whole(2, length, HD),
                whole(4, rows, HD),
                whole(4, 8, rows),
                SCALAR,
            ],
            scratch_shapes=[pltpu.VMEM((4, 8, HD), F32)],
        ),
        out_shape=[
            jax.ShapeDtypeStruct((2, length, HD), BF16),
            jax.ShapeDtypeStruct((2, length, HD), BF16),
            jax.ShapeDtypeStruct((4, rows, HD), F32),
            jax.ShapeDtypeStruct((4, 8, rows), F32),
            NEXT,
        ],
        compiler_params=params(BIG),
        cost_estimate=COST,
        name="local_state",
    )(pos, key, value, log_decay)


def spread(item, qh):
    tail = item[qh * HD : qh * HD + TAIL, :].astype(F32)
    return item[0 : qh * HD, :].astype(F32), tail[0:8, :] + tail[8:16, :]


def pack(states, logs):
    high = logs.astype(BF16).astype(F32)
    return states.astype(BF16), jnp.concatenate([high, logs - high], axis=0).astype(BF16)


def decay(states, logs, qh):
    factor = jnp.exp(logs)
    return jnp.concatenate(
        [states[i * HD : (i + 1) * HD, :] * factor[i : i + 1, :] for i in range(qh)], axis=0
    )


def joined(early, late, qh):
    return decay(early[0], late[1], qh) + late[0], early[1] + late[1]


def store(ref, item, qh):
    states, tail = pack(*item)
    ref[0 : qh * HD, :] = states
    ref[qh * HD : qh * HD + TAIL, :] = tail


def chip_kernel(pos, keep_ref, recv_ref, send_out, keep_out, *, qh):
    first = core_of(pos) == 0
    for out, part in ((send_out, 1 - x_of(pos)), (keep_out, x_of(pos))):
        own, other = keep_ref[part], recv_ref[part]
        early = spread(jnp.where(first, own, other), qh)
        late = spread(jnp.where(first, other, own), qh)
        store(out, joined(early, late, qh), qh)


def plane_kernel(pos, keep_ref, recv_ref, out, *, qh):
    first = x_of(pos) == 0
    own, other = keep_ref[...], recv_ref[...]
    early = spread(jnp.where(first, own, other), qh)
    late = spread(jnp.where(first, other, own), qh)
    store(out, joined(early, late, qh), qh)


def enter_kernel(pos, keep_ref, recv_ref, *refs, qh):
    planes, (send_out, keep_out) = refs[:-2], refs[-2:]
    total = None
    for ref in reversed(planes):
        item = spread(ref[...], qh)
        total = item if total is None else joined(total, item, qh)
    first = x_of(pos) == 0
    early = spread(jnp.where(first, keep_ref[...], recv_ref[...]), qh)
    if total is None:
        total = (jnp.zeros_like(early[0]), jnp.zeros_like(early[1]))
    later = joined(total, early, qh)
    zero, one = pack(*total), pack(*later)
    for out, take in ((send_out, first), (keep_out, jnp.logical_not(first))):
        out[0 : qh * HD, :] = jnp.where(take, one[0], zero[0])
        out[qh * HD : qh * HD + TAIL, :] = jnp.where(take, one[1], zero[1])


def core_kernel(pos, enter_keep, enter_recv, keep_ref, recv_ref, send_out, keep_out, *, qh):
    first = core_of(pos) == 0
    for part in range(2):
        entering = spread(jnp.where(x_of(pos) == part, enter_keep[...], enter_recv[...]), qh)
        own = spread(jnp.where(first, keep_ref[part], recv_ref[part]), qh)
        later = joined(entering, own, qh)[0].astype(BF16)
        now = entering[0].astype(BF16)
        send_out[part] = jnp.where(first, later, now)
        keep_out[part] = jnp.where(first, now, later)


def with_token(kernel, pos, token, *refs):
    refs[-1][0] = token[0]
    kernel(pos, *refs[:-1])


def small(kernel, pos, arrays, outs, qh, name, token):
    return pl.pallas_call(
        functools.partial(with_token, functools.partial(kernel, qh=qh)),
        in_specs=[SCALAR, SCALAR] + [pl.BlockSpec(memory_space=pltpu.VMEM)] * len(arrays),
        out_specs=[pl.BlockSpec(memory_space=pltpu.VMEM)] * len(outs) + [SCALAR],
        out_shape=[jax.ShapeDtypeStruct(s, BF16) for s in outs] + [NEXT],
        compiler_params=pltpu.CompilerParams(vmem_limit_bytes=24 * 2**20),
        cost_estimate=COST,
        name=name,
    )(pos, token, *arrays)


def intra_kernel(q_ref, k_ref, v_ref, cum_ref, cumt_ref, token, out_ref, after, *, qh):
    after[0] = token[0]
    rows = q_ref.shape[0]
    causal = iota((rows, rows), 0) >= iota((rows, rows), 1)
    cum, cumt = cum_ref[0], cumt_ref[0]
    for i in range(qh):
        cols = slice(i * HD, (i + 1) * HD)
        scores = mm_bt(q_ref[:, cols], k_ref[:, cols])
        gap = jnp.where(causal, cum[:, i : i + 1] - cumt[i : i + 1, :], LOW)
        weights = (scores * jnp.exp(gap)).astype(BF16)
        out_ref[:, cols] = mm(weights, v_ref[:, cols]).astype(BF16)


def intra(query, key, value, cum, cumt, token):
    rows, width = query.shape
    wide = width // 4
    block = pl.BlockSpec((rows, wide), lambda i: (0, i))
    return pl.pallas_call(
        functools.partial(intra_kernel, qh=wide // HD),
        grid=(4,),
        in_specs=[
            block,
            block,
            block,
            pl.BlockSpec((1, rows, HD), lambda i: (i, 0, 0)),
            pl.BlockSpec((1, 8, rows), lambda i: (i, 0, 0)),
            SCALAR,
        ],
        out_specs=[block, SCALAR],
        out_shape=[jax.ShapeDtypeStruct((rows, width), BF16), NEXT],
        compiler_params=params(BIG),
        cost_estimate=COST,
        name="intra",
    )(query, key, value, cum, cumt, token)


def carry_kernel(pos, q_ref, inner_ref, cum_ref, keep_ref, recv_ref, token, out_ref, ss_ref, after, *, qh):
    after[0] = token[0]
    quarter = pl.program_id(0)
    part = quarter // 2
    mine = quarter % 2 == core_of(pos)
    factor = jnp.exp(cum_ref[0])
    state = jnp.where(mine, keep_ref[part], recv_ref[part])
    total = jnp.zeros((q_ref.shape[0], HD), F32)
    for i in range(qh):
        cols = slice(i * HD, (i + 1) * HD)
        carried = mm(q_ref[:, cols], state[i * HD : (i + 1) * HD, :])
        raw = inner_ref[:, cols].astype(F32) + factor[:, i : i + 1] * carried
        out_ref[:, cols] = raw.astype(BF16)
        total = total + raw * raw

    @pl.when(quarter == 0)
    def _():
        ss_ref[...] = total

    @pl.when(quarter > 0)
    def _():
        ss_ref[...] += total


def carry(pos, query, inner, cum, keep, recv, token):
    rows, width = query.shape
    wide = width // 4
    block = pl.BlockSpec((rows, wide), lambda i: (0, i))
    whole = pl.BlockSpec(keep.shape, lambda i: (0, 0, 0))
    return pl.pallas_call(
        functools.partial(carry_kernel, qh=wide // HD),
        grid=(4,),
        in_specs=[
            SCALAR,
            block,
            block,
            pl.BlockSpec((1, rows, HD), lambda i: (i, 0, 0)),
            whole,
            whole,
            SCALAR,
        ],
        out_specs=[block, pl.BlockSpec((rows, HD), lambda i: (0, 0)), SCALAR],
        out_shape=[jax.ShapeDtypeStruct((rows, width), BF16), jax.ShapeDtypeStruct((rows, HD), F32), NEXT],
        compiler_params=params(BIG),
        cost_estimate=COST,
        name="carry",
    )(pos, query, inner, cum, keep, recv, token)


def finish_kernel(raw_ref, *refs, features):
    squares, (gain_ref, gate_ref, token, out_ref, factor) = refs[:-5], refs[-5:]

    @pl.when(pl.program_id(0) == 0)
    def _():
        square = squares[0][...]
        for more in squares[1:]:
            square = square + more[...]
        mean = jnp.sum(square, axis=1, keepdims=True) / features
        factor[...] = jnp.broadcast_to(lax.rsqrt(mean + EPS), factor.shape)

    for i in range(out_ref.shape[1] // HD):
        cols = slice(i * HD, (i + 1) * HD)
        gate = 0.5 * jnp.tanh(0.5 * gate_ref[:, cols].astype(F32)) + 0.5
        raw = raw_ref[:, cols].astype(F32)
        out_ref[:, cols] = (raw * factor[...] * gain_ref[:, cols] * gate).astype(BF16)


def finish(raw, squares, gain, gate, features, token):
    rows, width = raw.shape
    wide = width // 4
    block = pl.BlockSpec((rows, wide), lambda i: (0, i))
    return pl.pallas_call(
        functools.partial(finish_kernel, features=features),
        grid=(4,),
        in_specs=[block]
        + [pl.BlockSpec((rows, HD), lambda i: (0, 0))] * len(squares)
        + [pl.BlockSpec((1, wide), lambda i: (0, i)), block, SCALAR],
        out_specs=block,
        out_shape=jax.ShapeDtypeStruct((rows, width), BF16),
        scratch_shapes=[pltpu.VMEM((rows, HD), F32)],
        compiler_params=params(BIG),
        cost_estimate=COST,
        name="finish",
    )(raw, *squares, gain.reshape(1, width), gate, token)


def soft_kernel(pos, q_ref, *refs, group, distances, planes, last, passed, kv_count, begin, form):
    pair, fold = form
    pair = min(pair, group)
    count = len(distances) * PLANE
    keys, values, refs = refs[:count], refs[count : 2 * count], refs[2 * count :]
    first = distances[0] == 0
    if not first:
        acc_in, stat_in, refs = refs[0], refs[1], refs[2:]
    token, every, refs = refs[0], refs[1:passed], refs[passed:]
    if last:
        out_ref, after, acc, stat, key_all, value_all = refs
    else:
        acc, stat, after = refs
        stat = stat.at[0]
    after[0] = token[0]
    rows = q_ref.shape[0]
    lane = iota((rows, HD), 1)
    causal = iota((rows, rows), 0) >= iota((rows, rows), 1)
    flags = [None, x_of(pos) == 1, core_of(pos) == 1, x_of(pos) == 1]

    if not first:
        acc[...] = acc_in[...]
        stat[...] = stat_in[0]

    def attend(keyed, valued, fresh):
        wide = jnp.concatenate([v[...] for v in valued], axis=0)
        wide = jnp.concatenate([wide, jnp.ones_like(wide)], axis=1)
        keyed = [k[...] for k in keyed]
        if fresh:
            own = keyed[0].astype(F32)
            shifts = [
                jnp.sum(q_ref[:, g * HD : (g + 1) * HD].astype(F32) * own, axis=1, keepdims=True)
                for g in range(group)
            ]
        else:
            shifts = [stat[:, g : g + 1] for g in range(group)]
        hidden = [0.0] + [
            jnp.where(flags[n], 0.0, LOW).astype(F32) if fresh else 0.0 for n in range(1, len(keyed))
        ]
        if fold:
            keyed = [
                jnp.concatenate(
                    [k, jnp.where(lane < 3, 1.0, jnp.where(lane == 3, h, 0.0)).astype(BF16)], axis=1
                )
                for k, h in zip(keyed, hidden)
            ]

        def scored(i):
            parts = []
            for g in range(i, i + pair):
                query = q_ref[:, g * HD : (g + 1) * HD]
                if fold:
                    high = shifts[g].astype(BF16).astype(F32)
                    middle = (shifts[g] - high).astype(BF16).astype(F32)
                    low = shifts[g] - high - middle
                    more = jnp.where(lane == 0, -high, jnp.where(lane == 1, -middle, jnp.where(lane == 2, -low, 1.0)))
                    query = jnp.concatenate([query, more.astype(BF16)], axis=1)
                parts.append(query)
            query = jnp.concatenate(parts, axis=0)
            return [mm_bt(query, k) for k in keyed]

        scores = scored(0)
        for i in range(0, group, pair):
            ahead = scored(i + pair) if i + pair < group else None
            shift = jnp.concatenate(shifts[i : i + pair], axis=0) * SCALE2
            probs = []
            for n, s in enumerate(scores):
                if fold:
                    x = s * SCALE2
                else:
                    x = s * SCALE2 - (shift - hidden[n])
                if fresh and n == 0:
                    x = jnp.concatenate(
                        [jnp.where(causal, x[m * rows : (m + 1) * rows], LOW) for m in range(pair)], axis=0
                    )
                probs.append(jnp.exp2(x).astype(BF16))
            out = mm(jnp.concatenate(probs, axis=1), wide)
            for n in range(pair):
                g = i + n
                cols = slice(g * HD, (g + 1) * HD)
                band = slice(n * rows, (n + 1) * rows)
                summed, total = out[band, :HD], out[band, HD:]
                if fresh:
                    acc[:, cols] = summed
                    old = jnp.where(lane == g, shifts[g], 0.0 if g == 0 else stat[...])
                    stat[...] = jnp.where(lane == group + g, total, old)
                else:
                    acc[:, cols] += summed
                    stat[...] += jnp.where(lane == group + g, total, 0.0)
            scores = ahead

    for n, distance in enumerate(distances):
        here = slice(n * PLANE, (n + 1) * PLANE)
        if distance == 0:
            attend(keys[here], values[here], True)
        else:
            pl.when(z_of(pos) >= distance)(functools.partial(attend, keys[here], values[here], False))
    if not last:
        return
    for g in range(group):
        cols = slice(g * HD, (g + 1) * HD)
        out_ref[:, cols] = (acc[:, cols] / stat[:, group + g : group + g + 1]).astype(BF16)

    sums = jnp.where((lane >= group) & (lane < 2 * group), stat[...], 0.0)
    fine = jnp.min(jnp.where(sums < LIMIT, 1.0, 0.0))

    @pl.when(fine < 0.5)
    def _():
        head = begin + pl.program_id(0)
        for n in range(planes * PLANE):
            here = pl.ds(n * rows, rows)
            pltpu.sync_copy(every[n].at[:, pl.ds(pl.multiple_of(head * HD, HD), HD)], key_all.at[here])
            pltpu.sync_copy(
                every[n].at[:, pl.ds(pl.multiple_of((kv_count + head) * HD, HD), HD)], value_all.at[here]
            )

        def one(g, carry):
            cols = pl.ds(pl.multiple_of(g * HD, HD), HD)
            query = q_ref[:, cols]
            top = total = summed = None
            for n in range(planes * PLANE):
                here = slice(n * rows, (n + 1) * rows)
                x = mm_bt(query, key_all[here, :]) * SCALE2
                if n == 0:
                    x = jnp.where(causal, x, LOW)
                else:
                    shown = flags[n] if n < PLANE else z_of(pos) >= n // PLANE
                    x = jnp.where(shown, x, LOW)
                high = jnp.max(x, axis=1, keepdims=True)
                if n > 0:
                    high = jnp.maximum(high, top)
                probs = jnp.exp2(x - high)
                part = mm(probs.astype(BF16), value_all[here, :])
                more = jnp.sum(probs, axis=1, keepdims=True)
                if n > 0:
                    keep = jnp.exp2(top - high)
                    part = part + keep * summed
                    more = more + keep * total
                top, total, summed = high, more, part
            out_ref[:, cols] = (summed / total).astype(BF16)
            return carry

        lax.fori_loop(0, group, one, 0)


def soft_step(pos, query, pieces, distances, state, into, span, kv_count, planes, last, token, form):
    rows, width = query.shape
    group = width // HD // kv_count
    first = distances[0] == 0
    begin, count = span
    block = pl.BlockSpec((rows, group * HD), lambda k: (0, begin + k))
    stat = pl.BlockSpec((1, rows, HD), lambda k: (begin + k, 0, 0))
    keys = pl.BlockSpec((rows, HD), lambda k: (0, begin + k))
    values = pl.BlockSpec((rows, HD), lambda k: (0, kv_count + begin + k))
    used = [a for d in distances for a in pieces[d]]
    in_specs = [SCALAR, block] + [keys] * len(used) + [values] * len(used)
    operands = [pos, query] + used + used
    aliases = {}
    if not first:
        if not last:
            aliases = {len(operands): 0, len(operands) + 1: 1}
        in_specs += [block, stat]
        operands += list(state)
    in_specs.append(SCALAR)
    operands.append(token)
    rest = [a for d in range(planes) for a in pieces[d]] if last else []
    if into is not None:
        for i, a in enumerate(into):
            aliases[len(operands) + len(rest) + i] = i
        rest = rest + list(into)
    in_specs += [ANY] * len(rest)
    operands += rest
    if last:
        out_specs = [block, SCALAR]
        out_shape = [jax.ShapeDtypeStruct((rows, width), BF16), NEXT]
        scratch = [pltpu.VMEM((rows, group * HD), F32), pltpu.VMEM((rows, HD), F32)]
        scratch += [pltpu.VMEM((planes * PLANE * rows, HD), BF16)] * 2
    else:
        out_specs = [block, stat, SCALAR]
        out_shape = [
            jax.ShapeDtypeStruct((rows, width), F32),
            jax.ShapeDtypeStruct((kv_count, rows, HD), F32),
            NEXT,
        ]
        scratch = []
    return pl.pallas_call(
        functools.partial(
            soft_kernel,
            group=group,
            distances=distances,
            planes=planes,
            last=last,
            passed=1 + len(rest),
            kv_count=kv_count,
            begin=begin,
            form=form,
        ),
        grid=(count,),
        in_specs=in_specs,
        out_specs=out_specs,
        out_shape=out_shape,
        scratch_shapes=scratch,
        input_output_aliases=aliases,
        compiler_params=params(),
        cost_estimate=COST,
        name="softmax",
    )(*operands)


def local(
    light_query,
    light_key,
    light_value,
    log_decay,
    out_gate,
    norm_gain,
    soft_query,
    soft_key,
    soft_value,
    *,
    ctx,
    tp,
):
    rows, heads = log_decay.shape
    qh = heads // 4
    length = qh * HD + TAIL
    planes = ctx // PLANE
    kv_count = soft_key.shape[1] // HD
    place = lax.axis_index("ctx")
    pos = place.astype(jnp.int32).reshape(1)

    def over_core(a):
        return lax.ppermute(a, "ctx", [(i, i ^ 1) for i in range(ctx)])

    def over_x(a):
        return lax.ppermute(a, "ctx", [(i, i ^ 2) for i in range(ctx)])

    def over_z(a, d):
        return lax.ppermute(a, "ctx", [(i, i + PLANE * d) for i in range(ctx - PLANE * d)])

    def after(a, token):
        return lax.optimization_barrier((a, token))[0]

    paired = jnp.concatenate([soft_key, soft_value], axis=1)
    crossed = over_x(paired)
    arrived = [paired, over_z(paired, 1)]

    def forward(token):
        arrived.append(over_z(after(arrived[-1], token), 1))

    pieces = [[paired, crossed, over_core(paired)]]

    half = max(kv_count // 2, 1)
    spans = [(0, half), (half, kv_count - half)] if kv_count > 1 else [(0, 1)]

    def soft(distances, state, last, token, span=None, into=None, form=(2, False)):
        *state, token = soft_step(
            pos, soft_query, pieces, distances, state, into, span or (0, kv_count), kv_count, planes, last, token, form
        )
        return state, token

    send, keep, cum, cumt, token = local_state(
        pos, light_key, light_value, after(log_decay.T, pieces[0][2])
    )
    other = over_core(send)
    quarter = (length, HD)

    def cross(d, token):
        a = after(arrived[d], token)
        pieces.append([a, over_x(a)])

    def spread_core(d, token):
        pieces[d] += [over_core(after(a, token)) for a in pieces[d]]

    inner, token = intra(light_query, light_key, light_value, cum, cumt, token)
    pieces[0].append(over_core(after(crossed, token)))
    forward(token)
    cross(1, token)
    chip_send, chip_keep, token = small(chip_kernel, pos, [keep, other], [quarter, quarter], qh, "chip", token)
    chip_other = over_x(chip_send)
    state, token = soft((0,), None, False, token, spans[0], None, FORMS[0])
    plane, token = small(plane_kernel, pos, [chip_keep, chip_other], [quarter], qh, "plane", token)
    earlier = [over_z(plane, d) for d in range(1, planes)]
    cross(2, token)
    forward(token)
    if len(spans) > 1:
        state, token = soft((0,), None, False, token, spans[1], state, FORMS[1])
    spread_core(1, token)
    spread_core(2, token)
    cross(3, token)
    for d in range(3, planes - 1):
        forward(token)
        cross(d + 1, token)
    rest = (planes - 1,)
    for middle in [(1, 2)] + [(d,) for d in range(3, planes - 1)]:
        for n, span in enumerate(spans):
            state, token = soft(middle, state, False, token, span, None, FORMS[2 + n])
            if n == 0:
                spread_core(middle[-1] + 1, token)
    enter_send, enter_keep, token = small(
        enter_kernel, pos, [chip_keep, chip_other] + earlier, [quarter, quarter], qh, "enter", token
    )
    enter_other = over_x(enter_send)
    both = (2, qh * HD, HD)
    soft_out, token = soft(rest, state, True, token, spans[0], None, FORMS[4])
    state_send, state_keep, token = small(
        core_kernel, pos, [enter_keep, enter_other, keep, other], [both, both], qh, "core", token
    )
    state_other = over_core(state_send)
    for begin, count in spans[1:]:
        soft_out, token = soft(rest, state, True, token, (begin, 1), soft_out, FORMS[5])
    raw, square, token = carry(pos, light_query, inner, cum, state_keep, state_other, token)
    for begin, count in spans[1:]:
        if count > 1:
            soft_out, token = soft(rest, state, True, token, (begin + 1, count - 1), soft_out, FORMS[5])
    squares = [square]
    step = 1
    while step < tp:
        square = sum(squares)
        squares = [square, lax.ppermute(square, "tp", [(i, i ^ step) for i in range(tp)])]
        step *= 2
    light_out = finish(raw, squares, norm_gain, out_gate, heads * HD * tp, token)
    return (light_out, soft_out[0])


def solution(mesh):
    both = P("ctx", "tp")
    return jax.shard_map(
        functools.partial(local, ctx=mesh.shape["ctx"], tp=mesh.shape["tp"]),
        mesh=mesh,
        in_specs=(both, both, both, both, both, P("tp"), both, both, both),
        out_specs=(both, both),
        check_vma=False,
    )
```

```python
import functools
import math

import jax
import jax.numpy as jnp
from jax import lax
from jax.experimental import pallas as pl
from jax.experimental.pallas import tpu as pltpu
from jax.sharding import PartitionSpec as P

HD = 128
EPS = 1e-06
LOW = -1e30
LIMIT = 2.0**100
PLANE = 4
TAIL = 16
VMEM = 32 * 2**20
BIG = 60 * 2**20
F32 = jnp.float32
BF16 = jnp.bfloat16
HIGH = lax.Precision.HIGHEST
SCALAR = pl.BlockSpec(memory_space=pltpu.SMEM)
ANY = pl.BlockSpec(memory_space=pl.ANY)
NEXT = jax.ShapeDtypeStruct((1,), jnp.int32)
FORMS = [(2, False, False), (2, False, False), (2, True, False), (2, False, True), (1, False, False), (2, False, False), (2, False, False)]
COST = pl.CostEstimate(flops=1000, bytes_accessed=2**20, transcendentals=0)
SCALE2 = HD ** (-0.5) * math.log2(math.e)


def params(limit=None):
    return pltpu.CompilerParams(vmem_limit_bytes=limit or VMEM)


def mm(a, b):
    return lax.dot_general(a, b, (((1,), (0,)), ((), ())), preferred_element_type=F32)


def mm_bt(a, b):
    return lax.dot_general(a, b, (((1,), (1,)), ((), ())), preferred_element_type=F32)


def mm_at(a, b):
    return lax.dot_general(a, b, (((0,), (0,)), ((), ())), preferred_element_type=F32)


def z_of(pos):
    return pos[0] // PLANE


def x_of(pos):
    return (pos[0] // 2) % 2


def core_of(pos):
    return pos[0] % 2


def iota(shape, dim):
    return lax.broadcasted_iota(jnp.int32, shape, dim)


def state_kernel(pos, k_ref, v_ref, ld_ref, send_ref, keep_ref, cum_ref, cumt_ref, after, fin, *, qh, heads):
    after[0] = pos[0]
    step = pl.program_id(0)
    rows = ld_ref.shape[1]

    @pl.when(step == 0)
    def _():
        upper = (iota((rows, rows), 0) <= iota((rows, rows), 1)).astype(F32).astype(BF16)
        ld = ld_ref[...]
        high = ld.astype(BF16)
        rest = ld - high.astype(F32)
        middle = rest.astype(BF16)
        low = (rest - middle.astype(F32)).astype(BF16)
        cumt = mm(high, upper) + (mm(middle, upper) + mm(low, upper))
        full = jnp.concatenate([cumt, jnp.zeros((HD - heads, rows), F32)], axis=0)
        cum = jnp.transpose(full)
        ends = jnp.broadcast_to(cumt[:, rows - 1 : rows], (heads, HD))
        fin[...] = jnp.zeros_like(fin)
        cumt_ref[...] = jnp.zeros_like(cumt_ref)
        cum_ref[...] = jnp.zeros_like(cum_ref)
        for i in range(4):
            cum_ref[i, :, 0:qh] = cum[:, i * qh : (i + 1) * qh]
            cumt_ref[i, 0:qh, :] = cumt[i * qh : (i + 1) * qh, :]
            fin[i, 0:qh, :] = ends[i * qh : (i + 1) * qh, :]

    core = pos[0] & 1
    kept = step // 2
    part = step % 2
    quarter = part * 2 + jnp.where(kept == 1, core, 1 - core)
    cum = cum_ref[quarter]
    weight = jnp.exp(cum[rows - 1 : rows, :] - cum)
    tail = fin[quarter]
    high = tail.astype(BF16).astype(F32)
    tail = jnp.concatenate([high, tail - high], axis=0).astype(BF16)
    states = []
    for i in range(qh):
        cols = slice(i * HD, (i + 1) * HD)
        keyed = (k_ref[:, cols].astype(F32) * weight[:, i : i + 1]).astype(BF16)
        states.append(mm_at(keyed, v_ref[:, cols]).astype(BF16))

    def put(ref):
        for i in range(qh):
            ref[part, i * HD : (i + 1) * HD, :] = states[i]
        ref[part, qh * HD : qh * HD + TAIL, :] = tail

    @pl.when(kept == 0)
    def _():
        put(send_ref)

    @pl.when(kept == 1)
    def _():
        put(keep_ref)


def local_state(pos, key, value, log_decay):
    heads, rows = log_decay.shape
    qh = heads // 4
    length = qh * HD + TAIL

    def columns(step, pos):
        core = pos[0] & 1
        return (0, (step % 2) * 2 + jnp.where(step // 2 == 1, core, 1 - core))

    whole = lambda *shape: pl.BlockSpec(shape, lambda step, pos: (0,) * len(shape))
    return pl.pallas_call(
        functools.partial(state_kernel, qh=qh, heads=heads),
        grid_spec=pltpu.PrefetchScalarGridSpec(
            num_scalar_prefetch=1,
            grid=(4,),
            in_specs=[
                pl.BlockSpec((rows, qh * HD), columns),
                pl.BlockSpec((rows, qh * HD), columns),
                whole(heads, rows),
            ],
            out_specs=[
                whole(2, length, HD),
                whole(2, length, HD),
                whole(4, rows, HD),
                whole(4, 8, rows),
                SCALAR,
            ],
            scratch_shapes=[pltpu.VMEM((4, 8, HD), F32)],
        ),
        out_shape=[
            jax.ShapeDtypeStruct((2, length, HD), BF16),
            jax.ShapeDtypeStruct((2, length, HD), BF16),
            jax.ShapeDtypeStruct((4, rows, HD), F32),
            jax.ShapeDtypeStruct((4, 8, rows), F32),
            NEXT,
        ],
        compiler_params=params(BIG),
        cost_estimate=COST,
        name="local_state",
    )(pos, key, value, log_decay)


def spread(item, qh):
    tail = item[qh * HD : qh * HD + TAIL, :].astype(F32)
    return item[0 : qh * HD, :].astype(F32), tail[0:8, :] + tail[8:16, :]


def pack(states, logs):
    high = logs.astype(BF16).astype(F32)
    return states.astype(BF16), jnp.concatenate([high, logs - high], axis=0).astype(BF16)


def decay(states, logs, qh):
    factor = jnp.exp(logs)
    return jnp.concatenate(
        [states[i * HD : (i + 1) * HD, :] * factor[i : i + 1, :] for i in range(qh)], axis=0
    )


def joined(early, late, qh):
    return decay(early[0], late[1], qh) + late[0], early[1] + late[1]


def store(ref, item, qh):
    states, tail = pack(*item)
    ref[0 : qh * HD, :] = states
    ref[qh * HD : qh * HD + TAIL, :] = tail


def chip_kernel(pos, keep_ref, recv_ref, send_out, keep_out, *, qh):
    first = core_of(pos) == 0
    for out, part in ((send_out, 1 - x_of(pos)), (keep_out, x_of(pos))):
        own, other = keep_ref[part], recv_ref[part]
        early = spread(jnp.where(first, own, other), qh)
        late = spread(jnp.where(first, other, own), qh)
        store(out, joined(early, late, qh), qh)


def plane_kernel(pos, keep_ref, recv_ref, out, *, qh):
    first = x_of(pos) == 0
    own, other = keep_ref[...], recv_ref[...]
    early = spread(jnp.where(first, own, other), qh)
    late = spread(jnp.where(first, other, own), qh)
    store(out, joined(early, late, qh), qh)


def enter_kernel(pos, keep_ref, recv_ref, *refs, qh):
    planes, (send_out, keep_out) = refs[:-2], refs[-2:]
    total = None
    for ref in reversed(planes):
        item = spread(ref[...], qh)
        total = item if total is None else joined(total, item, qh)
    first = x_of(pos) == 0
    early = spread(jnp.where(first, keep_ref[...], recv_ref[...]), qh)
    if total is None:
        total = (jnp.zeros_like(early[0]), jnp.zeros_like(early[1]))
    later = joined(total, early, qh)
    zero, one = pack(*total), pack(*later)
    for out, take in ((send_out, first), (keep_out, jnp.logical_not(first))):
        out[0 : qh * HD, :] = jnp.where(take, one[0], zero[0])
        out[qh * HD : qh * HD + TAIL, :] = jnp.where(take, one[1], zero[1])


def core_kernel(pos, enter_keep, enter_recv, keep_ref, recv_ref, send_out, keep_out, *, qh):
    first = core_of(pos) == 0
    for part in range(2):
        entering = spread(jnp.where(x_of(pos) == part, enter_keep[...], enter_recv[...]), qh)
        own = spread(jnp.where(first, keep_ref[part], recv_ref[part]), qh)
        later = joined(entering, own, qh)[0].astype(BF16)
        now = entering[0].astype(BF16)
        send_out[part] = jnp.where(first, later, now)
        keep_out[part] = jnp.where(first, now, later)


def with_token(kernel, pos, token, *refs):
    refs[-1][0] = token[0]
    kernel(pos, *refs[:-1])


def small(kernel, pos, arrays, outs, qh, name, token):
    return pl.pallas_call(
        functools.partial(with_token, functools.partial(kernel, qh=qh)),
        in_specs=[SCALAR, SCALAR] + [pl.BlockSpec(memory_space=pltpu.VMEM)] * len(arrays),
        out_specs=[pl.BlockSpec(memory_space=pltpu.VMEM)] * len(outs) + [SCALAR],
        out_shape=[jax.ShapeDtypeStruct(s, BF16) for s in outs] + [NEXT],
        compiler_params=pltpu.CompilerParams(vmem_limit_bytes=24 * 2**20),
        cost_estimate=COST,
        name=name,
    )(pos, token, *arrays)


def light_kernel(pos, q_ref, k_ref, v_ref, cum_ref, cumt_ref, keep_ref, recv_ref, token, out_ref, ss_ref, after, *, qh):
    after[0] = token[0]
    rows = q_ref.shape[0]
    quarter = pl.program_id(0)
    part = quarter // 2
    mine = quarter % 2 == core_of(pos)
    causal = iota((rows, rows), 0) >= iota((rows, rows), 1)
    cum, cumt = cum_ref[0], cumt_ref[0]
    factor = jnp.exp(cum)
    state = jnp.where(mine, keep_ref[part], recv_ref[part])
    total = jnp.zeros((rows, HD), F32)
    for i in range(qh):
        cols = slice(i * HD, (i + 1) * HD)
        query = q_ref[:, cols]
        scores = mm_bt(query, k_ref[:, cols])
        gap = jnp.where(causal, cum[:, i : i + 1] - cumt[i : i + 1, :], LOW)
        weights = (scores * jnp.exp(gap)).astype(BF16)
        carried = mm(query, state[i * HD : (i + 1) * HD, :])
        raw = mm(weights, v_ref[:, cols]) + factor[:, i : i + 1] * carried
        out_ref[:, cols] = raw.astype(BF16)
        total = total + raw * raw

    @pl.when(quarter == 0)
    def _():
        ss_ref[...] = total

    @pl.when(quarter > 0)
    def _():
        ss_ref[...] += total


def light(pos, query, key, value, cum, cumt, keep, recv, token):
    rows, width = query.shape
    wide = width // 4
    block = pl.BlockSpec((rows, wide), lambda i: (0, i))
    whole = pl.BlockSpec(keep.shape, lambda i: (0, 0, 0))
    return pl.pallas_call(
        functools.partial(light_kernel, qh=wide // HD),
        grid=(4,),
        in_specs=[
            SCALAR,
            block,
            block,
            block,
            pl.BlockSpec((1, rows, HD), lambda i: (i, 0, 0)),
            pl.BlockSpec((1, 8, rows), lambda i: (i, 0, 0)),
            whole,
            whole,
            SCALAR,
        ],
        out_specs=[block, pl.BlockSpec((rows, HD), lambda i: (0, 0)), SCALAR],
        out_shape=[jax.ShapeDtypeStruct((rows, width), BF16), jax.ShapeDtypeStruct((rows, HD), F32), NEXT],
        compiler_params=params(),
        cost_estimate=COST,
        name="light",
    )(pos, query, key, value, cum, cumt, keep, recv, token)


def finish_kernel(raw_ref, *refs, features):
    squares, (gain_ref, gate_ref, token, out_ref, factor) = refs[:-5], refs[-5:]

    @pl.when(pl.program_id(0) == 0)
    def _():
        square = squares[0][...]
        for more in squares[1:]:
            square = square + more[...]
        mean = jnp.sum(square, axis=1, keepdims=True) / features
        factor[...] = jnp.broadcast_to(lax.rsqrt(mean + EPS), factor.shape)

    for i in range(out_ref.shape[1] // HD):
        cols = slice(i * HD, (i + 1) * HD)
        gate = 0.5 * jnp.tanh(0.5 * gate_ref[:, cols].astype(F32)) + 0.5
        raw = raw_ref[:, cols].astype(F32)
        out_ref[:, cols] = (raw * factor[...] * gain_ref[:, cols] * gate).astype(BF16)


def finish(raw, squares, gain, gate, features, token):
    rows, width = raw.shape
    wide = width // 4
    block = pl.BlockSpec((rows, wide), lambda i: (0, i))
    return pl.pallas_call(
        functools.partial(finish_kernel, features=features),
        grid=(4,),
        in_specs=[block]
        + [pl.BlockSpec((rows, HD), lambda i: (0, 0))] * len(squares)
        + [pl.BlockSpec((1, wide), lambda i: (0, i)), block, SCALAR],
        out_specs=block,
        out_shape=jax.ShapeDtypeStruct((rows, width), BF16),
        scratch_shapes=[pltpu.VMEM((rows, HD), F32)],
        compiler_params=params(),
        cost_estimate=COST,
        name="finish",
    )(raw, *squares, gain.reshape(1, width), gate, token)


def shown(pos, rule):
    if rule == "x":
        return x_of(pos) == 1
    if rule == "core":
        return core_of(pos) == 1
    return z_of(pos) >= rule


def soft_kernel(pos, q_ref, *refs, group, rules, all_rules, last, passed, kv_count, begin, form):
    pair, fold, early = form
    pair = min(pair, group)
    count = len(rules)
    keys, values, refs = refs[:count], refs[count : 2 * count], refs[2 * count :]
    first = rules[0] == "own"
    if not first:
        acc_in, stat_in, refs = refs[0], refs[1], refs[2:]
    token, every, refs = refs[0], refs[1:passed], refs[passed:]
    if last:
        out_ref, after, acc, stat, key_all, value_all = refs
    else:
        acc, stat, after = refs
        stat = stat.at[0]
    after[0] = token[0]
    rows = q_ref.shape[0]
    lane = iota((rows, HD), 1)
    causal = iota((rows, rows), 0) >= iota((rows, rows), 1)

    if not first:
        acc[...] = acc_in[...]
        stat[...] = stat_in[0]

    def attend(keyed, valued, fresh, hidden):
        wide = jnp.concatenate([v[...] for v in valued], axis=0)
        wide = jnp.concatenate([wide, jnp.ones_like(wide)], axis=1)
        keyed = [k[...] for k in keyed]
        if fresh:
            own = keyed[0].astype(F32)
            shifts = [
                jnp.sum(q_ref[:, g * HD : (g + 1) * HD].astype(F32) * own, axis=1, keepdims=True)
                for g in range(group)
            ]
        else:
            shifts = [stat[:, g : g + 1] for g in range(group)]
        if fold:
            keyed = [
                jnp.concatenate(
                    [k, jnp.where(lane < 3, 1.0, jnp.where(lane == 3, h, 0.0)).astype(BF16)], axis=1
                )
                for k, h in zip(keyed, hidden)
            ]

        def scored(i):
            parts = []
            for g in range(i, i + pair):
                query = q_ref[:, g * HD : (g + 1) * HD]
                if fold:
                    high = shifts[g].astype(BF16).astype(F32)
                    middle = (shifts[g] - high).astype(BF16).astype(F32)
                    low = shifts[g] - high - middle
                    more = jnp.where(lane == 0, -high, jnp.where(lane == 1, -middle, jnp.where(lane == 2, -low, 1.0)))
                    query = jnp.concatenate([query, more.astype(BF16)], axis=1)
                parts.append(query)
            query = jnp.concatenate(parts, axis=0)
            return [mm_bt(query, k) for k in keyed]

        ahead = scored(0)
        for i in range(0, group, pair):
            scores = ahead if early or i == 0 else scored(i)
            if early and i + pair < group:
                ahead = scored(i + pair)
            shift = jnp.concatenate(shifts[i : i + pair], axis=0) * SCALE2
            probs = []
            for n, s in enumerate(scores):
                if fold:
                    x = s * SCALE2
                else:
                    x = s * SCALE2 - (shift - hidden[n])
                if fresh and n == 0:
                    x = jnp.concatenate(
                        [jnp.where(causal, x[m * rows : (m + 1) * rows], LOW) for m in range(pair)], axis=0
                    )
                probs.append(jnp.exp2(x).astype(BF16))
            out = mm(jnp.concatenate(probs, axis=1), wide)
            for n in range(pair):
                g = i + n
                cols = slice(g * HD, (g + 1) * HD)
                band = slice(n * rows, (n + 1) * rows)
                summed, total = out[band, :HD], out[band, HD:]
                if fresh:
                    acc[:, cols] = summed
                    old = jnp.where(lane == g, shifts[g], 0.0 if g == 0 else stat[...])
                    stat[...] = jnp.where(lane == group + g, total, old)
                else:
                    acc[:, cols] += summed
                    stat[...] += jnp.where(lane == group + g, total, 0.0)

    if first:
        attend(keys, values, True, [0.0] + [jnp.where(shown(pos, r), 0.0, LOW).astype(F32) for r in rules[1:]])
    elif len(set(rules)) == 1:
        pl.when(shown(pos, rules[0]))(lambda: attend(keys, values, False, [0.0] * count))
    else:
        some = functools.reduce(jnp.logical_or, [shown(pos, r) for r in rules])
        hidden = [jnp.where(shown(pos, r), 0.0, LOW).astype(F32) for r in rules]
        pl.when(some)(lambda: attend(keys, values, False, hidden))
    if not last:
        return
    for g in range(group):
        cols = slice(g * HD, (g + 1) * HD)
        out_ref[:, cols] = (acc[:, cols] / stat[:, group + g : group + g + 1]).astype(BF16)

    sums = jnp.where((lane >= group) & (lane < 2 * group), stat[...], 0.0)
    fine = jnp.min(jnp.where(sums < LIMIT, 1.0, 0.0))

    @pl.when(fine < 0.5)
    def _():
        head = begin + pl.program_id(0)
        for n in range(len(all_rules)):
            here = pl.ds(n * rows, rows)
            pltpu.sync_copy(every[n].at[:, pl.ds(pl.multiple_of(head * HD, HD), HD)], key_all.at[here])
            pltpu.sync_copy(
                every[n].at[:, pl.ds(pl.multiple_of((kv_count + head) * HD, HD), HD)], value_all.at[here]
            )

        def one(g, carry):
            cols = pl.ds(pl.multiple_of(g * HD, HD), HD)
            query = q_ref[:, cols]
            top = total = summed = None
            for n, rule in enumerate(all_rules):
                here = slice(n * rows, (n + 1) * rows)
                x = mm_bt(query, key_all[here, :]) * SCALE2
                if n == 0:
                    x = jnp.where(causal, x, LOW)
                else:
                    x = jnp.where(shown(pos, rule), x, LOW)
                high = jnp.max(x, axis=1, keepdims=True)
                if n > 0:
                    high = jnp.maximum(high, top)
                probs = jnp.exp2(x - high)
                part = mm(probs.astype(BF16), value_all[here, :])
                more = jnp.sum(probs, axis=1, keepdims=True)
                if n > 0:
                    keep = jnp.exp2(top - high)
                    part = part + keep * summed
                    more = more + keep * total
                top, total, summed = high, more, part
            out_ref[:, cols] = (summed / total).astype(BF16)
            return carry

        lax.fori_loop(0, group, one, 0)


def soft_step(pos, query, blocks, every, state, into, span, kv_count, last, token, form):
    rows, width = query.shape
    group = width // HD // kv_count
    used, rules = zip(*blocks)
    used = list(used)
    first = rules[0] == "own"
    begin, count = span
    block = pl.BlockSpec((rows, group * HD), lambda k: (0, begin + k))
    stat = pl.BlockSpec((1, rows, HD), lambda k: (begin + k, 0, 0))
    keys = pl.BlockSpec((rows, HD), lambda k: (0, begin + k))
    values = pl.BlockSpec((rows, HD), lambda k: (0, kv_count + begin + k))
    in_specs = [SCALAR, block] + [keys] * len(used) + [values] * len(used)
    operands = [pos, query] + used + used
    aliases = {}
    if not first:
        if not last:
            aliases = {len(operands): 0, len(operands) + 1: 1}
        in_specs += [block, stat]
        operands += list(state)
    in_specs.append(SCALAR)
    operands.append(token)
    rest = [a for a, _ in every] if last else []
    if into is not None:
        for i, a in enumerate(into):
            aliases[len(operands) + len(rest) + i] = i
        rest = rest + list(into)
    in_specs += [ANY] * len(rest)
    operands += rest
    if last:
        out_specs = [block, SCALAR]
        out_shape = [jax.ShapeDtypeStruct((rows, width), BF16), NEXT]
        scratch = [pltpu.VMEM((rows, group * HD), F32), pltpu.VMEM((rows, HD), F32)]
        scratch += [pltpu.VMEM((len(every) * rows, HD), BF16)] * 2
    else:
        out_specs = [block, stat, SCALAR]
        out_shape = [
            jax.ShapeDtypeStruct((rows, width), F32),
            jax.ShapeDtypeStruct((kv_count, rows, HD), F32),
            NEXT,
        ]
        scratch = []
    return pl.pallas_call(
        functools.partial(
            soft_kernel,
            group=group,
            rules=rules,
            all_rules=[rule for _, rule in every],
            last=last,
            passed=1 + len(rest),
            kv_count=kv_count,
            begin=begin,
            form=form,
        ),
        grid=(count,),
        in_specs=in_specs,
        out_specs=out_specs,
        out_shape=out_shape,
        scratch_shapes=scratch,
        input_output_aliases=aliases,
        compiler_params=params(),
        cost_estimate=COST,
        name="softmax",
    )(*operands)


def local(
    light_query,
    light_key,
    light_value,
    log_decay,
    out_gate,
    norm_gain,
    soft_query,
    soft_key,
    soft_value,
    *,
    ctx,
    tp,
):
    rows, heads = log_decay.shape
    qh = heads // 4
    length = qh * HD + TAIL
    planes = ctx // PLANE
    kv_count = soft_key.shape[1] // HD
    place = lax.axis_index("ctx")
    pos = place.astype(jnp.int32).reshape(1)

    def over_core(a):
        return lax.ppermute(a, "ctx", [(i, i ^ 1) for i in range(ctx)])

    def over_x(a):
        return lax.ppermute(a, "ctx", [(i, i ^ 2) for i in range(ctx)])

    def over_z(a, d):
        return lax.ppermute(a, "ctx", [(i, i + PLANE * d) for i in range(ctx - PLANE * d)])

    def after(a, token):
        return lax.optimization_barrier((a, token))[0]

    half = max(kv_count // 2, 1)
    spans = [(0, half), (half, kv_count - half)] if kv_count > 1 else [(0, 1)]
    every = []

    def soft(blocks, state, token, form, span=None, last=False, into=None):
        if not any(a is blocks[0][0] for a, _ in every):
            every.extend(blocks)
        *state, token = soft_step(
            pos, soft_query, blocks, every, state, into, span or (0, kv_count), kv_count, last, token, form
        )
        return state, token

    def pair(a, rule, token):
        return [(a, rule), (over_core(after(a, token)), rule)]

    paired = jnp.concatenate([soft_key, soft_value], axis=1)
    own = [(paired, "own"), (over_core(paired), "core")]
    beside = over_x(paired)
    same = over_z(paired, 1)

    send, keep, cum, cumt, token = local_state(
        pos, light_key, light_value, after(log_decay.T, own[1][0])
    )
    other = over_core(send)
    quarter = (length, HD)
    both = (2, qh * HD, HD)

    state, token = soft(own, None, token, FORMS[0])
    blocks = pair(beside, "x", token) + pair(same, 1, token)
    ahead = over_z(after(same, token), 1)
    beside = over_x(after(same, token))
    state, token = soft(blocks, state, token, FORMS[1], spans[0])
    chip_send, chip_keep, token = small(chip_kernel, pos, [keep, other], [quarter, quarter], qh, "chip", token)
    chip_other = over_x(chip_send)
    if len(spans) > 1:
        state, token = soft(blocks, state, token, FORMS[1], spans[1])
    plane, token = small(plane_kernel, pos, [chip_keep, chip_other], [quarter], qh, "plane", token)
    earlier = [over_z(plane, d) for d in range(1, planes)]
    for d in range(1, planes - 1):
        same = ahead
        blocks = pair(beside, d, token) + pair(same, d + 1, token)
        if d < planes - 2:
            beside = over_x(after(same, token))
            ahead = over_z(after(same, token), 1)
            for span in spans:
                state, token = soft(blocks, state, token, FORMS[2], span)
    enter_send, enter_keep, token = small(
        enter_kernel, pos, [chip_keep, chip_other] + earlier, [quarter, quarter], qh, "enter", token
    )
    enter_other = over_x(enter_send)
    state, token = soft(blocks, state, token, FORMS[3], spans[0])
    beside = over_x(after(same, token))
    state_send, state_keep, token = small(
        core_kernel, pos, [enter_keep, enter_other, keep, other], [both, both], qh, "core", token
    )
    state_other = over_core(state_send)
    if len(spans) > 1:
        state, token = soft(blocks, state, token, FORMS[4], spans[1])
    blocks = pair(beside, planes - 1, token)
    raw, square, token = light(
        pos, light_query, light_key, light_value, cum, cumt, state_keep, state_other, token
    )
    soft_out, token = soft(blocks, state, token, FORMS[5], None, True)
    squares = [square]
    step = 1
    while step < tp:
        square = sum(squares)
        squares = [square, lax.ppermute(square, "tp", [(i, i ^ step) for i in range(tp)])]
        step *= 2
    light_out = finish(raw, squares, norm_gain, out_gate, heads * HD * tp, token)
    return (light_out, soft_out[0])


def solution(mesh):
    both = P("ctx", "tp")
    return jax.shard_map(
        functools.partial(local, ctx=mesh.shape["ctx"], tp=mesh.shape["tp"]),
        mesh=mesh,
        in_specs=(both, both, both, both, both, P("tp"), both, both, both),
        out_specs=(both, both),
        check_vma=False,
    )
```

```python
import functools
import math

import jax
import jax.numpy as jnp
from jax import lax
from jax.experimental import pallas as pl
from jax.experimental.pallas import tpu as pltpu
from jax.sharding import PartitionSpec as P

HD = 128
EPS = 1e-06
LOW = -1e30
LIMIT = 2.0**100
PLANE = 4
TAIL = 16
VMEM = 32 * 2**20
BIG = 60 * 2**20
F32 = jnp.float32
BF16 = jnp.bfloat16
HIGH = lax.Precision.HIGHEST
SCALAR = pl.BlockSpec(memory_space=pltpu.SMEM)
ANY = pl.BlockSpec(memory_space=pl.ANY)
NEXT = jax.ShapeDtypeStruct((1,), jnp.int32)
FORMS = [(2, False, False), (2, False, True), (2, True, False), (4, True, True), (2, False, False), (2, False, True), (2, False, False), (2, False, True)] * 4
COST = pl.CostEstimate(flops=1000, bytes_accessed=2**20, transcendentals=0)
SCALE2 = HD ** (-0.5) * math.log2(math.e)


def params(limit=None):
    return pltpu.CompilerParams(vmem_limit_bytes=limit or VMEM)


def mm(a, b):
    return lax.dot_general(a, b, (((1,), (0,)), ((), ())), preferred_element_type=F32)


def mm_bt(a, b):
    return lax.dot_general(a, b, (((1,), (1,)), ((), ())), preferred_element_type=F32)


def mm_at(a, b):
    return lax.dot_general(a, b, (((0,), (0,)), ((), ())), preferred_element_type=F32)


def z_of(pos):
    return pos[0] // PLANE


def x_of(pos):
    return (pos[0] // 2) % 2


def core_of(pos):
    return pos[0] % 2


def iota(shape, dim):
    return lax.broadcasted_iota(jnp.int32, shape, dim)


def state_kernel(pos, k_ref, v_ref, ld_ref, send_ref, keep_ref, cum_ref, cumt_ref, after, fin, *, qh, heads):
    after[0] = pos[0]
    step = pl.program_id(0)
    rows = ld_ref.shape[1]

    @pl.when(step == 0)
    def _():
        upper = (iota((rows, rows), 0) <= iota((rows, rows), 1)).astype(F32).astype(BF16)
        ld = ld_ref[...]
        high = ld.astype(BF16)
        rest = ld - high.astype(F32)
        middle = rest.astype(BF16)
        low = (rest - middle.astype(F32)).astype(BF16)
        cumt = mm(high, upper) + (mm(middle, upper) + mm(low, upper))
        full = jnp.concatenate([cumt, jnp.zeros((HD - heads, rows), F32)], axis=0)
        cum = jnp.transpose(full)
        ends = jnp.broadcast_to(cumt[:, rows - 1 : rows], (heads, HD))
        fin[...] = jnp.zeros_like(fin)
        cumt_ref[...] = jnp.zeros_like(cumt_ref)
        cum_ref[...] = jnp.zeros_like(cum_ref)
        for i in range(4):
            cum_ref[i, :, 0:qh] = cum[:, i * qh : (i + 1) * qh]
            cumt_ref[i, 0:qh, :] = cumt[i * qh : (i + 1) * qh, :]
            fin[i, 0:qh, :] = ends[i * qh : (i + 1) * qh, :]

    core = pos[0] & 1
    kept = step // 2
    part = step % 2
    quarter = part * 2 + jnp.where(kept == 1, core, 1 - core)
    cum = cum_ref[quarter]
    weight = jnp.exp(cum[rows - 1 : rows, :] - cum)
    tail = fin[quarter]
    high = tail.astype(BF16).astype(F32)
    tail = jnp.concatenate([high, tail - high], axis=0).astype(BF16)
    states = []
    for i in range(qh):
        cols = slice(i * HD, (i + 1) * HD)
        keyed = (k_ref[:, cols].astype(F32) * weight[:, i : i + 1]).astype(BF16)
        states.append(mm_at(keyed, v_ref[:, cols]).astype(BF16))

    def put(ref):
        for i in range(qh):
            ref[part, i * HD : (i + 1) * HD, :] = states[i]
        ref[part, qh * HD : qh * HD + TAIL, :] = tail

    @pl.when(kept == 0)
    def _():
        put(send_ref)

    @pl.when(kept == 1)
    def _():
        put(keep_ref)


def local_state(pos, key, value, log_decay):
    heads, rows = log_decay.shape
    qh = heads // 4
    length = qh * HD + TAIL

    def columns(step, pos):
        core = pos[0] & 1
        return (0, (step % 2) * 2 + jnp.where(step // 2 == 1, core, 1 - core))

    whole = lambda *shape: pl.BlockSpec(shape, lambda step, pos: (0,) * len(shape))
    return pl.pallas_call(
        functools.partial(state_kernel, qh=qh, heads=heads),
        grid_spec=pltpu.PrefetchScalarGridSpec(
            num_scalar_prefetch=1,
            grid=(4,),
            in_specs=[
                pl.BlockSpec((rows, qh * HD), columns),
                pl.BlockSpec((rows, qh * HD), columns),
                whole(heads, rows),
            ],
            out_specs=[
                whole(2, length, HD),
                whole(2, length, HD),
                whole(4, rows, HD),
                whole(4, 8, rows),
                SCALAR,
            ],
            scratch_shapes=[pltpu.VMEM((4, 8, HD), F32)],
        ),
        out_shape=[
            jax.ShapeDtypeStruct((2, length, HD), BF16),
            jax.ShapeDtypeStruct((2, length, HD), BF16),
            jax.ShapeDtypeStruct((4, rows, HD), F32),
            jax.ShapeDtypeStruct((4, 8, rows), F32),
            NEXT,
        ],
        compiler_params=params(BIG),
        cost_estimate=COST,
        name="local_state",
    )(pos, key, value, log_decay)


def spread(item, qh):
    tail = item[qh * HD : qh * HD + TAIL, :].astype(F32)
    return item[0 : qh * HD, :].astype(F32), tail[0:8, :] + tail[8:16, :]


def pack(states, logs):
    high = logs.astype(BF16).astype(F32)
    return states.astype(BF16), jnp.concatenate([high, logs - high], axis=0).astype(BF16)


def decay(states, logs, qh):
    factor = jnp.exp(logs)
    return jnp.concatenate(
        [states[i * HD : (i + 1) * HD, :] * factor[i : i + 1, :] for i in range(qh)], axis=0
    )


def joined(early, late, qh):
    return decay(early[0], late[1], qh) + late[0], early[1] + late[1]


def store(ref, item, qh):
    states, tail = pack(*item)
    ref[0 : qh * HD, :] = states
    ref[qh * HD : qh * HD + TAIL, :] = tail


def chip_kernel(pos, keep_ref, recv_ref, send_out, keep_out, *, qh):
    first = core_of(pos) == 0
    for out, part in ((send_out, 1 - x_of(pos)), (keep_out, x_of(pos))):
        own, other = keep_ref[part], recv_ref[part]
        early = spread(jnp.where(first, own, other), qh)
        late = spread(jnp.where(first, other, own), qh)
        store(out, joined(early, late, qh), qh)


def plane_kernel(pos, keep_ref, recv_ref, out, *, qh):
    first = x_of(pos) == 0
    own, other = keep_ref[...], recv_ref[...]
    early = spread(jnp.where(first, own, other), qh)
    late = spread(jnp.where(first, other, own), qh)
    store(out, joined(early, late, qh), qh)


def step_kernel(pos, early_ref, late_ref, out, *, qh):
    store(out, joined(spread(early_ref[...], qh), spread(late_ref[...], qh), qh), qh)


def enter_kernel(pos, keep_ref, recv_ref, total_ref, send_out, keep_out, *, qh):
    first = x_of(pos) == 0
    early = spread(jnp.where(first, keep_ref[...], recv_ref[...]), qh)
    total = spread(total_ref[...], qh)
    zero, one = pack(*total), pack(*joined(total, early, qh))
    for out, take in ((send_out, first), (keep_out, jnp.logical_not(first))):
        out[0 : qh * HD, :] = jnp.where(take, one[0], zero[0])
        out[qh * HD : qh * HD + TAIL, :] = jnp.where(take, one[1], zero[1])


def core_kernel(pos, enter_keep, enter_recv, keep_ref, recv_ref, send_out, keep_out, *, qh):
    first = core_of(pos) == 0
    for part in range(2):
        entering = spread(jnp.where(x_of(pos) == part, enter_keep[...], enter_recv[...]), qh)
        own = spread(jnp.where(first, keep_ref[part], recv_ref[part]), qh)
        later = joined(entering, own, qh)[0].astype(BF16)
        now = entering[0].astype(BF16)
        send_out[part] = jnp.where(first, later, now)
        keep_out[part] = jnp.where(first, now, later)


def with_token(kernel, pos, token, *refs):
    refs[-1][0] = token[0]
    kernel(pos, *refs[:-1])


def small(kernel, pos, arrays, outs, qh, name, token):
    return pl.pallas_call(
        functools.partial(with_token, functools.partial(kernel, qh=qh)),
        in_specs=[SCALAR, SCALAR] + [pl.BlockSpec(memory_space=pltpu.VMEM)] * len(arrays),
        out_specs=[pl.BlockSpec(memory_space=pltpu.VMEM)] * len(outs) + [SCALAR],
        out_shape=[jax.ShapeDtypeStruct(s, BF16) for s in outs] + [NEXT],
        compiler_params=pltpu.CompilerParams(vmem_limit_bytes=24 * 2**20),
        cost_estimate=COST,
        name=name,
    )(pos, token, *arrays)


def light_kernel(pos, q_ref, k_ref, v_ref, cum_ref, cumt_ref, keep_ref, recv_ref, token, out_ref, ss_ref, after, *, qh):
    after[0] = token[0]
    rows = q_ref.shape[0]
    quarter = pl.program_id(0)
    part = quarter // 2
    mine = quarter % 2 == core_of(pos)
    causal = iota((rows, rows), 0) >= iota((rows, rows), 1)
    cum, cumt = cum_ref[0], cumt_ref[0]
    factor = jnp.exp(cum)
    state = jnp.where(mine, keep_ref[part], recv_ref[part])
    total = jnp.zeros((rows, HD), F32)
    for i in range(qh):
        cols = slice(i * HD, (i + 1) * HD)
        query = q_ref[:, cols]
        scores = mm_bt(query, k_ref[:, cols])
        gap = jnp.where(causal, cum[:, i : i + 1] - cumt[i : i + 1, :], LOW)
        weights = (scores * jnp.exp(gap)).astype(BF16)
        carried = mm(query, state[i * HD : (i + 1) * HD, :])
        raw = mm(weights, v_ref[:, cols]) + factor[:, i : i + 1] * carried
        out_ref[:, cols] = raw.astype(BF16)
        total = total + raw * raw

    @pl.when(quarter == 0)
    def _():
        ss_ref[...] = total

    @pl.when(quarter > 0)
    def _():
        ss_ref[...] += total


def light(pos, query, key, value, cum, cumt, keep, recv, token):
    rows, width = query.shape
    wide = width // 4
    block = pl.BlockSpec((rows, wide), lambda i: (0, i))
    whole = pl.BlockSpec(keep.shape, lambda i: (0, 0, 0))
    return pl.pallas_call(
        functools.partial(light_kernel, qh=wide // HD),
        grid=(4,),
        in_specs=[
            SCALAR,
            block,
            block,
            block,
            pl.BlockSpec((1, rows, HD), lambda i: (i, 0, 0)),
            pl.BlockSpec((1, 8, rows), lambda i: (i, 0, 0)),
            whole,
            whole,
            SCALAR,
        ],
        out_specs=[block, pl.BlockSpec((rows, HD), lambda i: (0, 0)), SCALAR],
        out_shape=[jax.ShapeDtypeStruct((rows, width), BF16), jax.ShapeDtypeStruct((rows, HD), F32), NEXT],
        compiler_params=params(),
        cost_estimate=COST,
        name="light",
    )(pos, query, key, value, cum, cumt, keep, recv, token)


def finish_kernel(raw_ref, *refs, features):
    squares, (gain_ref, gate_ref, token, out_ref, factor) = refs[:-5], refs[-5:]

    @pl.when(pl.program_id(0) == 0)
    def _():
        square = squares[0][...]
        for more in squares[1:]:
            square = square + more[...]
        mean = jnp.sum(square, axis=1, keepdims=True) / features
        factor[...] = jnp.broadcast_to(lax.rsqrt(mean + EPS), factor.shape)

    for i in range(out_ref.shape[1] // HD):
        cols = slice(i * HD, (i + 1) * HD)
        gate = 0.5 * jnp.tanh(0.5 * gate_ref[:, cols].astype(F32)) + 0.5
        raw = raw_ref[:, cols].astype(F32)
        out_ref[:, cols] = (raw * factor[...] * gain_ref[:, cols] * gate).astype(BF16)


def finish(raw, squares, gain, gate, features, token):
    rows, width = raw.shape
    wide = width // 4
    block = pl.BlockSpec((rows, wide), lambda i: (0, i))
    return pl.pallas_call(
        functools.partial(finish_kernel, features=features),
        grid=(4,),
        in_specs=[block]
        + [pl.BlockSpec((rows, HD), lambda i: (0, 0))] * len(squares)
        + [pl.BlockSpec((1, wide), lambda i: (0, i)), block, SCALAR],
        out_specs=block,
        out_shape=jax.ShapeDtypeStruct((rows, width), BF16),
        scratch_shapes=[pltpu.VMEM((rows, HD), F32)],
        compiler_params=params(),
        cost_estimate=COST,
        name="finish",
    )(raw, *squares, gain.reshape(1, width), gate, token)


def shown(pos, rule):
    if rule == "x":
        return x_of(pos) == 1
    if rule == "core":
        return core_of(pos) == 1
    return z_of(pos) >= rule


def soft_kernel(pos, q_ref, *refs, group, rules, all_rules, last, passed, kv_count, begin, form):
    pair, fold, ones = form
    pair = min(pair, group)
    count = len(rules)
    keys, values, refs = refs[:count], refs[count : 2 * count], refs[2 * count :]
    first = rules[0] == "own"
    if not first:
        acc_in, stat_in, refs = refs[0], refs[1], refs[2:]
    token, every, refs = refs[0], refs[1:passed], refs[passed:]
    if last:
        out_ref, after, acc, stat, key_all, value_all = refs
    else:
        acc, stat, after = refs
        stat = stat.at[0]
    after[0] = token[0]
    rows = q_ref.shape[0]
    lane = iota((rows, HD), 1)
    causal = iota((rows, rows), 0) >= iota((rows, rows), 1)

    if not first:
        acc[...] = acc_in[...]
        stat[...] = stat_in[0]

    def attend(keyed, valued, fresh, hidden):
        wide = jnp.concatenate([v[...] for v in valued], axis=0)
        if ones:
            wide = jnp.concatenate([wide, jnp.ones_like(wide)], axis=1)
        keyed = [k[...] for k in keyed]
        if fresh:
            own = keyed[0].astype(F32)
            shifts = [
                jnp.sum(q_ref[:, g * HD : (g + 1) * HD].astype(F32) * own, axis=1, keepdims=True)
                for g in range(group)
            ]
        else:
            shifts = [stat[:, g : g + 1] for g in range(group)]
        if fold:
            keyed = [
                jnp.concatenate(
                    [k, jnp.where(lane < 3, 1.0, jnp.where(lane == 3, h, 0.0)).astype(BF16)], axis=1
                )
                for k, h in zip(keyed, hidden)
            ]

        def scored(i):
            parts = []
            for g in range(i, i + pair):
                query = q_ref[:, g * HD : (g + 1) * HD]
                if fold:
                    high = shifts[g].astype(BF16).astype(F32)
                    middle = (shifts[g] - high).astype(BF16).astype(F32)
                    low = shifts[g] - high - middle
                    more = jnp.where(lane == 0, -high, jnp.where(lane == 1, -middle, jnp.where(lane == 2, -low, 1.0)))
                    query = jnp.concatenate([query, more.astype(BF16)], axis=1)
                parts.append(query)
            query = jnp.concatenate(parts, axis=0)
            return [mm_bt(query, k) for k in keyed]

        for i in range(0, group, pair):
            scores = scored(i)
            shift = jnp.concatenate(shifts[i : i + pair], axis=0) * SCALE2
            probs, mass = [], None
            for n, s in enumerate(scores):
                if fold:
                    x = s * SCALE2
                else:
                    x = s * SCALE2 - (shift - hidden[n])
                if fresh and n == 0:
                    x = jnp.concatenate(
                        [jnp.where(causal, x[m * rows : (m + 1) * rows], LOW) for m in range(pair)], axis=0
                    )
                prob = jnp.exp2(x)
                probs.append(prob.astype(BF16))
                if not ones:
                    mass = prob if mass is None else mass + prob
            out = mm(jnp.concatenate(probs, axis=1), wide)
            if not ones:
                mass = jnp.sum(mass, axis=1, keepdims=True)
            for n in range(pair):
                g = i + n
                cols = slice(g * HD, (g + 1) * HD)
                band = slice(n * rows, (n + 1) * rows)
                summed, total = out[band, :HD], out[band, HD:] if ones else mass[band]
                if fresh:
                    acc[:, cols] = summed
                    old = jnp.where(lane == g, shifts[g], 0.0 if g == 0 else stat[...])
                    stat[...] = jnp.where(lane == group + g, total, old)
                else:
                    acc[:, cols] += summed
                    stat[...] += jnp.where(lane == group + g, total, 0.0)

    if first:
        attend(keys, values, True, [0.0] + [jnp.where(shown(pos, r), 0.0, LOW).astype(F32) for r in rules[1:]])
    elif len(set(rules)) == 1:
        pl.when(shown(pos, rules[0]))(lambda: attend(keys, values, False, [0.0] * count))
    else:
        some = functools.reduce(jnp.logical_or, [shown(pos, r) for r in rules])
        hidden = [jnp.where(shown(pos, r), 0.0, LOW).astype(F32) for r in rules]
        pl.when(some)(lambda: attend(keys, values, False, hidden))
    if not last:
        return
    inverse = 1.0 / jnp.where((lane >= group) & (lane < 2 * group), stat[...], 1.0)
    for g in range(group):
        cols = slice(g * HD, (g + 1) * HD)
        out_ref[:, cols] = (acc[:, cols] * inverse[:, group + g : group + g + 1]).astype(BF16)

    sums = jnp.where((lane >= group) & (lane < 2 * group), stat[...], 0.0)
    fine = jnp.min(jnp.where(sums < LIMIT, 1.0, 0.0))

    @pl.when(fine < 0.5)
    def _():
        head = begin + pl.program_id(0)
        for n in range(len(all_rules)):
            here = pl.ds(n * rows, rows)
            pltpu.sync_copy(every[n].at[:, pl.ds(pl.multiple_of(head * HD, HD), HD)], key_all.at[here])
            pltpu.sync_copy(
                every[n].at[:, pl.ds(pl.multiple_of((kv_count + head) * HD, HD), HD)], value_all.at[here]
            )

        def one(g, carry):
            cols = pl.ds(pl.multiple_of(g * HD, HD), HD)
            query = q_ref[:, cols]
            top = total = summed = None
            for n, rule in enumerate(all_rules):
                here = slice(n * rows, (n + 1) * rows)
                x = mm_bt(query, key_all[here, :]) * SCALE2
                if n == 0:
                    x = jnp.where(causal, x, LOW)
                else:
                    x = jnp.where(shown(pos, rule), x, LOW)
                high = jnp.max(x, axis=1, keepdims=True)
                if n > 0:
                    high = jnp.maximum(high, top)
                probs = jnp.exp2(x - high)
                part = mm(probs.astype(BF16), value_all[here, :])
                more = jnp.sum(probs, axis=1, keepdims=True)
                if n > 0:
                    keep = jnp.exp2(top - high)
                    part = part + keep * summed
                    more = more + keep * total
                top, total, summed = high, more, part
            out_ref[:, cols] = (summed / total).astype(BF16)
            return carry

        lax.fori_loop(0, group, one, 0)


def soft_step(pos, query, blocks, every, state, into, span, kv_count, last, token, form):
    rows, width = query.shape
    group = width // HD // kv_count
    used, rules = zip(*blocks)
    used = list(used)
    first = rules[0] == "own"
    begin, count = span
    block = pl.BlockSpec((rows, group * HD), lambda k: (0, begin + k))
    stat = pl.BlockSpec((1, rows, HD), lambda k: (begin + k, 0, 0))
    keys = pl.BlockSpec((rows, HD), lambda k: (0, begin + k))
    values = pl.BlockSpec((rows, HD), lambda k: (0, kv_count + begin + k))
    in_specs = [SCALAR, block] + [keys] * len(used) + [values] * len(used)
    operands = [pos, query] + used + used
    aliases = {}
    if not first:
        if not last:
            aliases = {len(operands): 0, len(operands) + 1: 1}
        in_specs += [block, stat]
        operands += list(state)
    in_specs.append(SCALAR)
    operands.append(token)
    rest = [a for a, _ in every] if last else []
    if into is not None:
        for i, a in enumerate(into):
            aliases[len(operands) + len(rest) + i] = i
        rest = rest + list(into)
    in_specs += [ANY] * len(rest)
    operands += rest
    if last:
        out_specs = [block, SCALAR]
        out_shape = [jax.ShapeDtypeStruct((rows, width), BF16), NEXT]
        scratch = [pltpu.VMEM((rows, group * HD), F32), pltpu.VMEM((rows, HD), F32)]
        scratch += [pltpu.VMEM((len(every) * rows, HD), BF16)] * 2
    else:
        out_specs = [block, stat, SCALAR]
        out_shape = [
            jax.ShapeDtypeStruct((rows, width), F32),
            jax.ShapeDtypeStruct((kv_count, rows, HD), F32),
            NEXT,
        ]
        scratch = []
    return pl.pallas_call(
        functools.partial(
            soft_kernel,
            group=group,
            rules=rules,
            all_rules=[rule for _, rule in every],
            last=last,
            passed=1 + len(rest),
            kv_count=kv_count,
            begin=begin,
            form=form,
        ),
        grid=(count,),
        in_specs=in_specs,
        out_specs=out_specs,
        out_shape=out_shape,
        scratch_shapes=scratch,
        input_output_aliases=aliases,
        compiler_params=params(),
        cost_estimate=COST,
        name="softmax",
    )(*operands)


def local(
    light_query,
    light_key,
    light_value,
    log_decay,
    out_gate,
    norm_gain,
    soft_query,
    soft_key,
    soft_value,
    *,
    ctx,
    tp,
):
    rows, heads = log_decay.shape
    qh = heads // 4
    length = qh * HD + TAIL
    planes = ctx // PLANE
    kv_count = soft_key.shape[1] // HD
    place = lax.axis_index("ctx")
    pos = place.astype(jnp.int32).reshape(1)

    def over_core(a):
        return lax.ppermute(a, "ctx", [(i, i ^ 1) for i in range(ctx)])

    def over_x(a):
        return lax.ppermute(a, "ctx", [(i, i ^ 2) for i in range(ctx)])

    def over_z(a, d):
        return lax.ppermute(a, "ctx", [(i, i + PLANE * d) for i in range(ctx - PLANE * d)])

    def after(a, token):
        return lax.optimization_barrier((a, token))[0]

    half = max(kv_count // 2, 1)
    spans = [(0, half), (half, kv_count - half)] if kv_count > 1 else [(0, 1)]
    every = []

    def soft(blocks, state, token, form, span=None, last=False, into=None):
        if not any(a is blocks[0][0] for a, _ in every):
            every.extend(blocks)
        *state, token = soft_step(
            pos, soft_query, blocks, every, state, into, span or (0, kv_count), kv_count, last, token, form
        )
        return state, token

    def pair(a, rule, token):
        return [(a, rule), (over_core(after(a, token)), rule)]

    paired = jnp.concatenate([soft_key, soft_value], axis=1)
    own = [(paired, "own"), (over_core(paired), "core")]
    beside = over_x(paired)
    same = over_z(paired, 1)

    send, keep, cum, cumt, token = local_state(
        pos, light_key, light_value, after(log_decay.T, own[1][0])
    )
    other = over_core(send)
    quarter = (length, HD)
    both = (2, qh * HD, HD)

    state, token = soft(own, None, token, FORMS[0])
    blocks = pair(beside, "x", token) + pair(same, 1, token)
    ahead = over_z(after(same, token), 1)
    beside = over_x(after(same, token))
    state, token = soft(blocks, state, token, FORMS[0], spans[0])
    chip_send, chip_keep, token = small(chip_kernel, pos, [keep, other], [quarter, quarter], qh, "chip", token)
    chip_other = over_x(chip_send)
    if len(spans) > 1:
        state, token = soft(blocks, state, token, FORMS[1], spans[1])
    plane, token = small(plane_kernel, pos, [chip_keep, chip_other], [quarter], qh, "plane", token)
    before = over_z(plane, 1)

    def hop(before, token):
        out, token = small(step_kernel, pos, [before, plane], [quarter], qh, "step", token)
        return over_z(out, 1), token

    hops = planes - 2
    for d in range(1, planes - 1):
        same = ahead
        blocks = pair(beside, d, token) + pair(same, d + 1, token)
        beside = over_x(after(same, token))
        if d < planes - 2:
            ahead = over_z(after(same, token), 1)
        for n, span in enumerate(spans):
            state, token = soft(blocks, state, token, FORMS[2 * d + n], span)
            if hops:
                before, token = hop(before, token)
                hops -= 1
    assert hops == 0
    enter_send, enter_keep, token = small(
        enter_kernel, pos, [chip_keep, chip_other, before], [quarter, quarter], qh, "enter", token
    )
    enter_other = over_x(enter_send)
    blocks = pair(beside, planes - 1, token)
    soft_out, token = soft(blocks, state, token, FORMS[6], spans[0], True)
    state_send, state_keep, token = small(
        core_kernel, pos, [enter_keep, enter_other, keep, other], [both, both], qh, "core", token
    )
    state_other = over_core(state_send)
    if len(spans) > 1:
        soft_out, token = soft(blocks, state, token, FORMS[7], spans[1], True, soft_out)
    raw, square, token = light(
        pos, light_query, light_key, light_value, cum, cumt, state_keep, state_other, token
    )
    squares = [square]
    step = 1
    while step < tp:
        square = sum(squares)
        squares = [square, lax.ppermute(square, "tp", [(i, i ^ step) for i in range(tp)])]
        step *= 2
    light_out = finish(raw, squares, norm_gain, out_gate, heads * HD * tp, token)
    return (light_out, soft_out[0])


def solution(mesh):
    both = P("ctx", "tp")
    return jax.shard_map(
        functools.partial(local, ctx=mesh.shape["ctx"], tp=mesh.shape["tp"]),
        mesh=mesh,
        in_specs=(both, both, both, both, both, P("tp"), both, both, both),
        out_specs=(both, both),
        check_vma=False,
    )
```

```python
import functools
import math

import jax
import jax.numpy as jnp
from jax import lax
from jax.experimental import pallas as pl
from jax.experimental.pallas import tpu as pltpu
from jax.sharding import PartitionSpec as P

HD = 128
EPS = 1e-06
LOW = -1e30
LIMIT = 2.0**100
PLANE = 4
TAIL = 16
VMEM = 32 * 2**20
BIG = 60 * 2**20
F32 = jnp.float32
BF16 = jnp.bfloat16
HIGH = lax.Precision.HIGHEST
SCALAR = pl.BlockSpec(memory_space=pltpu.SMEM)
ANY = pl.BlockSpec(memory_space=pl.ANY)
NEXT = jax.ShapeDtypeStruct((1,), jnp.int32)
FORMS = [(2, True), (2, False), (2, True), (2, False), (2, True), (2, False)]
COST = pl.CostEstimate(flops=1000, bytes_accessed=2**20, transcendentals=0)
SCALE = HD ** (-0.5)
SCALE2 = HD ** (-0.5) * math.log2(math.e)


def params(limit=None):
    return pltpu.CompilerParams(vmem_limit_bytes=limit or VMEM)


def mm(a, b):
    return lax.dot_general(a, b, (((1,), (0,)), ((), ())), preferred_element_type=F32)


def mm_bt(a, b):
    return lax.dot_general(a, b, (((1,), (1,)), ((), ())), preferred_element_type=F32)


def mm_at(a, b):
    return lax.dot_general(a, b, (((0,), (0,)), ((), ())), preferred_element_type=F32)


def z_of(pos):
    return pos[0] // PLANE


def x_of(pos):
    return (pos[0] // 2) % 2


def core_of(pos):
    return pos[0] % 2


def iota(shape, dim):
    return lax.broadcasted_iota(jnp.int32, shape, dim)


def state_kernel(pos, k_ref, v_ref, ld_ref, send_ref, keep_ref, cum_ref, cumt_ref, after, fin, *, qh, heads):
    after[0] = pos[0]
    step = pl.program_id(0)
    rows = ld_ref.shape[1]

    @pl.when(step == 0)
    def _():
        upper = (iota((rows, rows), 0) <= iota((rows, rows), 1)).astype(F32).astype(BF16)
        ld = ld_ref[...]
        high = ld.astype(BF16)
        rest = ld - high.astype(F32)
        middle = rest.astype(BF16)
        low = (rest - middle.astype(F32)).astype(BF16)
        cumt = mm(high, upper) + (mm(middle, upper) + mm(low, upper))
        full = jnp.concatenate([cumt, jnp.zeros((HD - heads, rows), F32)], axis=0)
        cum = jnp.transpose(full)
        ends = jnp.broadcast_to(cumt[:, rows - 1 : rows], (heads, HD))
        fin[...] = jnp.zeros_like(fin)
        cumt_ref[...] = jnp.zeros_like(cumt_ref)
        cum_ref[...] = jnp.zeros_like(cum_ref)
        for i in range(4):
            cum_ref[i, :, 0:qh] = cum[:, i * qh : (i + 1) * qh]
            cumt_ref[i, 0:qh, :] = cumt[i * qh : (i + 1) * qh, :]
            fin[i, 0:qh, :] = ends[i * qh : (i + 1) * qh, :]

    core = pos[0] & 1
    kept = step // 2
    part = step % 2
    quarter = part * 2 + jnp.where(kept == 1, core, 1 - core)
    cum = cum_ref[quarter]
    weight = jnp.exp(cum[rows - 1 : rows, :] - cum)
    tail = fin[quarter]
    high = tail.astype(BF16).astype(F32)
    tail = jnp.concatenate([high, tail - high], axis=0).astype(BF16)
    states = []
    for i in range(qh):
        cols = slice(i * HD, (i + 1) * HD)
        keyed = (k_ref[:, cols].astype(F32) * weight[:, i : i + 1]).astype(BF16)
        states.append(mm_at(keyed, v_ref[:, cols]).astype(BF16))

    def put(ref):
        for i in range(qh):
            ref[part, i * HD : (i + 1) * HD, :] = states[i]
        ref[part, qh * HD : qh * HD + TAIL, :] = tail

    @pl.when(kept == 0)
    def _():
        put(send_ref)

    @pl.when(kept == 1)
    def _():
        put(keep_ref)


def local_state(pos, key, value, log_decay):
    heads, rows = log_decay.shape
    qh = heads // 4
    length = qh * HD + TAIL

    def columns(step, pos):
        core = pos[0] & 1
        return (0, (step % 2) * 2 + jnp.where(step // 2 == 1, core, 1 - core))

    whole = lambda *shape: pl.BlockSpec(shape, lambda step, pos: (0,) * len(shape))
    return pl.pallas_call(
        functools.partial(state_kernel, qh=qh, heads=heads),
        grid_spec=pltpu.PrefetchScalarGridSpec(
            num_scalar_prefetch=1,
            grid=(4,),
            in_specs=[
                pl.BlockSpec((rows, qh * HD), columns),
                pl.BlockSpec((rows, qh * HD), columns),
                whole(heads, rows),
            ],
            out_specs=[
                whole(2, length, HD),
                whole(2, length, HD),
                whole(4, rows, HD),
                whole(4, 8, rows),
                SCALAR,
            ],
            scratch_shapes=[pltpu.VMEM((4, 8, HD), F32)],
        ),
        out_shape=[
            jax.ShapeDtypeStruct((2, length, HD), BF16),
            jax.ShapeDtypeStruct((2, length, HD), BF16),
            jax.ShapeDtypeStruct((4, rows, HD), F32),
            jax.ShapeDtypeStruct((4, 8, rows), F32),
            NEXT,
        ],
        compiler_params=params(BIG),
        cost_estimate=COST,
        name="local_state",
    )(pos, key, value, log_decay)


def spread(item, qh):
    tail = item[qh * HD : qh * HD + TAIL, :].astype(F32)
    return item[0 : qh * HD, :].astype(F32), tail[0:8, :] + tail[8:16, :]


def pack(states, logs):
    high = logs.astype(BF16).astype(F32)
    return states.astype(BF16), jnp.concatenate([high, logs - high], axis=0).astype(BF16)


def decay(states, logs, qh):
    factor = jnp.exp(logs)
    return jnp.concatenate(
        [states[i * HD : (i + 1) * HD, :] * factor[i : i + 1, :] for i in range(qh)], axis=0
    )


def joined(early, late, qh):
    return decay(early[0], late[1], qh) + late[0], early[1] + late[1]


def store(ref, item, qh):
    states, tail = pack(*item)
    ref[0 : qh * HD, :] = states
    ref[qh * HD : qh * HD + TAIL, :] = tail


def chip_kernel(pos, keep_ref, recv_ref, send_out, keep_out, *, qh):
    first = core_of(pos) == 0
    for out, part in ((send_out, 1 - x_of(pos)), (keep_out, x_of(pos))):
        own, other = keep_ref[part], recv_ref[part]
        early = spread(jnp.where(first, own, other), qh)
        late = spread(jnp.where(first, other, own), qh)
        store(out, joined(early, late, qh), qh)


def plane_kernel(pos, keep_ref, recv_ref, out, *, qh):
    first = x_of(pos) == 0
    own, other = keep_ref[...], recv_ref[...]
    early = spread(jnp.where(first, own, other), qh)
    late = spread(jnp.where(first, other, own), qh)
    store(out, joined(early, late, qh), qh)


def step_kernel(pos, early_ref, late_ref, out, *, qh):
    store(out, joined(spread(early_ref[...], qh), spread(late_ref[...], qh), qh), qh)


def enter_kernel(pos, keep_ref, recv_ref, total_ref, send_out, keep_out, *, qh):
    first = x_of(pos) == 0
    early = spread(jnp.where(first, keep_ref[...], recv_ref[...]), qh)
    total = spread(total_ref[...], qh)
    zero, one = pack(*total), pack(*joined(total, early, qh))
    for out, take in ((send_out, first), (keep_out, jnp.logical_not(first))):
        out[0 : qh * HD, :] = jnp.where(take, one[0], zero[0])
        out[qh * HD : qh * HD + TAIL, :] = jnp.where(take, one[1], zero[1])


def core_kernel(pos, enter_keep, enter_recv, keep_ref, recv_ref, send_out, keep_out, *, qh):
    first = core_of(pos) == 0
    for part in range(2):
        entering = spread(jnp.where(x_of(pos) == part, enter_keep[...], enter_recv[...]), qh)
        own = spread(jnp.where(first, keep_ref[part], recv_ref[part]), qh)
        later = joined(entering, own, qh)[0].astype(BF16)
        now = entering[0].astype(BF16)
        send_out[part] = jnp.where(first, later, now)
        keep_out[part] = jnp.where(first, now, later)


def with_token(kernel, pos, token, *refs):
    refs[-1][0] = token[0]
    kernel(pos, *refs[:-1])


def small(kernel, pos, arrays, outs, qh, name, token):
    return pl.pallas_call(
        functools.partial(with_token, functools.partial(kernel, qh=qh)),
        in_specs=[SCALAR, SCALAR] + [pl.BlockSpec(memory_space=pltpu.VMEM)] * len(arrays),
        out_specs=[pl.BlockSpec(memory_space=pltpu.VMEM)] * len(outs) + [SCALAR],
        out_shape=[jax.ShapeDtypeStruct(s, BF16) for s in outs] + [NEXT],
        compiler_params=pltpu.CompilerParams(vmem_limit_bytes=24 * 2**20),
        cost_estimate=COST,
        name=name,
    )(pos, token, *arrays)


def light_kernel(pos, q_ref, k_ref, v_ref, cum_ref, cumt_ref, keep_ref, recv_ref, token, out_ref, ss_ref, after, *, qh):
    after[0] = token[0]
    rows = q_ref.shape[0]
    quarter = pl.program_id(0)
    part = quarter // 2
    mine = quarter % 2 == core_of(pos)
    causal = iota((rows, rows), 0) >= iota((rows, rows), 1)
    cum, cumt = cum_ref[0], cumt_ref[0]
    factor = jnp.exp(cum)
    state = jnp.where(mine, keep_ref[part], recv_ref[part])
    total = jnp.zeros((rows, HD), F32)
    for i in range(qh):
        cols = slice(i * HD, (i + 1) * HD)
        query = q_ref[:, cols]
        scores = mm_bt(query, k_ref[:, cols])
        gap = jnp.where(causal, cum[:, i : i + 1] - cumt[i : i + 1, :], LOW)
        weights = (scores * jnp.exp(gap)).astype(BF16)
        carried = mm(query, state[i * HD : (i + 1) * HD, :])
        raw = mm(weights, v_ref[:, cols]) + factor[:, i : i + 1] * carried
        out_ref[:, cols] = raw.astype(BF16)
        total = total + raw * raw

    @pl.when(quarter == 0)
    def _():
        ss_ref[...] = total

    @pl.when(quarter > 0)
    def _():
        ss_ref[...] += total


def light(pos, query, key, value, cum, cumt, keep, recv, token):
    rows, width = query.shape
    wide = width // 4
    block = pl.BlockSpec((rows, wide), lambda i: (0, i))
    whole = pl.BlockSpec(keep.shape, lambda i: (0, 0, 0))
    return pl.pallas_call(
        functools.partial(light_kernel, qh=wide // HD),
        grid=(4,),
        in_specs=[
            SCALAR,
            block,
            block,
            block,
            pl.BlockSpec((1, rows, HD), lambda i: (i, 0, 0)),
            pl.BlockSpec((1, 8, rows), lambda i: (i, 0, 0)),
            whole,
            whole,
            SCALAR,
        ],
        out_specs=[block, pl.BlockSpec((rows, HD), lambda i: (0, 0)), SCALAR],
        out_shape=[jax.ShapeDtypeStruct((rows, width), BF16), jax.ShapeDtypeStruct((rows, HD), F32), NEXT],
        compiler_params=params(),
        cost_estimate=COST,
        name="light",
    )(pos, query, key, value, cum, cumt, keep, recv, token)


def finish_kernel(raw_ref, *refs, features):
    squares, (gain_ref, gate_ref, token, out_ref, factor) = refs[:-5], refs[-5:]

    @pl.when(pl.program_id(0) == 0)
    def _():
        square = squares[0][...]
        for more in squares[1:]:
            square = square + more[...]
        mean = jnp.sum(square, axis=1, keepdims=True) / features
        factor[...] = jnp.broadcast_to(lax.rsqrt(mean + EPS), factor.shape)

    for i in range(out_ref.shape[1] // HD):
        cols = slice(i * HD, (i + 1) * HD)
        gate = 0.5 * jnp.tanh(0.5 * gate_ref[:, cols].astype(F32)) + 0.5
        raw = raw_ref[:, cols].astype(F32)
        out_ref[:, cols] = (raw * factor[...] * gain_ref[:, cols] * gate).astype(BF16)


def finish(raw, squares, gain, gate, features, token):
    rows, width = raw.shape
    wide = width // 4
    block = pl.BlockSpec((rows, wide), lambda i: (0, i))
    return pl.pallas_call(
        functools.partial(finish_kernel, features=features),
        grid=(4,),
        in_specs=[block]
        + [pl.BlockSpec((rows, HD), lambda i: (0, 0))] * len(squares)
        + [pl.BlockSpec((1, wide), lambda i: (0, i)), block, SCALAR],
        out_specs=block,
        out_shape=jax.ShapeDtypeStruct((rows, width), BF16),
        scratch_shapes=[pltpu.VMEM((rows, HD), F32)],
        compiler_params=params(),
        cost_estimate=COST,
        name="finish",
    )(raw, *squares, gain.reshape(1, width), gate, token)


def shown(pos, rule):
    if rule == "x":
        return x_of(pos) == 1
    if rule == "core":
        return core_of(pos) == 1
    return z_of(pos) >= rule


def soft_kernel(pos, q_ref, *refs, group, rules, all_rules, last, passed, kv_count, begin, form):
    pair, natural = form
    pair = min(pair, group)
    count = len(rules)
    keys, values, refs = refs[:count], refs[count : 2 * count], refs[2 * count :]
    first = rules[0] == "own"
    if not first:
        acc_in, stat_in, refs = refs[0], refs[1], refs[2:]
    token, every, refs = refs[0], refs[1:passed], refs[passed:]
    if last:
        out_ref, after, acc, stat, key_all, value_all = refs
    else:
        acc, stat, after = refs
        stat = stat.at[0]
    after[0] = token[0]
    rows = q_ref.shape[0]
    lane = iota((rows, HD), 1)
    causal = iota((rows, rows), 0) >= iota((rows, rows), 1)

    if not first:
        acc[...] = acc_in[...]
        stat[...] = stat_in[0]

    def attend(keyed, valued, fresh, hidden):
        wide = jnp.concatenate([v[...] for v in valued], axis=0)
        wide = jnp.concatenate([wide, jnp.ones_like(wide)], axis=1)
        keyed = [k[...] for k in keyed]
        if fresh:
            own = keyed[0].astype(F32)
            shifts = [
                jnp.sum(q_ref[:, g * HD : (g + 1) * HD].astype(F32) * own, axis=1, keepdims=True)
                for g in range(group)
            ]
        else:
            shifts = [stat[:, g : g + 1] for g in range(group)]
        def scored(i):
            parts = []
            for g in range(i, i + pair):
                query = q_ref[:, g * HD : (g + 1) * HD]
                parts.append(query)
            query = jnp.concatenate(parts, axis=0)
            return [mm_bt(query, k) for k in keyed]

        for i in range(0, group, pair):
            scores = scored(i)
            scale = SCALE if natural else SCALE2
            shift = jnp.concatenate(shifts[i : i + pair], axis=0) * scale
            probs = []
            for n, s in enumerate(scores):
                x = s * scale - (shift - hidden[n])
                if fresh and n == 0:
                    x = jnp.concatenate(
                        [jnp.where(causal, x[m * rows : (m + 1) * rows], LOW) for m in range(pair)], axis=0
                    )
                probs.append((jnp.exp(x) if natural else jnp.exp2(x)).astype(BF16))
            out = mm(jnp.concatenate(probs, axis=1), wide)
            for n in range(pair):
                g = i + n
                cols = slice(g * HD, (g + 1) * HD)
                band = slice(n * rows, (n + 1) * rows)
                summed, total = out[band, :HD], out[band, HD:]
                if fresh:
                    acc[:, cols] = summed
                    old = jnp.where(lane == g, shifts[g], 0.0 if g == 0 else stat[...])
                    stat[...] = jnp.where(lane == group + g, total, old)
                else:
                    acc[:, cols] += summed
                    stat[...] += jnp.where(lane == group + g, total, 0.0)

    for begin_at in range(0, count, PLANE):
        here = slice(begin_at, begin_at + PLANE)
        some = rules[here]
        if some[0] == "own":
            hidden = [0.0] + [jnp.where(shown(pos, r), 0.0, LOW).astype(F32) for r in some[1:]]
            attend(keys[here], values[here], True, hidden)
        else:
            pl.when(shown(pos, some[0]))(
                functools.partial(attend, keys[here], values[here], False, [0.0] * PLANE)
            )
    if not last:
        return
    inverse = 1.0 / jnp.where((lane >= group) & (lane < 2 * group), stat[...], 1.0)
    for g in range(group):
        cols = slice(g * HD, (g + 1) * HD)
        out_ref[:, cols] = (acc[:, cols] * inverse[:, group + g : group + g + 1]).astype(BF16)

    sums = jnp.where((lane >= group) & (lane < 2 * group), stat[...], 0.0)
    fine = jnp.min(jnp.where(sums < LIMIT, 1.0, 0.0))

    @pl.when(fine < 0.5)
    def _():
        head = begin + pl.program_id(0)
        for n in range(len(all_rules)):
            here = pl.ds(n * rows, rows)
            pltpu.sync_copy(every[n].at[:, pl.ds(pl.multiple_of(head * HD, HD), HD)], key_all.at[here])
            pltpu.sync_copy(
                every[n].at[:, pl.ds(pl.multiple_of((kv_count + head) * HD, HD), HD)], value_all.at[here]
            )

        def one(g, carry):
            cols = pl.ds(pl.multiple_of(g * HD, HD), HD)
            query = q_ref[:, cols]
            top = total = summed = None
            for n, rule in enumerate(all_rules):
                here = slice(n * rows, (n + 1) * rows)
                x = mm_bt(query, key_all[here, :]) * SCALE2
                if n == 0:
                    x = jnp.where(causal, x, LOW)
                else:
                    x = jnp.where(shown(pos, rule), x, LOW)
                high = jnp.max(x, axis=1, keepdims=True)
                if n > 0:
                    high = jnp.maximum(high, top)
                probs = jnp.exp2(x - high)
                part = mm(probs.astype(BF16), value_all[here, :])
                more = jnp.sum(probs, axis=1, keepdims=True)
                if n > 0:
                    keep = jnp.exp2(top - high)
                    part = part + keep * summed
                    more = more + keep * total
                top, total, summed = high, more, part
            out_ref[:, cols] = (summed / total).astype(BF16)
            return carry

        lax.fori_loop(0, group, one, 0)


def soft_step(pos, query, blocks, every, state, into, span, kv_count, last, token, form):
    rows, width = query.shape
    group = width // HD // kv_count
    used, rules = zip(*blocks)
    used = list(used)
    first = rules[0] == "own"
    begin, count = span
    block = pl.BlockSpec((rows, group * HD), lambda k: (0, begin + k))
    stat = pl.BlockSpec((1, rows, HD), lambda k: (begin + k, 0, 0))
    keys = pl.BlockSpec((rows, HD), lambda k: (0, begin + k))
    values = pl.BlockSpec((rows, HD), lambda k: (0, kv_count + begin + k))
    in_specs = [SCALAR, block] + [keys] * len(used) + [values] * len(used)
    operands = [pos, query] + used + used
    aliases = {}
    if not first:
        if not last:
            aliases = {len(operands): 0, len(operands) + 1: 1}
        in_specs += [block, stat]
        operands += list(state)
    in_specs.append(SCALAR)
    operands.append(token)
    rest = [a for a, _ in every] if last else []
    if into is not None:
        for i, a in enumerate(into):
            aliases[len(operands) + len(rest) + i] = i
        rest = rest + list(into)
    in_specs += [ANY] * len(rest)
    operands += rest
    if last:
        out_specs = [block, SCALAR]
        out_shape = [jax.ShapeDtypeStruct((rows, width), BF16), NEXT]
        scratch = [pltpu.VMEM((rows, group * HD), F32), pltpu.VMEM((rows, HD), F32)]
        scratch += [pltpu.VMEM((len(every) * rows, HD), BF16)] * 2
    else:
        out_specs = [block, stat, SCALAR]
        out_shape = [
            jax.ShapeDtypeStruct((rows, width), F32),
            jax.ShapeDtypeStruct((kv_count, rows, HD), F32),
            NEXT,
        ]
        scratch = []
    return pl.pallas_call(
        functools.partial(
            soft_kernel,
            group=group,
            rules=rules,
            all_rules=[rule for _, rule in every],
            last=last,
            passed=1 + len(rest),
            kv_count=kv_count,
            begin=begin,
            form=form,
        ),
        grid=(count,),
        in_specs=in_specs,
        out_specs=out_specs,
        out_shape=out_shape,
        scratch_shapes=scratch,
        input_output_aliases=aliases,
        compiler_params=params(),
        cost_estimate=COST,
        name="softmax",
    )(*operands)


def local(
    light_query,
    light_key,
    light_value,
    log_decay,
    out_gate,
    norm_gain,
    soft_query,
    soft_key,
    soft_value,
    *,
    ctx,
    tp,
):
    rows, heads = log_decay.shape
    qh = heads // 4
    length = qh * HD + TAIL
    planes = ctx // PLANE
    kv_count = soft_key.shape[1] // HD
    place = lax.axis_index("ctx")
    pos = place.astype(jnp.int32).reshape(1)

    def over_core(a):
        return lax.ppermute(a, "ctx", [(i, i ^ 1) for i in range(ctx)])

    def over_x(a):
        return lax.ppermute(a, "ctx", [(i, i ^ 2) for i in range(ctx)])

    def over_z(a, d):
        return lax.ppermute(a, "ctx", [(i, i + PLANE * d) for i in range(ctx - PLANE * d)])

    def after(a, token):
        return lax.optimization_barrier((a, token))[0]

    half = max(kv_count // 2, 1)
    spans = [(0, half), (half, kv_count - half)] if kv_count > 1 else [(0, 1)]
    every = []

    def soft(blocks, state, token, form, span=None, last=False, into=None):
        for block in blocks:
            if not any(a is block[0] for a, _ in every):
                every.append(block)
        *state, token = soft_step(
            pos, soft_query, blocks, every, state, into, span or (0, kv_count), kv_count, last, token, form
        )
        return state, token

    def pair(a, rule, token):
        return [(a, rule), (over_core(after(a, token)), rule)]

    paired = jnp.concatenate([soft_key, soft_value], axis=1)
    own = [(paired, "own"), (over_core(paired), "core")]
    beside = over_x(paired)
    same = over_z(paired, 1)

    send, keep, cum, cumt, token = local_state(
        pos, light_key, light_value, after(log_decay.T, own[1][0])
    )
    other = over_core(send)
    quarter = (length, HD)
    both = (2, qh * HD, HD)

    own += pair(beside, "x", own[0][0])
    first, rest = spans[0], spans[1:]
    ahead = over_z(after(same, token), 1)
    beside = over_x(after(same, token))
    state, token = soft(own, None, token, FORMS[0], first)
    chip_send, chip_keep, token = small(chip_kernel, pos, [keep, other], [quarter, quarter], qh, "chip", token)
    chip_other = over_x(chip_send)
    for span in rest:
        state, token = soft(own, state, token, FORMS[1], span, False, state)
    plane, token = small(plane_kernel, pos, [chip_keep, chip_other], [quarter], qh, "plane", token)
    before = over_z(plane, 1)

    def hop(before, token):
        out, token = small(step_kernel, pos, [before, plane], [quarter], qh, "step", token)
        return over_z(out, 1), token

    def enter(token):
        send, keep, token = small(
            enter_kernel, pos, [chip_keep, chip_other, before], [quarter, quarter], qh, "enter", token
        )
        return keep, over_x(send), token

    def leave(token):
        send, now, token = small(
            core_kernel, pos, [enter_keep, enter_other, keep, other], [both, both], qh, "core", token
        )
        return now, over_core(send), token

    blocks = pair(same, 1, token) + pair(beside, 1, token)
    if planes == 4 and kv_count == 4:
        one = blocks
        same, beside = ahead, over_x(after(ahead, token))
        ahead = over_z(after(ahead, token), 1)
        state, token = soft(one, state, token, FORMS[2], (0, 2))
        before, token = hop(before, token)
        two = pair(same, 2, token) + pair(beside, 2, token)
        same, beside = ahead, over_x(after(ahead, token))
        state, token = soft(one + two, state, token, FORMS[3], (2, 2))
        before, token = hop(before, token)
        three = pair(same, 3, token) + pair(beside, 3, token)
        soft_out, token = soft(two + three, state, token, FORMS[4], (0, 1), True)
        enter_keep, enter_other, token = enter(token)
        soft_out, token = soft(two + three, state, token, FORMS[4], (1, 1), True, soft_out)
        state_keep, state_other, token = leave(token)
        soft_out, token = soft(three, state, token, FORMS[5], (2, 1), True, soft_out)
    else:
        for d in range(1, planes - 1):
            state, token = soft(blocks, state, token, FORMS[2])
            before, token = hop(before, token)
            same, beside = ahead, over_x(after(ahead, token))
            ahead = over_z(after(ahead, token), 1)
            blocks = pair(same, d + 1, token) + pair(beside, d + 1, token)
        enter_keep, enter_other, token = enter(token)
        soft_out, token = soft(blocks, state, token, FORMS[4], None, True)
        state_keep, state_other, token = leave(token)
    raw, square, token = light(
        pos, light_query, light_key, light_value, cum, cumt, state_keep, state_other, token
    )
    if planes == 4 and kv_count == 4:
        soft_out, token = soft(three, state, token, FORMS[5], (3, 1), True, soft_out)
    squares = [square]
    step = 1
    while step < tp:
        square = sum(squares)
        squares = [square, lax.ppermute(square, "tp", [(i, i ^ step) for i in range(tp)])]
        step *= 2
    light_out = finish(raw, squares, norm_gain, out_gate, heads * HD * tp, token)
    return (light_out, soft_out[0])


def solution(mesh):
    both = P("ctx", "tp")
    return jax.shard_map(
        functools.partial(local, ctx=mesh.shape["ctx"], tp=mesh.shape["tp"]),
        mesh=mesh,
        in_specs=(both, both, both, both, both, P("tp"), both, both, both),
        out_specs=(both, both),
        check_vma=False,
    )
```

```python
import functools
import math

import jax
import jax.numpy as jnp
from jax import lax
from jax.experimental import pallas as pl
from jax.experimental.pallas import tpu as pltpu
from jax.sharding import PartitionSpec as P

HD = 128
EPS = 1e-06
LOW = -1e30
LIMIT = 2.0**100
PLANE = 4
TAIL = 16
VMEM = 32 * 2**20
BIG = 60 * 2**20
F32 = jnp.float32
BF16 = jnp.bfloat16
HIGH = lax.Precision.HIGHEST
SCALAR = pl.BlockSpec(memory_space=pltpu.SMEM)
ANY = pl.BlockSpec(memory_space=pl.ANY)
NEXT = jax.ShapeDtypeStruct((1,), jnp.int32)
QUAD = 4
COST = pl.CostEstimate(flops=1000, bytes_accessed=2**20, transcendentals=0)
SCALE2 = HD ** (-0.5) * math.log2(math.e)


def params(limit=None):
    return pltpu.CompilerParams(vmem_limit_bytes=limit or VMEM)


def mm(a, b):
    return lax.dot_general(a, b, (((1,), (0,)), ((), ())), preferred_element_type=F32)


def mm_bt(a, b):
    return lax.dot_general(a, b, (((1,), (1,)), ((), ())), preferred_element_type=F32)


def mm_at(a, b):
    return lax.dot_general(a, b, (((0,), (0,)), ((), ())), preferred_element_type=F32)


def z_of(pos):
    return pos[0] // PLANE


def x_of(pos):
    return (pos[0] // 2) % 2


def core_of(pos):
    return pos[0] % 2


def iota(shape, dim):
    return lax.broadcasted_iota(jnp.int32, shape, dim)


def state_kernel(pos, k_ref, v_ref, ld_ref, send_ref, keep_ref, cum_ref, cumt_ref, after, fin, *, qh, heads):
    after[0] = pos[0]
    step = pl.program_id(0)
    rows = ld_ref.shape[1]

    @pl.when(step == 0)
    def _():
        upper = (iota((rows, rows), 0) <= iota((rows, rows), 1)).astype(F32).astype(BF16)
        ld = ld_ref[...]
        high = ld.astype(BF16)
        rest = ld - high.astype(F32)
        middle = rest.astype(BF16)
        low = (rest - middle.astype(F32)).astype(BF16)
        cumt = mm(high, upper) + (mm(middle, upper) + mm(low, upper))
        full = jnp.concatenate([cumt, jnp.zeros((HD - heads, rows), F32)], axis=0)
        cum = jnp.transpose(full)
        ends = jnp.broadcast_to(cumt[:, rows - 1 : rows], (heads, HD))
        fin[...] = jnp.zeros_like(fin)
        cumt_ref[...] = jnp.zeros_like(cumt_ref)
        cum_ref[...] = jnp.zeros_like(cum_ref)
        for i in range(4):
            cum_ref[i, :, 0:qh] = cum[:, i * qh : (i + 1) * qh]
            cumt_ref[i, 0:qh, :] = cumt[i * qh : (i + 1) * qh, :]
            fin[i, 0:qh, :] = ends[i * qh : (i + 1) * qh, :]

    core = pos[0] & 1
    kept = step // 2
    part = step % 2
    quarter = part * 2 + jnp.where(kept == 1, core, 1 - core)
    cum = cum_ref[quarter]
    weight = jnp.exp(cum[rows - 1 : rows, :] - cum)
    tail = fin[quarter]
    high = tail.astype(BF16).astype(F32)
    tail = jnp.concatenate([high, tail - high], axis=0).astype(BF16)
    states = []
    for i in range(qh):
        cols = slice(i * HD, (i + 1) * HD)
        keyed = (k_ref[:, cols].astype(F32) * weight[:, i : i + 1]).astype(BF16)
        states.append(mm_at(keyed, v_ref[:, cols]).astype(BF16))

    def put(ref):
        for i in range(qh):
            ref[part, i * HD : (i + 1) * HD, :] = states[i]
        ref[part, qh * HD : qh * HD + TAIL, :] = tail

    @pl.when(kept == 0)
    def _():
        put(send_ref)

    @pl.when(kept == 1)
    def _():
        put(keep_ref)


def local_state(pos, key, value, log_decay):
    heads, rows = log_decay.shape
    qh = heads // 4
    length = qh * HD + TAIL

    def columns(step, pos):
        core = pos[0] & 1
        return (0, (step % 2) * 2 + jnp.where(step // 2 == 1, core, 1 - core))

    whole = lambda *shape: pl.BlockSpec(shape, lambda step, pos: (0,) * len(shape))
    return pl.pallas_call(
        functools.partial(state_kernel, qh=qh, heads=heads),
        grid_spec=pltpu.PrefetchScalarGridSpec(
            num_scalar_prefetch=1,
            grid=(4,),
            in_specs=[
                pl.BlockSpec((rows, qh * HD), columns),
                pl.BlockSpec((rows, qh * HD), columns),
                whole(heads, rows),
            ],
            out_specs=[
                whole(2, length, HD),
                whole(2, length, HD),
                whole(4, rows, HD),
                whole(4, 8, rows),
                SCALAR,
            ],
            scratch_shapes=[pltpu.VMEM((4, 8, HD), F32)],
        ),
        out_shape=[
            jax.ShapeDtypeStruct((2, length, HD), BF16),
            jax.ShapeDtypeStruct((2, length, HD), BF16),
            jax.ShapeDtypeStruct((4, rows, HD), F32),
            jax.ShapeDtypeStruct((4, 8, rows), F32),
            NEXT,
        ],
        compiler_params=params(BIG),
        cost_estimate=COST,
        name="local_state",
    )(pos, key, value, log_decay)


def spread(item, qh):
    tail = item[qh * HD : qh * HD + TAIL, :].astype(F32)
    return item[0 : qh * HD, :].astype(F32), tail[0:8, :] + tail[8:16, :]


def pack(states, logs):
    high = logs.astype(BF16).astype(F32)
    return states.astype(BF16), jnp.concatenate([high, logs - high], axis=0).astype(BF16)


def decay(states, logs, qh):
    factor = jnp.exp(logs)
    return jnp.concatenate(
        [states[i * HD : (i + 1) * HD, :] * factor[i : i + 1, :] for i in range(qh)], axis=0
    )


def joined(early, late, qh):
    return decay(early[0], late[1], qh) + late[0], early[1] + late[1]


def store(ref, item, qh):
    states, tail = pack(*item)
    ref[0 : qh * HD, :] = states
    ref[qh * HD : qh * HD + TAIL, :] = tail


def chip_kernel(pos, keep_ref, recv_ref, send_out, keep_out, *, qh):
    first = core_of(pos) == 0
    for out, part in ((send_out, 1 - x_of(pos)), (keep_out, x_of(pos))):
        own, other = keep_ref[part], recv_ref[part]
        early = spread(jnp.where(first, own, other), qh)
        late = spread(jnp.where(first, other, own), qh)
        store(out, joined(early, late, qh), qh)


def plane_kernel(pos, keep_ref, recv_ref, out, *, qh):
    first = x_of(pos) == 0
    own, other = keep_ref[...], recv_ref[...]
    early = spread(jnp.where(first, own, other), qh)
    late = spread(jnp.where(first, other, own), qh)
    store(out, joined(early, late, qh), qh)


def step_kernel(pos, early_ref, late_ref, out, *, qh):
    store(out, joined(spread(early_ref[...], qh), spread(late_ref[...], qh), qh), qh)


def enter_kernel(pos, keep_ref, recv_ref, total_ref, send_out, keep_out, *, qh):
    first = x_of(pos) == 0
    early = spread(jnp.where(first, keep_ref[...], recv_ref[...]), qh)
    total = spread(total_ref[...], qh)
    zero, one = pack(*total), pack(*joined(total, early, qh))
    for out, take in ((send_out, first), (keep_out, jnp.logical_not(first))):
        out[0 : qh * HD, :] = jnp.where(take, one[0], zero[0])
        out[qh * HD : qh * HD + TAIL, :] = jnp.where(take, one[1], zero[1])


def core_kernel(pos, enter_keep, enter_recv, keep_ref, recv_ref, send_out, keep_out, *, qh):
    first = core_of(pos) == 0
    for part in range(2):
        entering = spread(jnp.where(x_of(pos) == part, enter_keep[...], enter_recv[...]), qh)
        own = spread(jnp.where(first, keep_ref[part], recv_ref[part]), qh)
        later = joined(entering, own, qh)[0].astype(BF16)
        now = entering[0].astype(BF16)
        send_out[part] = jnp.where(first, later, now)
        keep_out[part] = jnp.where(first, now, later)


def with_token(kernel, pos, token, *refs):
    refs[-1][0] = token[0]
    kernel(pos, *refs[:-1])


def small(kernel, pos, arrays, outs, qh, name, token):
    return pl.pallas_call(
        functools.partial(with_token, functools.partial(kernel, qh=qh)),
        in_specs=[SCALAR, SCALAR] + [pl.BlockSpec(memory_space=pltpu.VMEM)] * len(arrays),
        out_specs=[pl.BlockSpec(memory_space=pltpu.VMEM)] * len(outs) + [SCALAR],
        out_shape=[jax.ShapeDtypeStruct(s, BF16) for s in outs] + [NEXT],
        compiler_params=pltpu.CompilerParams(vmem_limit_bytes=24 * 2**20),
        cost_estimate=COST,
        name=name,
    )(pos, token, *arrays)


def light_kernel(pos, q_ref, k_ref, v_ref, cum_ref, cumt_ref, keep_ref, recv_ref, token, out_ref, ss_ref, after, *, qh):
    after[0] = token[0]
    rows = q_ref.shape[0]
    quarter = pl.program_id(0)
    part = quarter // 2
    mine = quarter % 2 == core_of(pos)
    causal = iota((rows, rows), 0) >= iota((rows, rows), 1)
    cum, cumt = cum_ref[0], cumt_ref[0]
    factor = jnp.exp(cum)
    state = jnp.where(mine, keep_ref[part], recv_ref[part])
    total = jnp.zeros((rows, HD), F32)
    for i in range(qh):
        cols = slice(i * HD, (i + 1) * HD)
        query = q_ref[:, cols]
        scores = mm_bt(query, k_ref[:, cols])
        gap = jnp.where(causal, cum[:, i : i + 1] - cumt[i : i + 1, :], LOW)
        weights = (scores * jnp.exp(gap)).astype(BF16)
        carried = mm(query, state[i * HD : (i + 1) * HD, :])
        raw = mm(weights, v_ref[:, cols]) + factor[:, i : i + 1] * carried
        out_ref[:, cols] = raw.astype(BF16)
        total = total + raw * raw

    @pl.when(quarter == 0)
    def _():
        ss_ref[...] = total

    @pl.when(quarter > 0)
    def _():
        ss_ref[...] += total


def light(pos, query, key, value, cum, cumt, keep, recv, token):
    rows, width = query.shape
    wide = width // 4
    block = pl.BlockSpec((rows, wide), lambda i: (0, i))
    whole = pl.BlockSpec(keep.shape, lambda i: (0, 0, 0))
    return pl.pallas_call(
        functools.partial(light_kernel, qh=wide // HD),
        grid=(4,),
        in_specs=[
            SCALAR,
            block,
            block,
            block,
            pl.BlockSpec((1, rows, HD), lambda i: (i, 0, 0)),
            pl.BlockSpec((1, 8, rows), lambda i: (i, 0, 0)),
            whole,
            whole,
            SCALAR,
        ],
        out_specs=[block, pl.BlockSpec((rows, HD), lambda i: (0, 0)), SCALAR],
        out_shape=[jax.ShapeDtypeStruct((rows, width), BF16), jax.ShapeDtypeStruct((rows, HD), F32), NEXT],
        compiler_params=params(),
        cost_estimate=COST,
        name="light",
    )(pos, query, key, value, cum, cumt, keep, recv, token)


def finish_kernel(raw_ref, *refs, features):
    squares, (gain_ref, gate_ref, token, out_ref, factor) = refs[:-5], refs[-5:]

    @pl.when(pl.program_id(0) == 0)
    def _():
        square = squares[0][...]
        for more in squares[1:]:
            square = square + more[...]
        mean = jnp.sum(square, axis=1, keepdims=True) / features
        factor[...] = jnp.broadcast_to(lax.rsqrt(mean + EPS), factor.shape)

    for i in range(out_ref.shape[1] // HD):
        cols = slice(i * HD, (i + 1) * HD)
        gate = 0.5 * jnp.tanh(0.5 * gate_ref[:, cols].astype(F32)) + 0.5
        raw = raw_ref[:, cols].astype(F32)
        out_ref[:, cols] = (raw * factor[...] * gain_ref[:, cols] * gate).astype(BF16)


def finish(raw, squares, gain, gate, features, token):
    rows, width = raw.shape
    wide = width // 4
    block = pl.BlockSpec((rows, wide), lambda i: (0, i))
    return pl.pallas_call(
        functools.partial(finish_kernel, features=features),
        grid=(4,),
        in_specs=[block]
        + [pl.BlockSpec((rows, HD), lambda i: (0, 0))] * len(squares)
        + [pl.BlockSpec((1, wide), lambda i: (0, i)), block, SCALAR],
        out_specs=block,
        out_shape=jax.ShapeDtypeStruct((rows, width), BF16),
        scratch_shapes=[pltpu.VMEM((rows, HD), F32)],
        compiler_params=params(),
        cost_estimate=COST,
        name="finish",
    )(raw, *squares, gain.reshape(1, width), gate, token)


def shown(pos, rule):
    if rule == "x":
        return x_of(pos) == 1
    if rule == "core":
        return core_of(pos) == 1
    return z_of(pos) >= rule


def soft_kernel(pos, q_ref, *refs, group, rules, planes, last, passed, kv_count, begin):
    quad = min(QUAD, group)
    pair = min(2, quad)
    count = len(rules)
    keys, values, refs = refs[:count], refs[count : 2 * count], refs[2 * count :]
    first = rules[0] == "own"
    if not first:
        acc_in, stat_in, refs = refs[0], refs[1], refs[2:]
    token, every, refs = refs[0], refs[1:passed], refs[passed:]
    if last:
        out_ref, after, acc, stat, key_all, value_all = refs
    else:
        acc, stat, after = refs
    after[0] = token[0]
    rows = q_ref.shape[0]
    lane = iota((rows, HD), 1)
    causal = iota((rows, rows), 0) >= iota((rows, rows), 1)

    if not first:
        acc[...] = acc_in[...]
        stat[...] = stat_in[...]

    def attend(keyed, valued, fresh, hidden):
        wide = jnp.concatenate([v[...] for v in valued], axis=0)
        wide = jnp.concatenate([wide, jnp.ones_like(wide)], axis=1)
        keyed = [k[...] for k in keyed]
        own = keyed[0].astype(F32)

        def some(j, carry):
            before = jnp.zeros((rows, HD), F32) if fresh else stat[j]
            now = before
            for i in range(0, quad, pair):
                cols = [pl.ds(pl.multiple_of((j * quad + i + m) * HD, HD), HD) for m in range(pair)]
                query = [q_ref[:, c] for c in cols]
                if fresh:
                    shifts = [jnp.sum(q.astype(F32) * own, axis=1, keepdims=True) for q in query]
                else:
                    shifts = [before[:, i + m : i + m + 1] for m in range(pair)]
                query = jnp.concatenate(query, axis=0)
                shift = jnp.concatenate(shifts, axis=0) * SCALE2
                probs = []
                for n, k in enumerate(keyed):
                    x = mm_bt(query, k) * SCALE2 - (shift - hidden[n])
                    if fresh and n == 0:
                        x = jnp.concatenate(
                            [jnp.where(causal, x[m * rows : (m + 1) * rows], LOW) for m in range(pair)], axis=0
                        )
                    probs.append(jnp.exp2(x).astype(BF16))
                out = mm(jnp.concatenate(probs, axis=1), wide)
                for m in range(pair):
                    band = slice(m * rows, (m + 1) * rows)
                    summed, total = out[band, :HD], out[band, HD:]
                    if fresh:
                        acc[:, cols[m]] = summed
                        now = jnp.where(lane == i + m, shifts[m], now)
                    else:
                        acc[:, cols[m]] += summed
                    now = jnp.where(lane == quad + i + m, now + total, now)
            stat[j] = now
            return carry

        lax.fori_loop(0, group // quad, some, 0)

    for begin_at in range(0, count, PLANE):
        here = slice(begin_at, begin_at + PLANE)
        some = rules[here]
        if some[0] == "own":
            hidden = [0.0] + [jnp.where(shown(pos, r), 0.0, LOW).astype(F32) for r in some[1:]]
            attend(keys[here], values[here], True, hidden)
        else:
            pl.when(shown(pos, some[0]))(
                functools.partial(attend, keys[here], values[here], False, [0.0] * PLANE)
            )
    if not last:
        return
    totals = (lane >= quad) & (lane < 2 * quad)
    fine = None
    for j in range(group // quad):
        inverse = 1.0 / jnp.where(totals, stat[j], 1.0)
        for m in range(quad):
            cols = slice((j * quad + m) * HD, (j * quad + m + 1) * HD)
            out_ref[:, cols] = (acc[:, cols] * inverse[:, quad + m : quad + m + 1]).astype(BF16)
        below = jnp.where(jnp.where(totals, stat[j], 0.0) < LIMIT, 1.0, 0.0)
        fine = below if fine is None else jnp.minimum(fine, below)

    @pl.when(jnp.min(fine) < 0.5)
    def _():
        head = begin + pl.program_id(0)
        for n in range(planes * PLANE):
            here = pl.ds(n * rows, rows)
            pltpu.sync_copy(every[n].at[:, pl.ds(pl.multiple_of(head * HD, HD), HD)], key_all.at[here])
            pltpu.sync_copy(
                every[n].at[:, pl.ds(pl.multiple_of((kv_count + head) * HD, HD), HD)], value_all.at[here]
            )

        def one(g, carry):
            cols = pl.ds(pl.multiple_of(g * HD, HD), HD)
            query = q_ref[:, cols]
            x = jnp.where(causal, mm_bt(query, key_all[0:rows, :]) * SCALE2, LOW)
            top = jnp.max(x, axis=1, keepdims=True)
            probs = jnp.exp2(x - top)
            total = jnp.sum(probs, axis=1, keepdims=True)
            summed = mm(probs.astype(BF16), value_all[0:rows, :])

            def more(n, sums):
                top, total, summed = sums
                here = pl.ds(pl.multiple_of(n * rows, rows), rows)
                near = jnp.where(n == 1, core_of(pos), x_of(pos)) == 1
                seen = jnp.where(n < PLANE, near, z_of(pos) >= n // PLANE)
                x = jnp.where(seen, mm_bt(query, key_all[here, :]) * SCALE2, LOW)
                high = jnp.maximum(jnp.max(x, axis=1, keepdims=True), top)
                probs = jnp.exp2(x - high)
                keep = jnp.exp2(top - high)
                part = mm(probs.astype(BF16), value_all[here, :])
                return high, keep * total + jnp.sum(probs, axis=1, keepdims=True), keep * summed + part

            top, total, summed = lax.fori_loop(1, planes * PLANE, more, (top, total, summed))
            out_ref[:, cols] = (summed / total).astype(BF16)
            return carry

        lax.fori_loop(0, group, one, 0)


def soft_step(pos, query, blocks, every, state, into, span, kv_count, last, token):
    rows, width = query.shape
    group = width // HD // kv_count
    used, rules = zip(*blocks)
    used = list(used)
    first = rules[0] == "own"
    begin, count = span
    block = pl.BlockSpec((rows, group * HD), lambda k: (0, begin + k))
    quads = group // min(QUAD, group)
    stat = pl.BlockSpec((quads, rows, HD), lambda k: (begin + k, 0, 0))
    keys = pl.BlockSpec((rows, HD), lambda k: (0, begin + k))
    values = pl.BlockSpec((rows, HD), lambda k: (0, kv_count + begin + k))
    in_specs = [SCALAR, block] + [keys] * len(used) + [values] * len(used)
    operands = [pos, query] + used + used
    aliases = {}
    if not first:
        if not last:
            aliases = {len(operands): 0, len(operands) + 1: 1}
        in_specs += [block, stat]
        operands += list(state)
    in_specs.append(SCALAR)
    operands.append(token)
    rest = [a for a, _ in every] if last else []
    if into is not None:
        for i, a in enumerate(into):
            aliases[len(operands) + len(rest) + i] = i
        rest = rest + list(into)
    in_specs += [ANY] * len(rest)
    operands += rest
    if last:
        out_specs = [block, SCALAR]
        out_shape = [jax.ShapeDtypeStruct((rows, width), BF16), NEXT]
        scratch = [pltpu.VMEM((rows, group * HD), F32), pltpu.VMEM((quads, rows, HD), F32)]
        scratch += [pltpu.VMEM((len(every) * rows, HD), BF16)] * 2
    else:
        out_specs = [block, stat, SCALAR]
        out_shape = [
            jax.ShapeDtypeStruct((rows, width), F32),
            jax.ShapeDtypeStruct((kv_count * quads, rows, HD), F32),
            NEXT,
        ]
        scratch = []
    return pl.pallas_call(
        functools.partial(
            soft_kernel,
            group=group,
            rules=rules,
            planes=len(every) // PLANE,
            last=last,
            passed=1 + len(rest),
            kv_count=kv_count,
            begin=begin,
        ),
        grid=(count,),
        in_specs=in_specs,
        out_specs=out_specs,
        out_shape=out_shape,
        scratch_shapes=scratch,
        input_output_aliases=aliases,
        compiler_params=params(),
        cost_estimate=COST,
        name="softmax",
    )(*operands)


def local(
    light_query,
    light_key,
    light_value,
    log_decay,
    out_gate,
    norm_gain,
    soft_query,
    soft_key,
    soft_value,
    *,
    ctx,
    tp,
):
    rows, heads = log_decay.shape
    qh = heads // 4
    length = qh * HD + TAIL
    planes = ctx // PLANE
    kv_count = soft_key.shape[1] // HD
    place = lax.axis_index("ctx")
    pos = place.astype(jnp.int32).reshape(1)

    def over_core(a):
        return lax.ppermute(a, "ctx", [(i, i ^ 1) for i in range(ctx)])

    def over_x(a):
        return lax.ppermute(a, "ctx", [(i, i ^ 2) for i in range(ctx)])

    def over_z(a, d):
        return lax.ppermute(a, "ctx", [(i, i + PLANE * d) for i in range(ctx - PLANE * d)])

    def after(a, token):
        return lax.optimization_barrier((a, token))[0]

    half = max(kv_count // 2, 1)
    spans = [(0, half), (half, kv_count - half)] if kv_count > 1 else [(0, 1)]
    every = []

    def soft(blocks, state, token, span=None, last=False, into=None):
        for block in blocks:
            if not any(a is block[0] for a, _ in every):
                every.append(block)
        *state, token = soft_step(
            pos, soft_query, blocks, every, state, into, span or (0, kv_count), kv_count, last, token
        )
        return state, token

    def pair(a, rule, token):
        return [(a, rule), (over_core(after(a, token)), rule)]

    paired = jnp.concatenate([soft_key, soft_value], axis=1)
    own = [(paired, "own"), (over_core(paired), "core")]
    beside = over_x(paired)
    same = over_z(paired, 1)

    send, keep, cum, cumt, token = local_state(
        pos, light_key, light_value, after(log_decay.T, own[1][0])
    )
    other = over_core(send)
    quarter = (length, HD)
    both = (2, qh * HD, HD)

    own += pair(beside, "x", own[0][0])
    first, rest = spans[0], spans[1:]
    ahead = over_z(after(same, token), 1)
    beside = over_x(after(same, token))
    state, token = soft(own, None, token, first)
    chip_send, chip_keep, token = small(chip_kernel, pos, [keep, other], [quarter, quarter], qh, "chip", token)
    chip_other = over_x(chip_send)
    for span in rest:
        state, token = soft(own, state, token, span, False, state)
    plane, token = small(plane_kernel, pos, [chip_keep, chip_other], [quarter], qh, "plane", token)
    def hop(before, token):
        out, token = small(step_kernel, pos, [before, plane], [quarter], qh, "step", token)
        return over_z(out, 1), token

    def enter(token):
        send, keep, token = small(
            enter_kernel, pos, [chip_keep, chip_other, before], [quarter, quarter], qh, "enter", token
        )
        return keep, over_x(send), token

    def leave(token):
        send, now, token = small(
            core_kernel, pos, [enter_keep, enter_other, keep, other], [both, both], qh, "core", token
        )
        return now, over_core(send), token

    blocks = pair(same, 1, token) + pair(beside, 1, token)
    if planes == 4 and kv_count == 4:
        one = blocks
        same, beside = ahead, over_x(after(ahead, token))
        ahead = over_z(after(ahead, token), 1)
        state, token = soft(one, state, token, (0, 2))
        before = over_z(after(plane, token), 1)
        two = pair(same, 2, token) + pair(beside, 2, token)
        same, beside = ahead, over_x(after(ahead, token))
        state, token = soft(one + two, state, token, (2, 2))
        before, token = hop(before, token)
        three = pair(same, 3, token) + pair(beside, 3, token)
        soft_out, token = soft(two + three, state, token, (0, 1), True)
        before, token = hop(before, token)
        soft_out, token = soft(two + three, state, token, (1, 1), True, soft_out)
        enter_keep, enter_other, token = enter(token)
        soft_out, token = soft(three, state, token, (2, 1), True, soft_out)
        state_keep, state_other, token = leave(token)
    else:
        before = over_z(plane, 1)
        for d in range(1, planes - 1):
            state, token = soft(blocks, state, token)
            before, token = hop(before, token)
            same, beside = ahead, over_x(after(ahead, token))
            ahead = over_z(after(ahead, token), 1)
            blocks = pair(same, d + 1, token) + pair(beside, d + 1, token)
        enter_keep, enter_other, token = enter(token)
        soft_out, token = soft(blocks, state, token, None, True)
        state_keep, state_other, token = leave(token)
    raw, square, token = light(
        pos, light_query, light_key, light_value, cum, cumt, state_keep, state_other, token
    )
    if planes == 4 and kv_count == 4:
        soft_out, token = soft(three, state, token, (3, 1), True, soft_out)
    squares = [square]
    step = 1
    while step < tp:
        square = sum(squares)
        squares = [square, lax.ppermute(square, "tp", [(i, i ^ step) for i in range(tp)])]
        step *= 2
    light_out = finish(raw, squares, norm_gain, out_gate, heads * HD * tp, token)
    return (light_out, soft_out[0])


def solution(mesh):
    both = P("ctx", "tp")
    return jax.shard_map(
        functools.partial(local, ctx=mesh.shape["ctx"], tp=mesh.shape["tp"]),
        mesh=mesh,
        in_specs=(both, both, both, both, both, P("tp"), both, both, both),
        out_specs=(both, both),
        check_vma=False,
    )
```

```python
import functools
import math

import jax
import jax.numpy as jnp
from jax import lax
from jax.experimental import pallas as pl
from jax.experimental.pallas import tpu as pltpu
from jax.sharding import PartitionSpec as P

HD = 128
EPS = 1e-06
LOW = -1e30
LIMIT = 2.0**100
PLANE = 4
TAIL = 16
VMEM = 32 * 2**20
F32 = jnp.float32
BF16 = jnp.bfloat16
HIGH = lax.Precision.HIGHEST
SCALAR = pl.BlockSpec(memory_space=pltpu.SMEM)
ANY = pl.BlockSpec(memory_space=pl.ANY)
NEXT = jax.ShapeDtypeStruct((1,), jnp.int32)
COST = pl.CostEstimate(flops=1000, bytes_accessed=2**20, transcendentals=0)
SCALE2 = HD ** (-0.5) * math.log2(math.e)


def params(**more):
    return pltpu.CompilerParams(vmem_limit_bytes=VMEM, **more)


def mm(a, b):
    return lax.dot_general(a, b, (((1,), (0,)), ((), ())), preferred_element_type=F32)


def mm_bt(a, b):
    return lax.dot_general(a, b, (((1,), (1,)), ((), ())), preferred_element_type=F32)


def mm_at(a, b):
    return lax.dot_general(a, b, (((0,), (0,)), ((), ())), preferred_element_type=F32)


def z_of(pos):
    return pos[0] // PLANE


def x_of(pos):
    return (pos[0] // 2) % 2


def core_of(pos):
    return pos[0] % 2


def iota(shape, dim):
    return lax.broadcasted_iota(jnp.int32, shape, dim)


def state_kernel(pos, k_ref, v_ref, ld_ref, send_ref, keep_ref, cum_ref, cumt_ref, after, fin, *, qh, heads):
    after[0] = pos[0]
    step = pl.program_id(0)
    rows = ld_ref.shape[1]

    @pl.when(step == 0)
    def _():
        upper = (iota((rows, rows), 0) <= iota((rows, rows), 1)).astype(F32).astype(BF16)
        ld = ld_ref[...]
        high = ld.astype(BF16)
        rest = ld - high.astype(F32)
        middle = rest.astype(BF16)
        low = (rest - middle.astype(F32)).astype(BF16)
        cumt = mm(high, upper) + (mm(middle, upper) + mm(low, upper))
        full = jnp.concatenate([cumt, jnp.zeros((HD - heads, rows), F32)], axis=0)
        cum = jnp.transpose(full)
        ends = jnp.broadcast_to(cumt[:, rows - 1 : rows], (heads, HD))
        fin[...] = jnp.zeros_like(fin)
        cumt_ref[...] = jnp.zeros_like(cumt_ref)
        cum_ref[...] = jnp.zeros_like(cum_ref)
        for i in range(4):
            cum_ref[i, :, 0:qh] = cum[:, i * qh : (i + 1) * qh]
            cumt_ref[i, 0:qh, :] = cumt[i * qh : (i + 1) * qh, :]
            fin[i, 0:qh, :] = ends[i * qh : (i + 1) * qh, :]

    core = pos[0] & 1
    kept = step // 2
    part = step % 2
    quarter = part * 2 + jnp.where(kept == 1, core, 1 - core)
    cum = cum_ref[quarter]
    weight = jnp.exp(cum[rows - 1 : rows, :] - cum)
    tail = fin[quarter]
    high = tail.astype(BF16).astype(F32)
    tail = jnp.concatenate([high, tail - high], axis=0).astype(BF16)
    states = []
    for i in range(qh):
        cols = slice(i * HD, (i + 1) * HD)
        keyed = (k_ref[:, cols].astype(F32) * weight[:, i : i + 1]).astype(BF16)
        states.append(mm_at(keyed, v_ref[:, cols]).astype(BF16))

    def put(ref):
        for i in range(qh):
            ref[part, i * HD : (i + 1) * HD, :] = states[i]
        ref[part, qh * HD : qh * HD + TAIL, :] = tail

    @pl.when(kept == 0)
    def _():
        put(send_ref)

    @pl.when(kept == 1)
    def _():
        put(keep_ref)


def local_state(pos, key, value, log_decay):
    heads, rows = log_decay.shape
    qh = heads // 4
    length = qh * HD + TAIL

    def columns(step, pos):
        core = pos[0] & 1
        return (0, (step % 2) * 2 + jnp.where(step // 2 == 1, core, 1 - core))

    whole = lambda *shape: pl.BlockSpec(shape, lambda step, pos: (0,) * len(shape))
    return pl.pallas_call(
        functools.partial(state_kernel, qh=qh, heads=heads),
        grid_spec=pltpu.PrefetchScalarGridSpec(
            num_scalar_prefetch=1,
            grid=(4,),
            in_specs=[
                pl.BlockSpec((rows, qh * HD), columns),
                pl.BlockSpec((rows, qh * HD), columns),
                whole(heads, rows),
            ],
            out_specs=[
                whole(2, length, HD),
                whole(2, length, HD),
                whole(4, rows, HD),
                whole(4, 8, rows),
                SCALAR,
            ],
            scratch_shapes=[pltpu.VMEM((4, 8, HD), F32)],
        ),
        out_shape=[
            jax.ShapeDtypeStruct((2, length, HD), BF16),
            jax.ShapeDtypeStruct((2, length, HD), BF16),
            jax.ShapeDtypeStruct((4, rows, HD), F32),
            jax.ShapeDtypeStruct((4, 8, rows), F32),
            NEXT,
        ],
        compiler_params=params(),
        cost_estimate=COST,
        name="local_state",
    )(pos, key, value, log_decay)


def spread(item, qh):
    tail = item[qh * HD : qh * HD + TAIL, :].astype(F32)
    return item[0 : qh * HD, :].astype(F32), tail[0:8, :] + tail[8:16, :]


def pack(states, logs):
    high = logs.astype(BF16).astype(F32)
    return states.astype(BF16), jnp.concatenate([high, logs - high], axis=0).astype(BF16)


def decay(states, logs, qh):
    factor = jnp.exp(logs)
    return jnp.concatenate(
        [states[i * HD : (i + 1) * HD, :] * factor[i : i + 1, :] for i in range(qh)], axis=0
    )


def joined(early, late, qh):
    return decay(early[0], late[1], qh) + late[0], early[1] + late[1]


def store(ref, item, qh):
    states, tail = pack(*item)
    ref[0 : qh * HD, :] = states
    ref[qh * HD : qh * HD + TAIL, :] = tail


def chip_kernel(pos, keep_ref, recv_ref, send_out, keep_out, *, qh):
    first = core_of(pos) == 0
    for out, part in ((send_out, 1 - x_of(pos)), (keep_out, x_of(pos))):
        own, other = keep_ref[part], recv_ref[part]
        early = spread(jnp.where(first, own, other), qh)
        late = spread(jnp.where(first, other, own), qh)
        store(out, joined(early, late, qh), qh)


def plane_kernel(pos, keep_ref, recv_ref, out, *, qh):
    first = x_of(pos) == 0
    own, other = keep_ref[...], recv_ref[...]
    early = spread(jnp.where(first, own, other), qh)
    late = spread(jnp.where(first, other, own), qh)
    store(out, joined(early, late, qh), qh)


def enter_kernel(pos, keep_ref, recv_ref, *refs, qh):
    planes, (send_out, keep_out) = refs[:-2], refs[-2:]
    total = None
    for ref in reversed(planes):
        item = spread(ref[...], qh)
        total = item if total is None else joined(total, item, qh)
    first = x_of(pos) == 0
    early = spread(jnp.where(first, keep_ref[...], recv_ref[...]), qh)
    if total is None:
        total = (jnp.zeros_like(early[0]), jnp.zeros_like(early[1]))
    later = joined(total, early, qh)
    zero, one = pack(*total), pack(*later)
    for out, take in ((send_out, first), (keep_out, jnp.logical_not(first))):
        out[0 : qh * HD, :] = jnp.where(take, one[0], zero[0])
        out[qh * HD : qh * HD + TAIL, :] = jnp.where(take, one[1], zero[1])


def core_kernel(pos, enter_keep, enter_recv, keep_ref, recv_ref, send_out, keep_out, *, qh):
    first = core_of(pos) == 0
    for part in range(2):
        entering = spread(jnp.where(x_of(pos) == part, enter_keep[...], enter_recv[...]), qh)
        own = spread(jnp.where(first, keep_ref[part], recv_ref[part]), qh)
        later = joined(entering, own, qh)[0].astype(BF16)
        now = entering[0].astype(BF16)
        send_out[part] = jnp.where(first, later, now)
        keep_out[part] = jnp.where(first, now, later)


def with_token(kernel, pos, token, *refs):
    refs[-1][0] = token[0]
    kernel(pos, *refs[:-1])


def small(kernel, pos, arrays, outs, qh, name, token):
    return pl.pallas_call(
        functools.partial(with_token, functools.partial(kernel, qh=qh)),
        in_specs=[SCALAR, SCALAR] + [pl.BlockSpec(memory_space=pltpu.VMEM)] * len(arrays),
        out_specs=[pl.BlockSpec(memory_space=pltpu.VMEM)] * len(outs) + [SCALAR],
        out_shape=[jax.ShapeDtypeStruct(s, BF16) for s in outs] + [NEXT],
        compiler_params=pltpu.CompilerParams(vmem_limit_bytes=24 * 2**20),
        cost_estimate=COST,
        name=name,
    )(pos, token, *arrays)


def light_kernel(pos, q_ref, k_ref, v_ref, cum_ref, cumt_ref, keep_ref, recv_ref, token, out_ref, ss_ref, after, *, qh):
    after[0] = token[0]
    rows = q_ref.shape[0]
    quarter = pl.program_id(0)
    part = quarter // 2
    mine = quarter % 2 == core_of(pos)
    causal = iota((rows, rows), 0) >= iota((rows, rows), 1)
    cum, cumt = cum_ref[0], cumt_ref[0]
    factor = jnp.exp(cum)
    state = jnp.where(mine, keep_ref[part], recv_ref[part])
    total = jnp.zeros((rows, HD), F32)
    for i in range(qh):
        cols = slice(i * HD, (i + 1) * HD)
        query = q_ref[:, cols]
        scores = mm_bt(query, k_ref[:, cols])
        gap = jnp.where(causal, cum[:, i : i + 1] - cumt[i : i + 1, :], LOW)
        weights = (scores * jnp.exp(gap)).astype(BF16)
        carried = mm(query, state[i * HD : (i + 1) * HD, :])
        raw = mm(weights, v_ref[:, cols]) + factor[:, i : i + 1] * carried
        out_ref[:, cols] = raw.astype(BF16)
        total = total + raw * raw

    @pl.when(quarter == 0)
    def _():
        ss_ref[...] = total

    @pl.when(quarter > 0)
    def _():
        ss_ref[...] += total


def light(pos, query, key, value, cum, cumt, keep, recv, token):
    rows, width = query.shape
    wide = width // 4
    block = pl.BlockSpec((rows, wide), lambda i: (0, i))
    whole = pl.BlockSpec(keep.shape, lambda i: (0, 0, 0))
    return pl.pallas_call(
        functools.partial(light_kernel, qh=wide // HD),
        grid=(4,),
        in_specs=[
            SCALAR,
            block,
            block,
            block,
            pl.BlockSpec((1, rows, HD), lambda i: (i, 0, 0)),
            pl.BlockSpec((1, 8, rows), lambda i: (i, 0, 0)),
            whole,
            whole,
            SCALAR,
        ],
        out_specs=[block, pl.BlockSpec((rows, HD), lambda i: (0, 0)), SCALAR],
        out_shape=[jax.ShapeDtypeStruct((rows, width), BF16), jax.ShapeDtypeStruct((rows, HD), F32), NEXT],
        compiler_params=params(),
        cost_estimate=COST,
        name="light",
    )(pos, query, key, value, cum, cumt, keep, recv, token)


def finish_kernel(raw_ref, *refs, features):
    squares, (gain_ref, gate_ref, token, out_ref, factor) = refs[:-5], refs[-5:]

    @pl.when(pl.program_id(0) == 0)
    def _():
        square = squares[0][...]
        for more in squares[1:]:
            square = square + more[...]
        mean = jnp.sum(square, axis=1, keepdims=True) / features
        factor[...] = jnp.broadcast_to(lax.rsqrt(mean + EPS), factor.shape)

    for i in range(out_ref.shape[1] // HD):
        cols = slice(i * HD, (i + 1) * HD)
        gate = 0.5 * jnp.tanh(0.5 * gate_ref[:, cols].astype(F32)) + 0.5
        raw = raw_ref[:, cols].astype(F32)
        out_ref[:, cols] = (raw * factor[...] * gain_ref[:, cols] * gate).astype(BF16)


def finish(raw, squares, gain, gate, features, token):
    rows, width = raw.shape
    wide = width // 4
    block = pl.BlockSpec((rows, wide), lambda i: (0, i))
    return pl.pallas_call(
        functools.partial(finish_kernel, features=features),
        grid=(4,),
        in_specs=[block]
        + [pl.BlockSpec((rows, HD), lambda i: (0, 0))] * len(squares)
        + [pl.BlockSpec((1, wide), lambda i: (0, i)), block, SCALAR],
        out_specs=block,
        out_shape=jax.ShapeDtypeStruct((rows, width), BF16),
        scratch_shapes=[pltpu.VMEM((rows, HD), F32)],
        compiler_params=params(),
        cost_estimate=COST,
        name="finish",
    )(raw, *squares, gain.reshape(1, width), gate, token)


def soft_kernel(pos, q_ref, *refs, group, distances, planes, last, passed, kv_count, begin):
    pair = min(2, group)
    count = len(distances) * PLANE
    keys, values, refs = refs[:count], refs[count : 2 * count], refs[2 * count :]
    first = distances[0] == 0
    if not first:
        acc_in, stat_in, refs = refs[0], refs[1], refs[2:]
    token, every, refs = refs[0], refs[1:passed], refs[passed:]
    if last:
        out_ref, after, acc, stat, key_all, value_all = refs
    else:
        acc, stat, after = refs
        stat = stat.at[0]
    after[0] = token[0]
    rows = q_ref.shape[0]
    lane = iota((rows, HD), 1)
    causal = iota((rows, rows), 0) >= iota((rows, rows), 1)
    flags = [None, x_of(pos) == 1, core_of(pos) == 1, x_of(pos) == 1]

    if not first:
        acc[...] = acc_in[...]
        stat[...] = stat_in[0]

    def attend(keyed, valued, fresh):
        wide = jnp.concatenate([v[...] for v in valued], axis=0)
        wide = jnp.concatenate([wide, jnp.ones_like(wide)], axis=1)
        keyed = [k[...] for k in keyed]
        if fresh:
            own = keyed[0].astype(F32)
            shifts = [
                jnp.sum(q_ref[:, g * HD : (g + 1) * HD].astype(F32) * own, axis=1, keepdims=True)
                for g in range(group)
            ]
        else:
            shifts = [stat[:, g : g + 1] for g in range(group)]
        hidden = [0.0] + [
            jnp.where(flags[n], 0.0, LOW).astype(F32) if fresh else 0.0 for n in range(1, len(keyed))
        ]
        def scored(i):
            parts = []
            for g in range(i, i + pair):
                query = q_ref[:, g * HD : (g + 1) * HD]
                parts.append(query)
            query = jnp.concatenate(parts, axis=0)
            return [mm_bt(query, k) for k in keyed]

        scores = scored(0)
        for i in range(0, group, pair):
            ahead = scored(i + pair) if i + pair < group else None
            shift = jnp.concatenate(shifts[i : i + pair], axis=0) * SCALE2
            probs = []
            for n, s in enumerate(scores):
                x = s * SCALE2 - (shift - hidden[n])
                if fresh and n == 0:
                    x = jnp.concatenate(
                        [jnp.where(causal, x[m * rows : (m + 1) * rows], LOW) for m in range(pair)], axis=0
                    )
                probs.append(jnp.exp2(x).astype(BF16))
            out = mm(jnp.concatenate(probs, axis=1), wide)
            for n in range(pair):
                g = i + n
                cols = slice(g * HD, (g + 1) * HD)
                band = slice(n * rows, (n + 1) * rows)
                summed, total = out[band, :HD], out[band, HD:]
                if fresh:
                    acc[:, cols] = summed
                    old = jnp.where(lane == g, shifts[g], 0.0 if g == 0 else stat[...])
                    stat[...] = jnp.where(lane == group + g, total, old)
                else:
                    acc[:, cols] += summed
                    stat[...] += jnp.where(lane == group + g, total, 0.0)
            scores = ahead

    for n, distance in enumerate(distances):
        here = slice(n * PLANE, (n + 1) * PLANE)
        if distance == 0:
            attend(keys[here], values[here], True)
        else:
            pl.when(z_of(pos) >= distance)(functools.partial(attend, keys[here], values[here], False))
    if not last:
        return
    totals = (lane >= group) & (lane < 2 * group)
    inverse = 1.0 / jnp.where(totals, stat[...], 1.0)
    for g in range(group):
        cols = slice(g * HD, (g + 1) * HD)
        out_ref[:, cols] = (acc[:, cols] * inverse[:, group + g : group + g + 1]).astype(BF16)

    sums = jnp.where(totals, stat[...], 0.0)
    fine = jnp.min(jnp.where(sums < LIMIT, 1.0, 0.0))

    @pl.when(fine < 0.5)
    def _():
        head = begin + pl.program_id(0)
        for n in range(planes * PLANE):
            here = pl.ds(n * rows, rows)
            pltpu.sync_copy(every[n].at[:, pl.ds(pl.multiple_of(head * HD, HD), HD)], key_all.at[here])
            pltpu.sync_copy(
                every[n].at[:, pl.ds(pl.multiple_of((kv_count + head) * HD, HD), HD)], value_all.at[here]
            )

        def one(g, carry):
            cols = pl.ds(pl.multiple_of(g * HD, HD), HD)
            query = q_ref[:, cols]
            x = jnp.where(causal, mm_bt(query, key_all[0:rows, :]) * SCALE2, LOW)
            top = jnp.max(x, axis=1, keepdims=True)
            probs = jnp.exp2(x - top)
            total = jnp.sum(probs, axis=1, keepdims=True)
            summed = mm(probs.astype(BF16), value_all[0:rows, :])

            def more(n, sums):
                top, total, summed = sums
                here = pl.ds(pl.multiple_of(n * rows, rows), rows)
                near = jnp.where(n == 2, core_of(pos), x_of(pos)) == 1
                seen = jnp.where(n < PLANE, near, z_of(pos) >= n // PLANE)
                x = jnp.where(seen, mm_bt(query, key_all[here, :]) * SCALE2, LOW)
                high = jnp.maximum(jnp.max(x, axis=1, keepdims=True), top)
                probs = jnp.exp2(x - high)
                keep = jnp.exp2(top - high)
                part = mm(probs.astype(BF16), value_all[here, :])
                return high, keep * total + jnp.sum(probs, axis=1, keepdims=True), keep * summed + part

            top, total, summed = lax.fori_loop(1, planes * PLANE, more, (top, total, summed))
            out_ref[:, cols] = (summed / total).astype(BF16)
            return carry

        lax.fori_loop(0, group, one, 0)


def soft_step(pos, query, pieces, distances, state, into, span, kv_count, planes, last, token):
    rows, width = query.shape
    group = width // HD // kv_count
    first = distances[0] == 0
    begin, count = span
    block = pl.BlockSpec((rows, group * HD), lambda k: (0, begin + k))
    stat = pl.BlockSpec((1, rows, HD), lambda k: (begin + k, 0, 0))
    keys = pl.BlockSpec((rows, HD), lambda k: (0, begin + k))
    values = pl.BlockSpec((rows, HD), lambda k: (0, kv_count + begin + k))
    used = [a for d in distances for a in pieces[d]]
    in_specs = [SCALAR, block] + [keys] * len(used) + [values] * len(used)
    operands = [pos, query] + used + used
    aliases = {}
    if not first:
        if not last:
            aliases = {len(operands): 0, len(operands) + 1: 1}
        in_specs += [block, stat]
        operands += list(state)
    in_specs.append(SCALAR)
    operands.append(token)
    rest = [a for d in range(planes) for a in pieces[d]] if last else []
    if into is not None:
        for i, a in enumerate(into):
            aliases[len(operands) + len(rest) + i] = i
        rest = rest + list(into)
    in_specs += [ANY] * len(rest)
    operands += rest
    if last:
        out_specs = [block, SCALAR]
        out_shape = [jax.ShapeDtypeStruct((rows, width), BF16), NEXT]
        scratch = [pltpu.VMEM((rows, group * HD), F32), pltpu.VMEM((rows, HD), F32)]
        scratch += [pltpu.VMEM((planes * PLANE * rows, HD), BF16)] * 2
    else:
        out_specs = [block, stat, SCALAR]
        out_shape = [
            jax.ShapeDtypeStruct((rows, width), F32),
            jax.ShapeDtypeStruct((kv_count, rows, HD), F32),
            NEXT,
        ]
        scratch = []
    return pl.pallas_call(
        functools.partial(
            soft_kernel,
            group=group,
            distances=distances,
            planes=planes,
            last=last,
            passed=1 + len(rest),
            kv_count=kv_count,
            begin=begin,
        ),
        grid=(count,),
        in_specs=in_specs,
        out_specs=out_specs,
        out_shape=out_shape,
        scratch_shapes=scratch,
        input_output_aliases=aliases,
        compiler_params=params(),
        cost_estimate=COST,
        name="softmax",
    )(*operands)


def local(
    light_query,
    light_key,
    light_value,
    log_decay,
    out_gate,
    norm_gain,
    soft_query,
    soft_key,
    soft_value,
    *,
    ctx,
    tp,
):
    rows, heads = log_decay.shape
    qh = heads // 4
    length = qh * HD + TAIL
    planes = ctx // PLANE
    kv_count = soft_key.shape[1] // HD
    place = lax.axis_index("ctx")
    pos = place.astype(jnp.int32).reshape(1)

    def over_core(a):
        return lax.ppermute(a, "ctx", [(i, i ^ 1) for i in range(ctx)])

    def over_x(a):
        return lax.ppermute(a, "ctx", [(i, i ^ 2) for i in range(ctx)])

    def over_z(a, d):
        return lax.ppermute(a, "ctx", [(i, i + PLANE * d) for i in range(ctx - PLANE * d)])

    def after(a, token):
        return lax.optimization_barrier((a, token))[0]

    paired = jnp.concatenate([soft_key, soft_value], axis=1)
    crossed = over_x(paired)
    arrived = [paired, over_z(paired, 1)]

    def forward(token):
        arrived.append(over_z(after(arrived[-1], token), 1))

    pieces = [[paired, crossed, over_core(paired), over_core(crossed)]]

    half = max(kv_count // 2, 1)
    spans = [(0, half), (half, kv_count - half)] if kv_count > 1 else [(0, 1)]

    def soft(distances, state, last, token, span=None, into=None):
        *state, token = soft_step(
            pos, soft_query, pieces, distances, state, into, span or (0, kv_count), kv_count, planes, last, token
        )
        return state, token

    send, keep, cum, cumt, token = local_state(
        pos, light_key, light_value, after(log_decay.T, pieces[0][2])
    )
    other = over_core(send)
    quarter = (length, HD)

    def cross(d, token):
        a = after(arrived[d], token)
        pieces.append([a, over_x(a)])

    def spread_core(d, token):
        pieces[d] += [over_core(after(a, token)) for a in pieces[d]]

    cross(1, token)
    forward(token)
    state, token = soft((0,), None, False, token, spans[0])
    chip_send, chip_keep, token = small(chip_kernel, pos, [keep, other], [quarter, quarter], qh, "chip", token)
    chip_other = over_x(chip_send)
    cross(2, token)
    forward(token)
    if len(spans) > 1:
        state, token = soft((0,), None, False, token, spans[1], state)
    plane, token = small(plane_kernel, pos, [chip_keep, chip_other], [quarter], qh, "plane", token)
    earlier = [over_z(plane, d) for d in range(1, planes)]
    spread_core(1, token)
    spread_core(2, token)
    cross(3, token)
    for d in range(3, planes - 1):
        forward(token)
        cross(d + 1, token)
    both = (2, qh * HD, HD)
    rest = (planes - 1,)
    for middle in [(1, 2)] + [(d,) for d in range(3, planes - 1)]:
        for n, span in enumerate(spans):
            state, token = soft(middle, state, False, token, span)
            if n == 0:
                spread_core(middle[-1] + 1, token)
    enter_send, enter_keep, token = small(
        enter_kernel, pos, [chip_keep, chip_other] + earlier, [quarter, quarter], qh, "enter", token
    )
    enter_other = over_x(enter_send)
    soft_out, token = soft(rest, state, True, token, spans[0])
    state_send, state_keep, token = small(
        core_kernel, pos, [enter_keep, enter_other, keep, other], [both, both], qh, "core", token
    )
    state_other = over_core(state_send)
    raw, square, token = light(
        pos, light_query, light_key, light_value, cum, cumt, state_keep, state_other, token
    )
    for span in spans[1:]:
        soft_out, token = soft(rest, state, True, token, span, soft_out)
    squares = [square]
    step = 1
    while step < tp:
        square = sum(squares)
        squares = [square, lax.ppermute(square, "tp", [(i, i ^ step) for i in range(tp)])]
        step *= 2
    light_out = finish(raw, squares, norm_gain, out_gate, heads * HD * tp, token)
    return (light_out, soft_out[0])


def solution(mesh):
    both = P("ctx", "tp")
    return jax.shard_map(
        functools.partial(local, ctx=mesh.shape["ctx"], tp=mesh.shape["tp"]),
        mesh=mesh,
        in_specs=(both, both, both, both, both, P("tp"), both, both, both),
        out_specs=(both, both),
        check_vma=False,
    )
```

```python
import functools
import math

import jax
import jax.numpy as jnp
from jax import lax
from jax.experimental import pallas as pl
from jax.experimental.pallas import tpu as pltpu
from jax.sharding import PartitionSpec as P

HD = 128
EPS = 1e-06
LOW = -1e30
LIMIT = 2.0**100
PLANE = 4
TAIL = 16
VMEM = 32 * 2**20
F32 = jnp.float32
BF16 = jnp.bfloat16
HIGH = lax.Precision.HIGHEST
SCALAR = pl.BlockSpec(memory_space=pltpu.SMEM)
ANY = pl.BlockSpec(memory_space=pl.ANY)
NEXT = jax.ShapeDtypeStruct((1,), jnp.int32)
COST = pl.CostEstimate(flops=1000, bytes_accessed=2**20, transcendentals=0)
SCALE2 = HD ** (-0.5) * math.log2(math.e)


def params(**more):
    return pltpu.CompilerParams(vmem_limit_bytes=VMEM, **more)


def mm(a, b):
    return lax.dot_general(a, b, (((1,), (0,)), ((), ())), preferred_element_type=F32)


def mm_bt(a, b):
    return lax.dot_general(a, b, (((1,), (1,)), ((), ())), preferred_element_type=F32)


def mm_at(a, b):
    return lax.dot_general(a, b, (((0,), (0,)), ((), ())), preferred_element_type=F32)


def z_of(pos):
    return pos[0] // PLANE


def x_of(pos):
    return (pos[0] // 2) % 2


def core_of(pos):
    return pos[0] % 2


def iota(shape, dim):
    return lax.broadcasted_iota(jnp.int32, shape, dim)


def state_kernel(pos, k_ref, v_ref, ld_ref, send_ref, keep_ref, cum_ref, cumt_ref, after, fin, *, qh, heads):
    after[0] = pos[0]
    step = pl.program_id(0)
    rows = ld_ref.shape[1]

    @pl.when(step == 0)
    def _():
        upper = (iota((rows, rows), 0) <= iota((rows, rows), 1)).astype(F32).astype(BF16)
        ld = ld_ref[...]
        high = ld.astype(BF16)
        rest = ld - high.astype(F32)
        middle = rest.astype(BF16)
        low = (rest - middle.astype(F32)).astype(BF16)
        cumt = mm(high, upper) + (mm(middle, upper) + mm(low, upper))
        full = jnp.concatenate([cumt, jnp.zeros((HD - heads, rows), F32)], axis=0)
        cum = jnp.transpose(full)
        ends = jnp.broadcast_to(cumt[:, rows - 1 : rows], (heads, HD))
        fin[...] = jnp.zeros_like(fin)
        cumt_ref[...] = jnp.zeros_like(cumt_ref)
        cum_ref[...] = jnp.zeros_like(cum_ref)
        for i in range(4):
            cum_ref[i, :, 0:qh] = cum[:, i * qh : (i + 1) * qh]
            cumt_ref[i, 0:qh, :] = cumt[i * qh : (i + 1) * qh, :]
            fin[i, 0:qh, :] = ends[i * qh : (i + 1) * qh, :]

    core = pos[0] & 1
    kept = step // 2
    part = step % 2
    quarter = part * 2 + jnp.where(kept == 1, core, 1 - core)
    cum = cum_ref[quarter]
    weight = jnp.exp(cum[rows - 1 : rows, :] - cum)
    tail = fin[quarter]
    high = tail.astype(BF16).astype(F32)
    tail = jnp.concatenate([high, tail - high], axis=0).astype(BF16)
    states = []
    for i in range(qh):
        cols = slice(i * HD, (i + 1) * HD)
        keyed = (k_ref[:, cols].astype(F32) * weight[:, i : i + 1]).astype(BF16)
        states.append(mm_at(keyed, v_ref[:, cols]).astype(BF16))

    def put(ref):
        for i in range(qh):
            ref[part, i * HD : (i + 1) * HD, :] = states[i]
        ref[part, qh * HD : qh * HD + TAIL, :] = tail

    @pl.when(kept == 0)
    def _():
        put(send_ref)

    @pl.when(kept == 1)
    def _():
        put(keep_ref)


def local_state(pos, key, value, log_decay):
    heads, rows = log_decay.shape
    qh = heads // 4
    length = qh * HD + TAIL

    def columns(step, pos):
        core = pos[0] & 1
        return (0, (step % 2) * 2 + jnp.where(step // 2 == 1, core, 1 - core))

    whole = lambda *shape: pl.BlockSpec(shape, lambda step, pos: (0,) * len(shape))
    return pl.pallas_call(
        functools.partial(state_kernel, qh=qh, heads=heads),
        grid_spec=pltpu.PrefetchScalarGridSpec(
            num_scalar_prefetch=1,
            grid=(4,),
            in_specs=[
                pl.BlockSpec((rows, qh * HD), columns),
                pl.BlockSpec((rows, qh * HD), columns),
                whole(heads, rows),
            ],
            out_specs=[
                whole(2, length, HD),
                whole(2, length, HD),
                whole(4, rows, HD),
                whole(4, 8, rows),
                SCALAR,
            ],
            scratch_shapes=[pltpu.VMEM((4, 8, HD), F32)],
        ),
        out_shape=[
            jax.ShapeDtypeStruct((2, length, HD), BF16),
            jax.ShapeDtypeStruct((2, length, HD), BF16),
            jax.ShapeDtypeStruct((4, rows, HD), F32),
            jax.ShapeDtypeStruct((4, 8, rows), F32),
            NEXT,
        ],
        compiler_params=params(),
        cost_estimate=COST,
        name="local_state",
    )(pos, key, value, log_decay)


def spread(item, qh):
    tail = item[qh * HD : qh * HD + TAIL, :].astype(F32)
    return item[0 : qh * HD, :].astype(F32), tail[0:8, :] + tail[8:16, :]


def pack(states, logs):
    high = logs.astype(BF16).astype(F32)
    return states.astype(BF16), jnp.concatenate([high, logs - high], axis=0).astype(BF16)


def decay(states, logs, qh):
    factor = jnp.exp(logs)
    return jnp.concatenate(
        [states[i * HD : (i + 1) * HD, :] * factor[i : i + 1, :] for i in range(qh)], axis=0
    )


def joined(early, late, qh):
    return decay(early[0], late[1], qh) + late[0], early[1] + late[1]


def store(ref, item, qh):
    states, tail = pack(*item)
    ref[0 : qh * HD, :] = states
    ref[qh * HD : qh * HD + TAIL, :] = tail


def chip_kernel(pos, keep_ref, recv_ref, send_out, keep_out, *, qh):
    first = core_of(pos) == 0
    for out, part in ((send_out, 1 - x_of(pos)), (keep_out, x_of(pos))):
        own, other = keep_ref[part], recv_ref[part]
        early = spread(jnp.where(first, own, other), qh)
        late = spread(jnp.where(first, other, own), qh)
        store(out, joined(early, late, qh), qh)


def plane_kernel(pos, keep_ref, recv_ref, out, *, qh):
    first = x_of(pos) == 0
    own, other = keep_ref[...], recv_ref[...]
    early = spread(jnp.where(first, own, other), qh)
    late = spread(jnp.where(first, other, own), qh)
    store(out, joined(early, late, qh), qh)


def enter_kernel(pos, keep_ref, recv_ref, *refs, qh):
    planes, (send_out, keep_out) = refs[:-2], refs[-2:]
    total = None
    for ref in reversed(planes):
        item = spread(ref[...], qh)
        total = item if total is None else joined(total, item, qh)
    first = x_of(pos) == 0
    early = spread(jnp.where(first, keep_ref[...], recv_ref[...]), qh)
    if total is None:
        total = (jnp.zeros_like(early[0]), jnp.zeros_like(early[1]))
    later = joined(total, early, qh)
    zero, one = pack(*total), pack(*later)
    for out, take in ((send_out, first), (keep_out, jnp.logical_not(first))):
        out[0 : qh * HD, :] = jnp.where(take, one[0], zero[0])
        out[qh * HD : qh * HD + TAIL, :] = jnp.where(take, one[1], zero[1])


def core_kernel(pos, enter_keep, enter_recv, keep_ref, recv_ref, send_out, keep_out, *, qh):
    first = core_of(pos) == 0
    for part in range(2):
        entering = spread(jnp.where(x_of(pos) == part, enter_keep[...], enter_recv[...]), qh)
        own = spread(jnp.where(first, keep_ref[part], recv_ref[part]), qh)
        later = joined(entering, own, qh)[0].astype(BF16)
        now = entering[0].astype(BF16)
        send_out[part] = jnp.where(first, later, now)
        keep_out[part] = jnp.where(first, now, later)


def with_token(kernel, pos, token, *refs):
    refs[-1][0] = token[0]
    kernel(pos, *refs[:-1])


def small(kernel, pos, arrays, outs, qh, name, token):
    return pl.pallas_call(
        functools.partial(with_token, functools.partial(kernel, qh=qh)),
        in_specs=[SCALAR, SCALAR] + [pl.BlockSpec(memory_space=pltpu.VMEM)] * len(arrays),
        out_specs=[pl.BlockSpec(memory_space=pltpu.VMEM)] * len(outs) + [SCALAR],
        out_shape=[jax.ShapeDtypeStruct(s, BF16) for s in outs] + [NEXT],
        compiler_params=pltpu.CompilerParams(vmem_limit_bytes=24 * 2**20),
        cost_estimate=COST,
        name=name,
    )(pos, token, *arrays)


def light_kernel(pos, q_ref, k_ref, v_ref, cum_ref, cumt_ref, keep_ref, recv_ref, token, out_ref, ss_ref, after, *, qh):
    after[0] = token[0]
    rows = q_ref.shape[0]
    quarter = pl.program_id(0)
    part = quarter // 2
    mine = quarter % 2 == core_of(pos)
    causal = iota((rows, rows), 0) >= iota((rows, rows), 1)
    cum, cumt = cum_ref[0], cumt_ref[0]
    factor = jnp.exp(cum)
    state = jnp.where(mine, keep_ref[part], recv_ref[part])
    total = jnp.zeros((rows, HD), F32)
    for i in range(qh):
        cols = slice(i * HD, (i + 1) * HD)
        query = q_ref[:, cols]
        scores = mm_bt(query, k_ref[:, cols])
        gap = jnp.where(causal, cum[:, i : i + 1] - cumt[i : i + 1, :], LOW)
        weights = (scores * jnp.exp(gap)).astype(BF16)
        carried = mm(query, state[i * HD : (i + 1) * HD, :])
        raw = mm(weights, v_ref[:, cols]) + factor[:, i : i + 1] * carried
        out_ref[:, cols] = raw.astype(BF16)
        total = total + raw * raw

    @pl.when(quarter == 0)
    def _():
        ss_ref[...] = total

    @pl.when(quarter > 0)
    def _():
        ss_ref[...] += total


def light(pos, query, key, value, cum, cumt, keep, recv, token):
    rows, width = query.shape
    wide = width // 4
    block = pl.BlockSpec((rows, wide), lambda i: (0, i))
    whole = pl.BlockSpec(keep.shape, lambda i: (0, 0, 0))
    return pl.pallas_call(
        functools.partial(light_kernel, qh=wide // HD),
        grid=(4,),
        in_specs=[
            SCALAR,
            block,
            block,
            block,
            pl.BlockSpec((1, rows, HD), lambda i: (i, 0, 0)),
            pl.BlockSpec((1, 8, rows), lambda i: (i, 0, 0)),
            whole,
            whole,
            SCALAR,
        ],
        out_specs=[block, pl.BlockSpec((rows, HD), lambda i: (0, 0)), SCALAR],
        out_shape=[jax.ShapeDtypeStruct((rows, width), BF16), jax.ShapeDtypeStruct((rows, HD), F32), NEXT],
        compiler_params=params(),
        cost_estimate=COST,
        name="light",
    )(pos, query, key, value, cum, cumt, keep, recv, token)


def finish_kernel(raw_ref, *refs, features):
    squares, (gain_ref, gate_ref, token, out_ref, factor) = refs[:-5], refs[-5:]

    @pl.when(pl.program_id(0) == 0)
    def _():
        square = squares[0][...]
        for more in squares[1:]:
            square = square + more[...]
        mean = jnp.sum(square, axis=1, keepdims=True) / features
        factor[...] = jnp.broadcast_to(lax.rsqrt(mean + EPS), factor.shape)

    for i in range(out_ref.shape[1] // HD):
        cols = slice(i * HD, (i + 1) * HD)
        gate = 0.5 * jnp.tanh(0.5 * gate_ref[:, cols].astype(F32)) + 0.5
        raw = raw_ref[:, cols].astype(F32)
        out_ref[:, cols] = (raw * factor[...] * gain_ref[:, cols] * gate).astype(BF16)


def finish(raw, squares, gain, gate, features, token):
    rows, width = raw.shape
    wide = width // 4
    block = pl.BlockSpec((rows, wide), lambda i: (0, i))
    return pl.pallas_call(
        functools.partial(finish_kernel, features=features),
        grid=(4,),
        in_specs=[block]
        + [pl.BlockSpec((rows, HD), lambda i: (0, 0))] * len(squares)
        + [pl.BlockSpec((1, wide), lambda i: (0, i)), block, SCALAR],
        out_specs=block,
        out_shape=jax.ShapeDtypeStruct((rows, width), BF16),
        scratch_shapes=[pltpu.VMEM((rows, HD), F32)],
        compiler_params=params(),
        cost_estimate=COST,
        name="finish",
    )(raw, *squares, gain.reshape(1, width), gate, token)


def soft_kernel(pos, q_ref, *refs, group, distances, planes, last, passed, kv_count, begin):
    pair = min(2, group)
    count = len(distances) * PLANE
    keys, values, refs = refs[:count], refs[count : 2 * count], refs[2 * count :]
    first = distances[0] == 0
    if not first:
        acc_in, stat_in, refs = refs[0], refs[1], refs[2:]
    token, every, refs = refs[0], refs[1:passed], refs[passed:]
    if last:
        out_ref, after, acc, stat, key_all, value_all = refs
    else:
        acc, stat, after = refs
        stat = stat.at[0]
    after[0] = token[0]
    rows = q_ref.shape[0]
    lane = iota((rows, HD), 1)
    causal = iota((rows, rows), 0) >= iota((rows, rows), 1)
    flags = [None, x_of(pos) == 1, core_of(pos) == 1, x_of(pos) == 1]

    if not first:
        acc[...] = acc_in[...]
        stat[...] = stat_in[0]

    def attend(keyed, valued, fresh):
        wide = jnp.concatenate([v[...] for v in valued], axis=0)
        wide = jnp.concatenate([wide, jnp.ones_like(wide)], axis=1)
        keyed = [k[...] for k in keyed]
        if fresh:
            own = keyed[0].astype(F32)
            shifts = [
                jnp.sum(q_ref[:, g * HD : (g + 1) * HD].astype(F32) * own, axis=1, keepdims=True)
                for g in range(group)
            ]
        else:
            shifts = [stat[:, g : g + 1] for g in range(group)]
        hidden = [0.0] + [
            jnp.where(flags[n], 0.0, LOW).astype(F32) if fresh else 0.0 for n in range(1, len(keyed))
        ]
        def scored(i):
            parts = []
            for g in range(i, i + pair):
                query = q_ref[:, g * HD : (g + 1) * HD]
                parts.append(query)
            query = jnp.concatenate(parts, axis=0)
            return [mm_bt(query, k) for k in keyed]

        scores = scored(0)
        for i in range(0, group, pair):
            ahead = scored(i + pair) if i + pair < group else None
            shift = jnp.concatenate(shifts[i : i + pair], axis=0) * SCALE2
            probs = []
            for n, s in enumerate(scores):
                x = s * SCALE2 - (shift - hidden[n])
                if fresh and n == 0:
                    x = jnp.concatenate(
                        [jnp.where(causal, x[m * rows : (m + 1) * rows], LOW) for m in range(pair)], axis=0
                    )
                probs.append(jnp.exp2(x).astype(BF16))
            out = mm(jnp.concatenate(probs, axis=1), wide)
            for n in range(pair):
                g = i + n
                cols = slice(g * HD, (g + 1) * HD)
                band = slice(n * rows, (n + 1) * rows)
                summed, total = out[band, :HD], out[band, HD:]
                if fresh:
                    acc[:, cols] = summed
                    old = jnp.where(lane == g, shifts[g], 0.0 if g == 0 else stat[...])
                    stat[...] = jnp.where(lane == group + g, total, old)
                else:
                    acc[:, cols] += summed
                    stat[...] += jnp.where(lane == group + g, total, 0.0)
            scores = ahead

    for n, distance in enumerate(distances):
        here = slice(n * PLANE, (n + 1) * PLANE)
        if distance == 0:
            attend(keys[here], values[here], True)
        else:
            pl.when(z_of(pos) >= distance)(functools.partial(attend, keys[here], values[here], False))
    if not last:
        return
    totals = (lane >= group) & (lane < 2 * group)
    inverse = 1.0 / jnp.where(totals, stat[...], 1.0)
    for g in range(group):
        cols = slice(g * HD, (g + 1) * HD)
        out_ref[:, cols] = (acc[:, cols] * inverse[:, group + g : group + g + 1]).astype(BF16)

    sums = jnp.where(totals, stat[...], 0.0)
    fine = jnp.min(jnp.where(sums < LIMIT, 1.0, 0.0))

    @pl.when(fine < 0.5)
    def _():
        head = begin + pl.program_id(0)
        for n in range(planes * PLANE):
            here = pl.ds(n * rows, rows)
            pltpu.sync_copy(every[n].at[:, pl.ds(pl.multiple_of(head * HD, HD), HD)], key_all.at[here])
            pltpu.sync_copy(
                every[n].at[:, pl.ds(pl.multiple_of((kv_count + head) * HD, HD), HD)], value_all.at[here]
            )

        def one(g, carry):
            cols = pl.ds(pl.multiple_of(g * HD, HD), HD)
            query = q_ref[:, cols]
            x = jnp.where(causal, mm_bt(query, key_all[0:rows, :]) * SCALE2, LOW)
            top = jnp.max(x, axis=1, keepdims=True)
            probs = jnp.exp2(x - top)
            total = jnp.sum(probs, axis=1, keepdims=True)
            summed = mm(probs.astype(BF16), value_all[0:rows, :])

            def more(n, sums):
                top, total, summed = sums
                here = pl.ds(pl.multiple_of(n * rows, rows), rows)
                near = jnp.where(n == 2, core_of(pos), x_of(pos)) == 1
                seen = jnp.where(n < PLANE, near, z_of(pos) >= n // PLANE)
                x = jnp.where(seen, mm_bt(query, key_all[here, :]) * SCALE2, LOW)
                high = jnp.maximum(jnp.max(x, axis=1, keepdims=True), top)
                probs = jnp.exp2(x - high)
                keep = jnp.exp2(top - high)
                part = mm(probs.astype(BF16), value_all[here, :])
                return high, keep * total + jnp.sum(probs, axis=1, keepdims=True), keep * summed + part

            top, total, summed = lax.fori_loop(1, planes * PLANE, more, (top, total, summed))
            out_ref[:, cols] = (summed / total).astype(BF16)
            return carry

        lax.fori_loop(0, group, one, 0)


def soft_step(pos, query, pieces, distances, state, into, span, kv_count, planes, last, token):
    rows, width = query.shape
    group = width // HD // kv_count
    first = distances[0] == 0
    begin, count = span
    block = pl.BlockSpec((rows, group * HD), lambda k: (0, begin + k))
    stat = pl.BlockSpec((1, rows, HD), lambda k: (begin + k, 0, 0))
    keys = pl.BlockSpec((rows, HD), lambda k: (0, begin + k))
    values = pl.BlockSpec((rows, HD), lambda k: (0, kv_count + begin + k))
    used = [a for d in distances for a in pieces[d]]
    in_specs = [SCALAR, block] + [keys] * len(used) + [values] * len(used)
    operands = [pos, query] + used + used
    aliases = {}
    if not first:
        if not last:
            aliases = {len(operands): 0, len(operands) + 1: 1}
        in_specs += [block, stat]
        operands += list(state)
    in_specs.append(SCALAR)
    operands.append(token)
    rest = [a for d in range(planes) for a in pieces[d]] if last else []
    if into is not None:
        for i, a in enumerate(into):
            aliases[len(operands) + len(rest) + i] = i
        rest = rest + list(into)
    in_specs += [ANY] * len(rest)
    operands += rest
    if last:
        out_specs = [block, SCALAR]
        out_shape = [jax.ShapeDtypeStruct((rows, width), BF16), NEXT]
        scratch = [pltpu.VMEM((rows, group * HD), F32), pltpu.VMEM((rows, HD), F32)]
        scratch += [pltpu.VMEM((planes * PLANE * rows, HD), BF16)] * 2
    else:
        out_specs = [block, stat, SCALAR]
        out_shape = [
            jax.ShapeDtypeStruct((rows, width), F32),
            jax.ShapeDtypeStruct((kv_count, rows, HD), F32),
            NEXT,
        ]
        scratch = []
    return pl.pallas_call(
        functools.partial(
            soft_kernel,
            group=group,
            distances=distances,
            planes=planes,
            last=last,
            passed=1 + len(rest),
            kv_count=kv_count,
            begin=begin,
        ),
        grid=(count,),
        in_specs=in_specs,
        out_specs=out_specs,
        out_shape=out_shape,
        scratch_shapes=scratch,
        input_output_aliases=aliases,
        compiler_params=params(),
        cost_estimate=COST,
        name="softmax",
    )(*operands)


def local(
    light_query,
    light_key,
    light_value,
    log_decay,
    out_gate,
    norm_gain,
    soft_query,
    soft_key,
    soft_value,
    *,
    ctx,
    tp,
):
    rows, heads = log_decay.shape
    qh = heads // 4
    length = qh * HD + TAIL
    planes = ctx // PLANE
    kv_count = soft_key.shape[1] // HD
    place = lax.axis_index("ctx")
    pos = place.astype(jnp.int32).reshape(1)

    def over_core(a):
        return lax.ppermute(a, "ctx", [(i, i ^ 1) for i in range(ctx)])

    def over_x(a):
        return lax.ppermute(a, "ctx", [(i, i ^ 2) for i in range(ctx)])

    def over_z(a, d):
        return lax.ppermute(a, "ctx", [(i, i + PLANE * d) for i in range(ctx - PLANE * d)])

    def after(a, token):
        return lax.optimization_barrier((a, token))[0]

    paired = jnp.concatenate([soft_key, soft_value], axis=1)
    crossed = over_x(paired)
    arrived = [paired, over_z(paired, 1)]

    def forward(token):
        arrived.append(over_z(after(arrived[-1], token), 1))

    pieces = [[paired, crossed, over_core(paired), over_core(crossed)]]

    half = max(kv_count // 2, 1)
    spans = [(0, half), (half, kv_count - half)] if kv_count > 1 else [(0, 1)]

    def soft(distances, state, last, token, span=None, into=None):
        *state, token = soft_step(
            pos, soft_query, pieces, distances, state, into, span or (0, kv_count), kv_count, planes, last, token
        )
        return state, token

    send, keep, cum, cumt, token = local_state(
        pos, light_key, light_value, after(log_decay.T, pieces[0][2])
    )
    other = over_core(send)
    quarter = (length, HD)

    def cross(d, token):
        a = after(arrived[d], token)
        pieces.append([a, over_x(a)])

    def spread_core(d, token):
        pieces[d] += [over_core(after(a, token)) for a in pieces[d]]

    cross(1, token)
    forward(token)
    state, token = soft((0,), None, False, token, spans[0])
    chip_send, chip_keep, token = small(chip_kernel, pos, [keep, other], [quarter, quarter], qh, "chip", token)
    chip_other = over_x(chip_send)
    cross(2, token)
    forward(token)
    if len(spans) > 1:
        state, token = soft((0,), None, False, token, spans[1], state)
    spread_core(1, token)
    plane, token = small(plane_kernel, pos, [chip_keep, chip_other], [quarter], qh, "plane", token)
    earlier = [over_z(plane, d) for d in range(1, planes)]
    spread_core(2, token)
    cross(3, token)
    for d in range(3, planes - 1):
        forward(token)
        cross(d + 1, token)
    both = (2, qh * HD, HD)
    rest = (planes - 1,)
    for middle in [(1, 2)] + [(d,) for d in range(3, planes - 1)]:
        for n, span in enumerate(spans):
            state, token = soft(middle, state, False, token, span)
            if n == 0:
                spread_core(middle[-1] + 1, token)
    enter_send, enter_keep, token = small(
        enter_kernel, pos, [chip_keep, chip_other] + earlier, [quarter, quarter], qh, "enter", token
    )
    enter_other = over_x(enter_send)
    soft_out, token = soft(rest, state, True, token, spans[0])
    state_send, state_keep, token = small(
        core_kernel, pos, [enter_keep, enter_other, keep, other], [both, both], qh, "core", token
    )
    state_other = over_core(state_send)
    raw, square, token = light(
        pos, light_query, light_key, light_value, cum, cumt, state_keep, state_other, token
    )
    for span in spans[1:]:
        soft_out, token = soft(rest, state, True, token, span, soft_out)
    squares = [square]
    step = 1
    while step < tp:
        square = sum(squares)
        squares = [square, lax.ppermute(square, "tp", [(i, i ^ step) for i in range(tp)])]
        step *= 2
    light_out = finish(raw, squares, norm_gain, out_gate, heads * HD * tp, token)
    return (light_out, soft_out[0])


def solution(mesh):
    both = P("ctx", "tp")
    return jax.shard_map(
        functools.partial(local, ctx=mesh.shape["ctx"], tp=mesh.shape["tp"]),
        mesh=mesh,
        in_specs=(both, both, both, both, both, P("tp"), both, both, both),
        out_specs=(both, both),
        check_vma=False,
    )
```
